32 devices in a mesh: lon: 4 (over z), lat: 8 (over y, x, core).
Axes of the slice: x: 2, y: 2, z: 4, core: 2. Of those that a mesh axis runs over, the one named last changes fastest.
Arguments:
- increment: float32 [4, 32, 64, 512], P(None, None, 'lat', 'lon'), may hold values from -6 to 6
- coef_lon: float32 [4, 64, 512], P(None, 'lat', 'lon'), may hold values from 0.4 to 0.49
- coef_lat: float32 [4, 64, 512], P(None, 'lat', 'lon'), may hold values from 0.4 to 0.49
- obs_values: float32 [4096, 128], P(('lon', 'lat')), may hold values from -1.8 to 1.8
- obs_weight: float32 [4096, 128], P(('lon', 'lat')), may hold values from 0.25 to 4
- obs_operator: float32 [3, 128, 128], replicated, may hold values from -0.5 to 0.5
- obs_columns: int32 [4096], P(('lon', 'lat')), may hold values from 0 to 1023
- obs_types: int32 [4096], P(('lon', 'lat')), may hold values from 0 to 2
- obs_counts: int32 [256], P(('lon', 'lat')), may hold values from 0 to 16, as said below
Outputs:
- gradient: float32 [4, 32, 64, 512], P(None, None, 'lat', 'lon')
- departures: float32 [4096, 128], P(('lon', 'lat'))
The draws below stay inside these ranges and needn't reach their ends.
Inputs may be any that keep to these rules, and one draw needn't show every extreme that they name: `obs_counts`: each entry counts the live slots of one bucket of 16; slots at or past the count are ignored. In every longitude block some owner latitude block receives full buckets from every source. `obs_columns`: the column within the owner's block, row times 128 plus column. `obs_types`: 0 radiosonde, 1 occultation, 2 radiance.
All inputs are finite; a program needn't handle non-finite values.
Results may differ from the reference program's by a relative error of at most 0.000073.
Values sent between devices are 32-bit elements; how exact they have to be, the bound alone decides.
No kernel may reach another device: no remote copies, remote signals or barrier semaphores. Data moves between devices by JAX's collectives and lax.ppermute only.
A program may use at most 64 MiB of HBM per device.

```python
import math
import jax
import jax.numpy as jnp
from jax import lax

FIELDS = 4
LEVELS = 32
LAT_DEV = 8
LON_DEV = 128
SLOTS = 16
STEPS = 4
PROFILE = 128
NLAT = 64
NLON = 512
ROWS = 4096
N_LON = 4
N_LAT = 8


def draw_obs_counts(key, part):
    key_list = jax.random.split(key, 4)
    grid_shape = (N_LON, N_LAT, N_LAT)
    busy_owner = jax.random.randint(key_list[0], (N_LON, 1, N_LAT), 0, 2)
    full_owner = jax.random.randint(key_list[1], (N_LON, 1, 1), 0, N_LAT)
    high_draw = jax.random.randint(key_list[2], grid_shape, 0, SLOTS + 1)
    low_draw = jax.random.randint(key_list[3], grid_shape, 0, SLOTS * 3 // 4 + 1)
    owner_index = jnp.arange(N_LAT, dtype=jnp.int32).reshape(1, 1, N_LAT)
    counted = jnp.where(busy_owner == 1, high_draw, low_draw)
    counted = jnp.where(owner_index == full_owner, SLOTS, counted)
    return counted.reshape(-1).astype(jnp.int32)


def place_ends(values, own_key, smallest, high):
    longest = values.shape.index(max(values.shape))
    spots = []
    for shift in (0, 1):
        where = [jax.random.randint(jax.random.fold_in(own_key, axis), (), 0, length) for axis, length in enumerate(values.shape)]
        where[longest] = (where[longest] + shift) % values.shape[longest]
        spots.append(tuple(where))
    return values.at[spots[0]].set(smallest).at[spots[1]].set(high)


def block_scale(stream_key, extent, shards, smallest, top_value):
    level, own = 1.0, jax.random.fold_in(stream_key, 6)
    for dim, blocks in shards:
        steps = jnp.exp(jax.random.uniform(jax.random.fold_in(own, dim), (blocks,), jnp.float32, smallest / len(shards), top_value / len(shards)))
        level = level * jnp.repeat(steps, extent[dim] // blocks).reshape([-1 if axis == dim else 1 for axis in range(len(extent))])
    return level


def normal_values(stream_key, shape, width, limit, cuts=(), kind=jnp.bfloat16):
    level = block_scale(stream_key, shape, cuts, -0.22, 0.18) if cuts else 1.0
    drawn = jax.random.normal(stream_key, shape, jnp.float32) * width * level
    return jnp.minimum(jnp.maximum(drawn, -limit), limit).astype(kind)


def setup_inputs(seed: int = 0) -> dict:
    arg_keys = jax.random.split(jax.random.key(seed), 10)
    return {
        "increment": normal_values(arg_keys[0], (FIELDS, LEVELS, NLAT, NLON), 1.0, 6.0, ((2, 8), (3, 4)), jnp.float32),
        "coef_lon": jnp.clip(0.4 + 0.09 * jax.random.uniform(arg_keys[1], (FIELDS, NLAT, NLON), jnp.float32) ** block_scale(arg_keys[1], (FIELDS, NLAT, NLON), ((1, 8), (2, 4)), -0.2, 0.2), 0.4, 0.49),
        "coef_lat": jnp.clip(0.4 + 0.09 * jax.random.uniform(arg_keys[2], (FIELDS, NLAT, NLON), jnp.float32) ** block_scale(arg_keys[2], (FIELDS, NLAT, NLON), ((1, 8), (2, 4)), -0.2, 0.2), 0.4, 0.49),
        "obs_values": normal_values(arg_keys[3], (ROWS, PROFILE), 0.3, 1.8, ((0, 32),), jnp.float32),
        "obs_weight": jnp.clip(jnp.exp(math.log(4.0) - 2.7725887 * jax.random.uniform(arg_keys[4], (ROWS, PROFILE), jnp.float32) ** block_scale(arg_keys[4], (ROWS, PROFILE), ((0, 32),), -0.2, 0.2)), 0.25, 4.0),
        "obs_operator": normal_values(arg_keys[5], (3, PROFILE, PROFILE), PROFILE ** -0.5, 0.5, (), jnp.float32),
        "obs_columns": place_ends(jax.random.randint(arg_keys[6], (ROWS,), 0, LAT_DEV * LON_DEV), jax.random.fold_in(arg_keys[6], 1), 0, (LAT_DEV * LON_DEV) - 1).astype(jnp.int32),
        "obs_types": place_ends(jax.random.randint(arg_keys[7], (ROWS,), 0, 3), jax.random.fold_in(arg_keys[7], 1), 0, 2).astype(jnp.int32),
        "obs_counts": draw_obs_counts(jax.random.fold_in(arg_keys[9], 71), 0),
    }


def spread_field(field_state, root_lon, root_lat, sign_value):
    scaled_lon = root_lon * field_state
    second_lon = jnp.roll(scaled_lon, -1, 2) + jnp.roll(scaled_lon, 1, 2) - 2.0 * scaled_lon
    scaled_lat = root_lat * field_state
    mirrored = jnp.roll(scaled_lat, NLON // 2, 2) * sign_value
    north_side = jnp.concatenate([scaled_lat[:, 1:, :], mirrored[:, -1:, :]], 1)
    south_side = jnp.concatenate([mirrored[:, :1, :], scaled_lat[:, :-1, :]], 1)
    second_lat = north_side + south_side - 2.0 * scaled_lat
    return field_state + root_lon * second_lon + root_lat * second_lat


def diffuse(grid_state, coef_lon, coef_lat):
    sign_table = jnp.array([1.0, 1.0, -1.0, -1.0], jnp.float32)

    def per_field(packed):
        field_state, root_lon, root_lat, sign_value = packed
        for turn in range(STEPS):
            field_state = spread_field(field_state, root_lon[None], root_lat[None], sign_value)
        return field_state

    return lax.map(per_field, (grid_state, coef_lon, coef_lat, sign_table))


def reference(increment, coef_lon, coef_lat, obs_values, obs_weight, obs_operator, obs_columns, obs_types, obs_counts):
    highest = lax.Precision.HIGHEST
    state = diffuse(increment, coef_lon, coef_lat)
    counts_grid = obs_counts.reshape(N_LON, N_LAT, N_LAT, 1)
    slot_index = jnp.arange(SLOTS, dtype=jnp.int32).reshape(1, 1, 1, SLOTS)
    live = (slot_index < counts_grid).reshape(-1)
    local_col = obs_columns.reshape(N_LON, N_LAT, N_LAT, SLOTS)
    owner_lat = jnp.arange(N_LAT, dtype=jnp.int32).reshape(1, 1, N_LAT, 1)
    source_lon = jnp.arange(N_LON, dtype=jnp.int32).reshape(N_LON, 1, 1, 1)
    grid_row = owner_lat * LAT_DEV + local_col // LON_DEV
    grid_col = source_lon * LON_DEV + local_col % LON_DEV
    flat_cell = (grid_row * NLON + grid_col).reshape(-1).astype(jnp.int32)
    flat_state = state.reshape(PROFILE, NLAT * NLON)
    columns = flat_state[:, flat_cell].T
    model_all = [jnp.dot(columns, obs_operator[kind], precision=highest) for kind in range(3)]
    model = jnp.where((obs_types == 0)[:, None], model_all[0], jnp.where((obs_types == 1)[:, None], model_all[1], model_all[2]))
    departures = jnp.where(live[:, None], obs_values - model, jnp.float32(0.0))
    weighted = obs_weight * departures
    adjoint_all = [jnp.dot(weighted, obs_operator[kind].T, precision=highest) for kind in range(3)]
    adjoint = jnp.where((obs_types == 0)[:, None], adjoint_all[0], jnp.where((obs_types == 1)[:, None], adjoint_all[1], adjoint_all[2]))
    forcing = jnp.zeros((PROFILE, NLAT * NLON), jnp.float32).at[:, flat_cell].add(adjoint.T)
    smoothed = diffuse(forcing.reshape(FIELDS, LEVELS, NLAT, NLON), coef_lon, coef_lat)
    return increment - smoothed, departures
```

```python
import functools

import jax
import jax.numpy as jnp
from jax import lax
from jax.experimental import pallas as pl
from jax.experimental.pallas import tpu as pltpu
from jax.sharding import PartitionSpec as P

STEPS = 4
ROWS = 8
LANES = 128
PLANES = ROWS + 2 * STEPS
EDGE = 2 * STEPS
VMEM = pltpu.VMEM
MIB = 1 << 20


def lane_of(shape):
    return lax.broadcasted_iota(jnp.int32, shape, len(shape) - 1)


def turn(x, by):
    by = by % LANES if isinstance(by, int) else by
    return pltpu.roll(x, by, x.ndim - 1)


def position():
    lat, count = (lax.axis_index("lat"), lax.axis_size("lat"))
    even = lat % 2 == 0
    pole = jnp.logical_or(lat == 0, lat == count - 1)
    return even, pole


def split(x):
    high = x.astype(jnp.bfloat16)
    low = (x - high.astype(jnp.float32)).astype(jnp.bfloat16)
    return high, low


def matmul(a, b, dims):
    return lax.dot_general(a, b, (dims, ((), ())), preferred_element_type=jnp.float32)


def edges_of(plane_list, rows):
    slot = lane_of((rows, LANES)) // EDGE
    tile = jnp.zeros((rows, LANES), jnp.float32)
    for r, plane in enumerate(plane_list):
        p = STEPS + r
        tile = jnp.where(slot == p, turn(plane, EDGE * p - (LANES - STEPS)), tile)
    return tile


def pack_kernel(inc, cl, ct, b_out, a_out, g_out):
    width = inc.shape[0] // ROWS
    fields = cl.shape[0] // ROWS
    even, _ = position()
    a_row = jnp.where(even, STEPS, 0)
    b_row = STEPS - a_row
    for out, first in ((b_out, b_row), (a_out, a_row)):
        for k in range(STEPS):
            out[k, 0:width, :] = inc[pl.ds(first + k, width, stride=ROWS), :]
            out[k, width : width + fields, :] = cl[pl.ds(first + k, fields, stride=ROWS), :]
            out[k, width + fields : width + 2 * fields, :] = ct[pl.ds(first + k, fields, stride=ROWS), :]
    g_out[0:width, :] = edges_of([inc[pl.ds(r, width, stride=ROWS), :] for r in range(ROWS)], width)
    for n, ref in enumerate((cl, ct)):
        rows = [ref[pl.ds(r, fields, stride=ROWS), :] for r in range(ROWS)]
        g_out[width + n * fields : width + (n + 1) * fields, :] = edges_of(rows, fields)


def slots_kernel(counts, values, weights, columns, types, out):
    owners, bucket = (out.shape[0], values.shape[1])
    slots = columns.shape[1]
    lane = lane_of((1, slots))
    limit = jnp.zeros((1, slots), jnp.int32)
    for d in range(owners):
        limit = jnp.where(lane // bucket == d, counts[d], limit)
    code = jnp.where(lane % bucket < limit, columns[...] * 4 + types[...], -1).astype(jnp.float32)
    out[:, 0:bucket, :] = values[...]
    out[:, bucket : 2 * bucket, :] = weights[...]
    for d in range(owners):
        at = d * bucket
        window = code[:, at // LANES * LANES : at // LANES * LANES + LANES]
        out[d, 2 * bucket : 2 * bucket + 8, :] = jnp.broadcast_to(turn(window, -(at % LANES)), (8, LANES))


def spread_coefs(co, cb, fields):
    for p in range(PLANES + 1):
        for f in range(fields):
            a = jnp.broadcast_to(co[p, f : f + 1, :], (8, LANES))
            b = jnp.broadcast_to(co[p, fields + f : fields + f + 1, :], (8, LANES))
            cb[f, p, 0] = a
            cb[f, p, 1] = b
            cb[f, p, 2] = 1.0 - 2.0 * (a * a + b * b)


def diffuse(xt, ht, cb, store):
    width = xt.shape[1]
    fields = cb.shape[0]
    per_field = width // fields // 8
    lane = lane_of((8, LANES))

    def body(i, carry):
        rows = pl.ds(pl.multiple_of(i * 8, 8), 8)
        fld = i // per_field
        f = {p: xt[p, rows, :] for p in range(PLANES)}
        rim = ht[rows, :]
        for step in range(STEPS):
            low, high = (step, PLANES - 1 - step)
            last = step == STEPS - 1
            rim_l, rim_t, rim_c = (cb[fld, PLANES, n] for n in range(3))
            g_rim = rim_l * rim
            joined = g_rim
            h = {p: cb[fld, p, 1] * f[p] for p in range(low, high + 1)}
            new = {}
            for p in range(low + 1, high):
                a = cb[fld, p, 0]
                g = a * f[p]
                ends = turn(g_rim, LANES - 1 - (EDGE * p + STEPS - 1))
                east = turn(jnp.where(lane == 0, ends, g), -1)
                west = turn(jnp.where(lane == LANES - 1, ends, g), 1)
                new[p] = cb[fld, p, 2] * f[p] + a * (east + west) + cb[fld, p, 1] * (h[p + 1] + h[p - 1])
                if not last:
                    moved = turn(g, EDGE * p + STEPS - 1 - (LANES - 1))
                    joined = jnp.where(lane // EDGE == p, moved, joined)
            if not last:
                east = turn(jnp.where(lane % EDGE == STEPS, joined, g_rim), -1)
                west = turn(jnp.where(lane % EDGE == STEPS - 1, joined, g_rim), 1)
                h_rim = rim_t * rim
                rim = rim_c * rim + rim_l * (east + west) + rim_t * (turn(h_rim, EDGE) + turn(h_rim, -EDGE))
            f = new
        store(i, rows, [f[STEPS + r] for r in range(ROWS)])
        return carry

    lax.fori_loop(0, width // 8, body, 0)


def join_rim(own, from_a, from_b, signed_rows, even, pole):
    rows = own.shape[0]
    slot = lane_of((rows, LANES)) // EDGE
    a_base = jnp.where(even, PLANES - STEPS, 0)
    b_base = jnp.where(even, 0, PLANES - STEPS)
    tile = jnp.where(slot // STEPS == a_base // STEPS, turn(from_a, LANES // 2), own)
    row = lax.broadcasted_iota(jnp.int32, (rows, LANES), 0)
    winds = jnp.logical_and(row >= signed_rows[0], row < signed_rows[1])
    from_b = jnp.where(jnp.logical_and(winds, pole), -from_b, from_b)
    for k in range(STEPS):
        plain = jnp.where(even, ROWS + k, STEPS + k)
        mirrored = jnp.where(even, ROWS - 1 - k, PLANES - STEPS - 1 - k)
        source = jnp.where(pole, mirrored, plain)
        shift = (EDGE * (b_base + k - source) + 2 * LANES) % LANES
        tile = jnp.where(slot == b_base + k, turn(from_b, shift), tile)
    return tile


def side_select(west, east):
    return jnp.where(lane_of(west.shape) % EDGE < STEPS, west, east)


def codes_by_slot(code_rows):
    parts = [
        jnp.broadcast_to(code_rows[:, t * LANES : (t + 1) * LANES], (LANES, LANES)).T
        for t in range(code_rows.shape[1] // LANES)
    ]
    return jnp.concatenate(parts, 0).astype(jnp.int32)


def one_hot(code, rows):
    cell = jnp.where(code >= 0, code // 4, -1)
    lane = lane_of(code.shape)
    return jnp.concatenate([jnp.where(cell == r * LANES + lane, 1.0, 0.0).astype(jnp.bfloat16) for r in rows], 1)


def scatter(adjoint_t, hot):
    high, low = split(adjoint_t)
    return matmul(jnp.concatenate([high, low], 1), jnp.concatenate([hot, hot], 0), ((1,), (0,)))


def middle_kernel(
    inc, cl, ct, a_in, b_in, g_west, g_east, rim_a, rim_b, slots_in, operator,
    dep_out, adj_out, code_out, g_out, f_out, co_out, xt, ht, cb,
):
    width = inc.shape[0] // ROWS
    fields = cl.shape[0] // ROWS
    owners, bucket = (slots_in.shape[0], (slots_in.shape[1] - 8) // 2)
    slots = owners * bucket
    even, pole = position()
    a_base = jnp.where(even, PLANES - STEPS, 0)
    b_base = jnp.where(even, 0, PLANES - STEPS)
    sign = jnp.where(pole, -1.0, 1.0).astype(jnp.float32)
    half = width // 2
    for k in range(STEPS):
        kk = jnp.where(pole, STEPS - 1 - k, k)
        xt[a_base + k] = a_in[k, 0:width, :]
        xt[b_base + k, 0:half, :] = b_in[kk, 0:half, :]
        xt[b_base + k, half:width, :] = b_in[kk, half:width, :] * sign
        co_out[a_base + k] = a_in[k, width : width + 2 * fields, :]
        co_out[b_base + k] = b_in[kk, width : width + 2 * fields, :]
    for r in range(ROWS):
        xt[STEPS + r] = inc[pl.ds(r, width, stride=ROWS), :]
        co_out[STEPS + r, 0:fields, :] = cl[pl.ds(r, fields, stride=ROWS), :]
        co_out[STEPS + r, fields : 2 * fields, :] = ct[pl.ds(r, fields, stride=ROWS), :]
    own = side_select(g_west[...], g_east[...])
    rim = join_rim(own, rim_a[...], rim_b[...], (half, width), even, pole)
    ht[...] = rim[0:width]
    co_out[PLANES] = rim[width : width + 2 * fields]
    spread_coefs(co_out, cb, fields)

    def store(i, rows, planes):
        for r in range(ROWS):
            xt[STEPS + r, rows, :] = planes[r]

    diffuse(xt, ht, cb, store)

    lane = lane_of((1, LANES))
    per_tile = LANES // bucket
    code_parts = []
    for t in range(slots // LANES):
        part = jnp.full((1, LANES), -1.0, jnp.float32)
        for n in range(per_tile):
            d = t * per_tile + n
            got = slots_in[d, 2 * bucket : 2 * bucket + 1, :]
            part = jnp.where(lane // bucket == n, turn(got, n * bucket), part)
        code_parts.append(part)
    code_row = jnp.concatenate(code_parts, 1)
    code = codes_by_slot(code_row)
    hot = one_hot(code, range(ROWS))

    high, low = split(jnp.concatenate([xt[STEPS + r] for r in range(ROWS)], 1))
    both = matmul(hot, jnp.concatenate([high, low], 0), ((1,), (1,)))
    column = both[:, 0:width] + both[:, width:]

    kind = jnp.where(code >= 0, code % 4, -1)
    op_high, op_low = split(operator[...])
    masks = [kind == n for n in range(3)]

    def by_kind(x, dims):
        x_high, x_low = split(x)
        zero = jnp.zeros_like(x_high)
        total = None
        for n in range(3):
            m_high = jnp.where(masks[n], x_high, zero)
            m_low = jnp.where(masks[n], x_low, zero)
            part = matmul(m_high, op_high[n], dims) + matmul(m_high, op_low[n], dims) + matmul(m_low, op_high[n], dims)
            total = part if total is None else total + part
        return total

    model = by_kind(column, ((1,), (0,)))
    values = slots_in[:, 0:bucket, :].reshape(slots, LANES)
    weights = slots_in[:, bucket : 2 * bucket, :].reshape(slots, LANES)
    departures = jnp.where(code >= 0, values - model, 0.0)
    dep_out[...] = departures
    adjoint_t = by_kind(weights * departures, ((1,), (1,))).T
    for t in range(slots // LANES):
        adj_out[t] = adjoint_t[:, t * LANES : (t + 1) * LANES]
        code_out[t] = jnp.broadcast_to(code_row[:, t * LANES : (t + 1) * LANES], (8, LANES))
    forcing = scatter(adjoint_t, hot)
    planes = [forcing[:, r * LANES : (r + 1) * LANES] for r in range(ROWS)]
    for r in range(ROWS):
        f_out[r] = planes[r]
    g_out[...] = edges_of(planes, width)


def last_kernel(inc, f_in, co, g_west, g_east, a_in, b_in, out, xt, ht, cb):
    width = inc.shape[0] // ROWS
    fields = co.shape[1] // 2
    tiles = (a_in.shape[0] - width) // (width + 8)
    even, pole = position()
    half = width // 2
    sign = jnp.where(pole, -1.0, 1.0).astype(jnp.float32)

    def halo(ref, rows, base, flip):
        code = codes_by_slot(
            jnp.concatenate([ref[width * (1 + tiles) + 8 * t : width * (1 + tiles) + 8 * t + 1, :] for t in range(tiles)], 1)
        )
        adjoint_t = jnp.concatenate([ref[width * (1 + t) : width * (2 + t), :] for t in range(tiles)], 1)
        got = scatter(adjoint_t, one_hot(code, rows))
        for k in range(STEPS):
            plane = got[:, k * LANES : (k + 1) * LANES]
            if flip:
                xt[base + k, 0:half, :] = plane[0:half]
                xt[base + k, half:width, :] = plane[half:width] * sign
            else:
                xt[base + k] = plane

    a_first = jnp.where(even, 0, STEPS)
    halo(a_in, [a_first + k for k in range(STEPS)], jnp.where(even, PLANES - STEPS, 0), False)
    plain = [jnp.where(even, STEPS + k, k) for k in range(STEPS)]
    mirrored = [jnp.where(even, STEPS - 1 - k, ROWS - 1 - k) for k in range(STEPS)]
    b_rows = [jnp.where(pole, m, n) for m, n in zip(mirrored, plain)]
    halo(b_in, b_rows, jnp.where(even, 0, PLANES - STEPS), True)
    for r in range(ROWS):
        xt[STEPS + r] = f_in[r]
    own = side_select(g_west[...], g_east[...])
    ht[...] = join_rim(own, a_in[0:width, :], b_in[0:width, :], (half, width), even, pole)
    spread_coefs(co, cb, fields)

    def store(i, rows, planes):
        for r in range(ROWS):
            at = pl.ds(i * 8 * ROWS + r, 8, stride=ROWS)
            out[at, :] = inc[at, :] - planes[r]

    diffuse(xt, ht, cb, store)


def call(kernel, outs, args, scratch=(), smem=(), flops=0, limit=48):
    specs = [pl.BlockSpec(memory_space=pltpu.SMEM if n in smem else VMEM) for n in range(len(args))]
    size = 4 * sum(x.size for x in list(args) + list(outs))
    return pl.pallas_call(
        kernel,
        out_shape=outs,
        in_specs=specs,
        out_specs=[pl.BlockSpec(memory_space=VMEM) for _ in outs],
        scratch_shapes=list(scratch),
        compiler_params=pltpu.CompilerParams(vmem_limit_bytes=limit * MIB),
        cost_estimate=pl.CostEstimate(flops=flops, bytes_accessed=size, transcendentals=0),
    )(*args)


def routes():
    lons, lats = (lax.axis_size("lon"), lax.axis_size("lat"))
    at = lambda lon, lat: lon % lons * lats + lat
    cells = [(lon, lat) for lon in range(lons) for lat in range(lats)]
    inner = [(at(o, a), at(o, a ^ 1)) for o, a in cells]
    outer = []
    for o, a in cells:
        if a in (0, lats - 1):
            outer.append((at(o, a), at(o + lons // 2, a)))
        else:
            outer.append((at(o, a), at(o, a - 1 if a % 2 == 0 else a + 1)))
    east = [(at(o, a), at(o + 1, a)) for o, a in cells]
    west = [(at(o, a), at(o - 1, a)) for o, a in cells]
    return inner, outer, east, west


def local(
    increment, coef_lon, coef_lat, obs_values, obs_weight, obs_operator, obs_columns, obs_types, obs_counts
):
    f32 = jnp.float32
    shape = functools.partial(jax.ShapeDtypeStruct, dtype=f32)
    inner, outer, east, west = routes()
    send = lambda x, route: lax.ppermute(x, ("lon", "lat"), route)
    lats = lax.axis_size("lat")
    slots = obs_values.shape[0]
    bucket = slots // lats
    fields = increment.shape[0]
    width = fields * increment.shape[1]
    tall = width + 2 * fields
    inc = increment.reshape(width * ROWS, LANES)
    cl = coef_lon.reshape(fields * ROWS, LANES)
    ct = coef_lat.reshape(fields * ROWS, LANES)

    b_send, a_send, g_send = call(
        pack_kernel, [shape((STEPS, tall, LANES)), shape((STEPS, tall, LANES)), shape((tall, LANES))], [inc, cl, ct]
    )
    g_west = send(g_send, east)
    g_east = send(g_send, west)
    b_in = send(b_send, outer)
    a_in = send(a_send, inner)
    (slots_send,) = call(
        slots_kernel,
        [shape((lats, 2 * bucket + 8, LANES))],
        [
            obs_counts,
            obs_values.reshape(lats, bucket, LANES),
            obs_weight.reshape(lats, bucket, LANES),
            obs_columns.reshape(1, slots),
            obs_types.reshape(1, slots),
        ],
        smem=(0,),
    )
    slots_in = lax.all_to_all(slots_send, "lat", split_axis=0, concat_axis=0, tiled=True)
    rim_send = side_select(g_west, g_east)
    rim_a = send(rim_send, inner)
    rim_b = send(rim_send, outer)
    scratch = [
        VMEM((PLANES, width, LANES), f32),
        VMEM((width, LANES), f32),
        VMEM((fields, PLANES + 1, 3, 8, LANES), f32),
    ]
    tiles = slots // LANES
    departures, adjoint, code, g_send, forcing, co = call(
        middle_kernel,
        [
            shape((slots, LANES)),
            shape((tiles, width, LANES)),
            shape((tiles, 8, LANES)),
            shape((width, LANES)),
            shape((ROWS, width, LANES)),
            shape((PLANES + 1, 2 * fields, LANES)),
        ],
        [inc, cl, ct, a_in, b_in, g_west, g_east, rim_a, rim_b, slots_in, obs_operator],
        scratch,
        flops=10**8,
    )
    g_west = send(g_send, east)
    g_east = send(g_send, west)
    back = lax.all_to_all(
        departures.reshape(lats, bucket, LANES), "lat", split_axis=0, concat_axis=0, tiled=True
    )
    payload = jnp.concatenate(
        [side_select(g_west, g_east), adjoint.reshape(-1, LANES), code.reshape(-1, LANES)], 0
    )
    a_in = send(payload, inner)
    b_in = send(payload, outer)
    (gradient,) = call(
        last_kernel,
        [shape((width * ROWS, LANES))],
        [inc, forcing, co, g_west, g_east, a_in, b_in],
        scratch,
        flops=10**8,
    )
    return (gradient.reshape(increment.shape), back.reshape(slots, LANES))


def solution(mesh):
    return jax.shard_map(
        local,
        mesh=mesh,
        in_specs=(
            P(None, None, "lat", "lon"),
            P(None, "lat", "lon"),
            P(None, "lat", "lon"),
            P(("lon", "lat"), None),
            P(("lon", "lat"), None),
            P(),
            P(("lon", "lat")),
            P(("lon", "lat")),
            P(("lon", "lat")),
        ),
        out_specs=(P(None, None, "lat", "lon"), P(("lon", "lat"), None)),
        check_vma=False,
    )
```

```python
import functools

import jax
import jax.numpy as jnp
from jax import lax
from jax.experimental import pallas as pl
from jax.experimental.pallas import tpu as pltpu
from jax.sharding import PartitionSpec as P

STEPS = 4
ROWS = 8
LANES = 128
PLANES = ROWS + 2 * STEPS
WIDE = LANES + 2 * STEPS
REGS = WIDE // 8
PADDED = LANES + 16
VMEM = pltpu.VMEM
HBM = pltpu.HBM
MIB = 1 << 20
F32 = jnp.float32


def iota(shape, axis):
    return lax.broadcasted_iota(jnp.int32, shape, axis)


def position():
    lat, count = (lax.axis_index("lat"), lax.axis_size("lat"))
    return lat % 2 == 0, jnp.logical_or(lat == 0, lat == count - 1)


def halo_places(even, pole):
    a_base = jnp.where(even, PLANES - STEPS, 0)
    b_base = jnp.where(even, 0, PLANES - STEPS)
    a_rows = [jnp.where(even, k, STEPS + k) for k in range(STEPS)]
    b_rows = [
        jnp.where(
            pole,
            jnp.where(even, STEPS - 1 - k, ROWS - 1 - k),
            jnp.where(even, STEPS + k, k),
        )
        for k in range(STEPS)
    ]
    return a_base, b_base, a_rows, b_rows


def wind_sign(pole, shape):
    flipped = jnp.logical_and(iota(shape, len(shape) - 1) >= LANES // 2, pole)
    return jnp.where(flipped, -1.0, 1.0).astype(F32)


def split(x):
    high = x.astype(jnp.bfloat16)
    low = (x - high.astype(F32)).astype(jnp.bfloat16)
    return high, low


def matmul(a, b, dims=((1,), (0,))):
    return lax.dot_general(a, b, (dims, ((), ())), preferred_element_type=F32)


def halves(x):
    return x[:, :LANES] + x[:, LANES:]


def pack_kernel(inc_hbm, cl_hbm, ct_hbm, own, coef, b_out, a_out, w_out, e_out, inc, cl, ct, raw, sems):
    copies = [
        pltpu.make_async_copy(src, dst, sems.at[n])
        for n, (src, dst) in enumerate(((inc_hbm, inc), (cl_hbm, cl), (ct_hbm, ct)))
    ]
    for copy in copies:
        copy.start()
    for copy in copies:
        copy.wait()
    fields = cl.shape[0] // ROWS
    even, _ = position()
    raw[...] = jnp.zeros(raw.shape, F32)
    for r in range(ROWS):
        own[r] = inc[pl.ds(r, LANES, stride=ROWS), :].T
        at = 8 * (STEPS + r)
        raw[at : at + fields, :] = cl[pl.ds(r, fields, stride=ROWS), :]
        raw[at + fields : at + 2 * fields, :] = ct[pl.ds(r, fields, stride=ROWS), :]
        w_out[r] = own[r, 0:STEPS, :]
        e_out[r] = own[r, LANES - STEPS : LANES, :]
    coef[...] = raw[...].T
    w_out[ROWS] = coef[0:STEPS, :]
    e_out[ROWS] = coef[LANES - STEPS : LANES, :]
    a_row = jnp.where(even, STEPS, 0)
    b_row = STEPS - a_row
    for out, first in ((b_out, b_row), (a_out, a_row)):
        for k in range(STEPS):
            out[k * LANES : (k + 1) * LANES, :] = own[first + k]
            at = STEPS * LANES + 8 * k
            out[at : at + 8, :] = raw[pl.ds(pl.multiple_of(8 * (STEPS + first + k), 8), 8), :]


def slots_kernel(counts, values, weights, columns, types, out):
    owners, bucket = (out.shape[0], values.shape[1])
    slots = columns.shape[1]
    lane = iota((1, slots), 1)
    limit = jnp.zeros((1, slots), jnp.int32)
    for d in range(owners):
        limit = jnp.where(lane // bucket == d, counts[d], limit)
    code = jnp.where(lane % bucket < limit, columns[...] * 4 + types[...], -1).astype(F32)
    out[:, 0:bucket, :] = values[...]
    out[:, bucket : 2 * bucket, :] = weights[...]
    for d in range(owners):
        at = d * bucket
        window = code[:, at // LANES * LANES : at // LANES * LANES + LANES]
        moved = pltpu.roll(window, (-at) % LANES, 1)
        out[d, 2 * bucket : 2 * bucket + 8, :] = jnp.broadcast_to(moved, (8, LANES))


def coefs_wide(coef, a_in, b_in, from_west, from_east, rim_a, rim_b, raw, co_out, even, pole):
    a_base, b_base, _, b_rows = halo_places(even, pole)
    raw[...] = jnp.zeros(raw.shape, F32)
    for k in range(STEPS):
        kk = jnp.where(pole, STEPS - 1 - k, k)
        at = STEPS * LANES
        raw[pl.ds(pl.multiple_of(8 * (a_base + k), 8), 8), :] = a_in[at + 8 * k : at + 8 * k + 8, :]
        raw[pl.ds(pl.multiple_of(8 * (b_base + k), 8), 8), :] = b_in[pl.ds(pl.multiple_of(at + 8 * kk, 8), 8), :]
    co_out[8 : 8 + LANES, :] = raw[...].T + coef[...]
    tile = jnp.concatenate([from_west[ROWS], from_east[ROWS]], 0)
    plane = iota((8, LANES), 1) // 8
    tile = jnp.where(plane // STEPS == a_base // STEPS, pltpu.roll(rim_a[ROWS], LANES // 2, 1), tile)
    for k in range(STEPS):
        shift = (8 * (b_base + k - STEPS - b_rows[k]) + 2 * LANES) % LANES
        tile = jnp.where(plane == b_base + k, pltpu.roll(rim_b[ROWS], shift, 1), tile)
    co_out[8 - STEPS : 8, :] = tile[0:STEPS]
    co_out[8 + LANES : 8 + LANES + STEPS, :] = tile[STEPS : 2 * STEPS]


def expand(co, cl, ct, cc):
    wide = jnp.concatenate([co[pl.ds(8 - STEPS + q, 8, stride=REGS), :] for q in range(REGS)], 0)
    high, low = split(wide)
    tall = 2 * LANES - 16
    row, col = (iota((tall, 2 * LANES), 0), iota((tall, 2 * LANES), 1))
    wanted = LANES - 16 + col // LANES * 4 + col % LANES // (LANES // 4)
    picks = [jnp.where(row == wanted + 8 * odd, 1.0, 0.0).astype(jnp.bfloat16) for odd in range(2)]
    for p in range(PLANES):
        first = LANES - 16 - p // 2 * 16
        pick = picks[p % 2][first : first + LANES, :]
        both = matmul(high, pick) + matmul(low, pick)
        a, b = (both[:, :LANES], both[:, LANES:])
        cl[p] = a
        ct[p] = b
        cc[p] = 1.0 - 2.0 * (a * a + b * b)


def diffuse(f, spare, cl, ct, cc, store=None):
    for step in range(STEPS):
        last = step == STEPS - 1 and store is not None

        def row(p, carry, f=f, spare=spare, last=last):
            regs = [pl.ds(8 * q, 8) for q in range(REGS)]
            here = [f[p, at, :] for at in regs]
            g = [cl[p, at, :] * x for at, x in zip(regs, here)]
            g = [pltpu.roll(g[-1], 1, 0)] + g + [pltpu.roll(g[0], 7, 0)]
            for q, at in enumerate(regs):
                sides = ct[p + 1, at, :] * f[p + 1, at, :] + ct[p - 1, at, :] * f[p - 1, at, :]
                new = cc[p, at, :] * here[q] + cl[p, at, :] * (g[q] + g[q + 2]) + ct[p, at, :] * sides
                if last:
                    store(p - STEPS, q, new)
                else:
                    spare[p, at, :] = new
            return carry

        lax.fori_loop(step + 1, PLANES - 1 - step, row, 0)
        f, spare = (spare, f)


def cell_of(n, rows):
    plane = (n * 482) >> 16
    rest = n - WIDE * plane
    column = (rest % 8) * REGS + rest // 8 - STEPS
    row = jnp.full(n.shape, -1, jnp.int32)
    for k, r in enumerate(rows):
        row = jnp.where(plane == k, r, row)
    inside = jnp.logical_and(jnp.logical_and(column >= 0, column < LANES), row >= 0)
    return jnp.where(inside, row * LANES + column, -2)


def scatter(adjoint, code_row, rows):
    high, low = split(adjoint)
    code = code_row.astype(jnp.int32)
    cell = jnp.where(code >= 0, code >> 2, -1)
    places = cell_of(iota((len(rows) * WIDE, LANES), 0), rows)
    hot = jnp.concatenate(
        [
            jnp.where(places == cell[:, t * LANES : (t + 1) * LANES], 1.0, 0.0).astype(jnp.bfloat16)
            for t in range(cell.shape[1] // LANES)
        ],
        1,
    )
    return halves(matmul(hot, jnp.concatenate([high, low], 1)))


def middle_kernel(
    own, coef, a_in, b_in, from_west, from_east, rim_a, rim_b, slots_in, operator,
    dep_out, adj_out, code_out, w_out, e_out, f_out, co_out,
    wide, raw, f, spare, cl, ct, cc,
):
    owners, bucket = (slots_in.shape[0], (slots_in.shape[1] - 8) // 2)
    slots = owners * bucket
    even, pole = position()
    a_base, b_base, a_rows, b_rows = halo_places(even, pole)
    sign = wind_sign(pole, (1, LANES))
    inner = slice(8, 8 + LANES)
    west, east = (slice(8 - STEPS, 8), slice(8 + LANES, 8 + LANES + STEPS))
    coefs_wide(coef, a_in, b_in, from_west, from_east, rim_a, rim_b, raw, co_out, even, pole)
    expand(co_out, cl, ct, cc)
    for k in range(STEPS):
        wide[a_base + k, inner, :] = a_in[k * LANES : (k + 1) * LANES, :]
        wide[a_base + k, west, :] = rim_a[a_rows[k], 0:STEPS, :]
        wide[a_base + k, east, :] = rim_a[a_rows[k], STEPS : 2 * STEPS, :]
        at = pl.multiple_of(jnp.where(pole, STEPS - 1 - k, k) * LANES, LANES)
        wide[b_base + k, inner, :] = b_in[pl.ds(at, LANES), :] * sign
        wide[b_base + k, west, :] = rim_b[b_rows[k], 0:STEPS, :] * sign
        wide[b_base + k, east, :] = rim_b[b_rows[k], STEPS : 2 * STEPS, :] * sign
    for r in range(ROWS):
        wide[STEPS + r, inner, :] = own[r]
        wide[STEPS + r, west, :] = from_west[r]
        wide[STEPS + r, east, :] = from_east[r]

    def interleave(p, carry):
        for q in range(REGS):
            f[p, pl.ds(8 * q, 8), :] = wide[p, pl.ds(8 - STEPS + q, 8, stride=REGS), :]
        return carry

    lax.fori_loop(0, PLANES, interleave, 0)
    diffuse(f, spare, cl, ct, cc)

    lane = iota((1, LANES), 1)
    per_tile = LANES // bucket
    code_parts = []
    for t in range(slots // LANES):
        part = jnp.full((1, LANES), -1.0, F32)
        for n in range(per_tile):
            got = slots_in[t * per_tile + n, 2 * bucket : 2 * bucket + 1, :]
            part = jnp.where(lane // bucket == n, pltpu.roll(got, n * bucket, 1), part)
        code_parts.append(part)
        code_out[8 * t : 8 * t + 8, :] = jnp.broadcast_to(part, (8, LANES))
    code_row = jnp.concatenate(code_parts, 1)
    code = jnp.concatenate([jnp.broadcast_to(part, (LANES, LANES)).T for part in code_parts], 0)
    code = code.astype(jnp.int32)
    cell = jnp.where(code >= 0, code >> 2, -1)
    kind = jnp.where(code >= 0, code & 3, -1)

    depth = ROWS * WIDE
    padded = (depth + LANES - 1) // LANES * LANES
    places = cell_of(iota((1, padded), 1), range(ROWS))
    hot = jnp.concatenate(
        [
            jnp.where(places[:, t : t + LANES] == cell, 1.0, 0.0).astype(jnp.bfloat16)
            for t in range(0, padded, LANES)
        ],
        1,
    )
    state = jnp.concatenate(split(f[STEPS : STEPS + ROWS].reshape(depth, LANES)), 1)
    state = jnp.concatenate([state, jnp.zeros((padded - depth, 2 * LANES), jnp.bfloat16)], 0)
    column = halves(matmul(hot, state))

    masks = [kind == n for n in range(3)]
    op_high, op_low = split(operator[...])
    zero = jnp.zeros((LANES, LANES), jnp.bfloat16)

    def by_kind(x):
        return jnp.concatenate([jnp.where(m, part, jnp.zeros_like(part)) for part in split(x) for m in masks], 1)

    forward = jnp.concatenate(
        [jnp.concatenate([op_high[n], op_low[n]], 1) for n in range(3)]
        + [jnp.concatenate([op_high[n], zero], 1) for n in range(3)],
        0,
    )
    model = halves(matmul(by_kind(column), forward))
    values = slots_in[:, 0:bucket, :].reshape(slots, LANES)
    weights = slots_in[:, bucket : 2 * bucket, :].reshape(slots, LANES)
    departures = jnp.where(code >= 0, values - model, 0.0)
    dep_out[...] = departures
    backward = jnp.concatenate(
        [
            jnp.concatenate([op_high[0], op_high[1], op_high[2]] * 2, 1),
            jnp.concatenate([op_low[0], op_low[1], op_low[2], zero, zero, zero], 1),
        ],
        0,
    )
    adjoint = halves(matmul(by_kind(weights * departures), backward, ((1,), (1,))))
    adj_out[...] = adjoint
    forcing = scatter(adjoint, code_row, range(ROWS))
    for r in range(ROWS):
        f_out[r] = forcing[r * WIDE : (r + 1) * WIDE]
    for r in range(ROWS):
        w_out[r] = f_out[r, pl.ds(8 * STEPS, STEPS, stride=8), :]
        e_out[r] = f_out[r, pl.ds(8 * (LANES - 7 * REGS) + 7, STEPS, stride=8), :]


def last_kernel(inc, f_in, co, from_west, from_east, a_in, b_in, out, f, spare, cl, ct, cc, wide):
    rims = 8 * ROWS
    slots = (a_in.shape[0] - rims) * LANES // (LANES + 8)
    even, pole = position()
    a_base, b_base, a_rows, b_rows = halo_places(even, pole)
    sign = wind_sign(pole, (1, LANES))
    west, east = (pl.ds(0, STEPS, stride=8), pl.ds(8 * (REGS - STEPS) + 7, STEPS, stride=8))

    def halo(ref, rows, base, scale):
        codes = [ref[rims + slots + 8 * t : rims + slots + 8 * t + 1, :] for t in range(slots // LANES)]
        got = scatter(ref[rims : rims + slots, :], jnp.concatenate(codes, 1), rows)
        for k in range(STEPS):
            f[base + k] = got[k * WIDE : (k + 1) * WIDE] * scale
            rim = ref[pl.ds(pl.multiple_of(8 * rows[k], 8), 8), :] * scale
            f[base + k, west, :] = rim[0:STEPS]
            f[base + k, east, :] = rim[STEPS : 2 * STEPS]

    halo(a_in, a_rows, a_base, 1.0)
    halo(b_in, b_rows, b_base, sign)
    for r in range(ROWS):
        f[STEPS + r] = f_in[r]
        f[STEPS + r, west, :] = from_west[r]
        f[STEPS + r, east, :] = from_east[r]
    expand(co, cl, ct, cc)

    def store(r, q, value):
        wide[r, pl.ds(8 - STEPS + q, 8, stride=REGS), :] = value

    diffuse(f, spare, cl, ct, cc, store)
    for r in range(ROWS):
        at = pl.ds(r, LANES, stride=ROWS)
        out[at, :] = inc[at, :] - wide[r, 8 : 8 + LANES, :].T


def call(kernel, outs, args, scratch=(), spaces=None, flops=0, limit=48):
    spaces = spaces or {}
    specs = [pl.BlockSpec(memory_space=spaces.get(n, VMEM)) for n in range(len(args))]
    size = 4 * sum(x.size for x in list(args) + list(outs))
    return pl.pallas_call(
        kernel,
        out_shape=outs,
        in_specs=specs,
        out_specs=[pl.BlockSpec(memory_space=VMEM) for _ in outs],
        scratch_shapes=list(scratch),
        compiler_params=pltpu.CompilerParams(vmem_limit_bytes=limit * MIB),
        cost_estimate=pl.CostEstimate(flops=flops, bytes_accessed=size, transcendentals=0),
    )(*args)


def routes():
    lons, lats = (lax.axis_size("lon"), lax.axis_size("lat"))
    at = lambda lon, lat: lon % lons * lats + lat
    cells = [(lon, lat) for lon in range(lons) for lat in range(lats)]
    inner = [(at(o, a), at(o, a ^ 1)) for o, a in cells]
    outer = []
    for o, a in cells:
        if a in (0, lats - 1):
            outer.append((at(o, a), at(o + lons // 2, a)))
        else:
            outer.append((at(o, a), at(o, a - 1 if a % 2 == 0 else a + 1)))
    east = [(at(o, a), at(o + 1, a)) for o, a in cells]
    west = [(at(o, a), at(o - 1, a)) for o, a in cells]
    return inner, outer, east, west


def local(
    increment, coef_lon, coef_lat, obs_values, obs_weight, obs_operator, obs_columns, obs_types, obs_counts
):
    shape = lambda *dims: jax.ShapeDtypeStruct(dims, F32)
    inner, outer, east, west = routes()
    send = lambda x, route: lax.ppermute(x, ("lon", "lat"), route)
    lats = lax.axis_size("lat")
    slots = obs_values.shape[0]
    bucket = slots // lats
    tiles = slots // LANES
    fields = increment.shape[0]
    inc = increment.reshape(-1, LANES)
    cl = coef_lon.reshape(fields * ROWS, LANES)
    ct = coef_lat.reshape(fields * ROWS, LANES)

    own, coef, b_send, a_send, w_send, e_send = call(
        pack_kernel,
        [
            shape(ROWS, LANES, LANES),
            shape(LANES, LANES),
            shape(STEPS * (LANES + 8), LANES),
            shape(STEPS * (LANES + 8), LANES),
            shape(ROWS + 1, STEPS, LANES),
            shape(ROWS + 1, STEPS, LANES),
        ],
        [inc, cl, ct],
        [
            VMEM(inc.shape, F32),
            VMEM(cl.shape, F32),
            VMEM(ct.shape, F32),
            VMEM((LANES, LANES), F32),
            pltpu.SemaphoreType.DMA((3,)),
        ],
        spaces={0: HBM, 1: HBM, 2: HBM},
    )
    b_in = send(b_send, outer)
    from_west = send(e_send, east)
    from_east = send(w_send, west)
    a_in = send(a_send, inner)
    (slots_send,) = call(
        slots_kernel,
        [shape(lats, 2 * bucket + 8, LANES)],
        [
            obs_counts,
            obs_values.reshape(lats, bucket, LANES),
            obs_weight.reshape(lats, bucket, LANES),
            obs_columns.reshape(1, slots),
            obs_types.reshape(1, slots),
        ],
        spaces={0: pltpu.SMEM},
    )
    slots_in = lax.all_to_all(slots_send, "lat", split_axis=0, concat_axis=0, tiled=True)
    rim_send = jnp.concatenate([from_west, from_east], 1)
    rim_a = send(rim_send, inner)
    rim_b = send(rim_send, outer)
    grid = VMEM((PLANES, WIDE, LANES), F32)
    departures, adjoint, code, w_send, e_send, forcing, co = call(
        middle_kernel,
        [
            shape(slots, LANES),
            shape(slots, LANES),
            shape(8 * tiles, LANES),
            shape(ROWS, STEPS, LANES),
            shape(ROWS, STEPS, LANES),
            shape(ROWS, WIDE, LANES),
            shape(PADDED, LANES),
        ],
        [own, coef, a_in, b_in, from_west, from_east, rim_a, rim_b, slots_in, obs_operator],
        [VMEM((PLANES, PADDED, LANES), F32), VMEM((LANES, LANES), F32)] + [grid] * 5,
        flops=10**8,
    )
    from_west = send(e_send, east)
    from_east = send(w_send, west)
    back = lax.all_to_all(
        departures.reshape(lats, bucket, LANES), "lat", split_axis=0, concat_axis=0, tiled=True
    )
    rims = jnp.concatenate([from_west, from_east], 1).reshape(8 * ROWS, LANES)
    payload = jnp.concatenate([rims, adjoint, code], 0)
    a_in = send(payload, inner)
    b_in = send(payload, outer)
    (gradient,) = call(
        last_kernel,
        [shape(*inc.shape)],
        [inc, forcing, co, from_west, from_east, a_in, b_in],
        [grid] * 5 + [VMEM((ROWS, PADDED, LANES), F32)],
        flops=10**8,
    )
    return (gradient.reshape(increment.shape), back.reshape(slots, LANES))


def solution(mesh):
    return jax.shard_map(
        local,
        mesh=mesh,
        in_specs=(
            P(None, None, "lat", "lon"),
            P(None, "lat", "lon"),
            P(None, "lat", "lon"),
            P(("lon", "lat"), None),
            P(("lon", "lat"), None),
            P(),
            P(("lon", "lat")),
            P(("lon", "lat")),
            P(("lon", "lat")),
        ),
        out_specs=(P(None, None, "lat", "lon"), P(("lon", "lat"), None)),
        check_vma=False,
    )
```

```python
import functools

import jax
import jax.numpy as jnp
from jax import lax
from jax.experimental import pallas as pl
from jax.experimental.pallas import tpu as pltpu
from jax.sharding import PartitionSpec as P

STEPS = 4
ROWS = 8
LANES = 128
PLANES = ROWS + 2 * STEPS
WIDE = LANES + 2 * STEPS
REGS = WIDE // 8
PADDED = LANES + 16
VMEM = pltpu.VMEM
HBM = pltpu.HBM
MIB = 1 << 20
LONG = 10**10
F32 = jnp.float32


def iota(shape, axis):
    return lax.broadcasted_iota(jnp.int32, shape, axis)


def position():
    lat, count = (lax.axis_index("lat"), lax.axis_size("lat"))
    return lat % 2 == 0, jnp.logical_or(lat == 0, lat == count - 1)


def halo_places(even, pole):
    a_base = jnp.where(even, PLANES - STEPS, 0)
    b_base = jnp.where(even, 0, PLANES - STEPS)
    a_rows = [jnp.where(even, k, STEPS + k) for k in range(STEPS)]
    b_rows = [
        jnp.where(
            pole,
            jnp.where(even, STEPS - 1 - k, ROWS - 1 - k),
            jnp.where(even, STEPS + k, k),
        )
        for k in range(STEPS)
    ]
    return a_base, b_base, a_rows, b_rows


def wind_sign(pole, shape):
    flipped = jnp.logical_and(iota(shape, len(shape) - 1) >= LANES // 2, pole)
    return jnp.where(flipped, -1.0, 1.0).astype(F32)


def split(x):
    high = x.astype(jnp.bfloat16)
    low = (x - high.astype(F32)).astype(jnp.bfloat16)
    return high, low


def matmul(a, b, dims=((1,), (0,))):
    return lax.dot_general(a, b, (dims, ((), ())), preferred_element_type=F32)


def halves(x):
    return x[:, :LANES] + x[:, LANES:]


def pack_kernel(
    inc_hbm, cl_hbm, ct_hbm, values, weights, columns_hbm, types_hbm, counts_hbm,
    own, coef, b_out, a_out, rim_out, w_out, e_out, slots_out,
    inc, cl, ct, raw, columns, types, counts, sems,
):
    owners, bucket = (slots_out.shape[0], values.shape[1])
    moves = (
        (inc_hbm, inc),
        (cl_hbm, cl),
        (ct_hbm, ct),
        (columns_hbm, columns),
        (types_hbm, types),
        (counts_hbm, counts),
        (values, slots_out.at[:, pl.ds(0, bucket), :]),
        (weights, slots_out.at[:, pl.ds(bucket, bucket), :]),
    )
    copies = [pltpu.make_async_copy(src, dst, sems.at[n]) for n, (src, dst) in enumerate(moves)]
    for copy in copies:
        copy.start()
    for copy in copies[:3]:
        copy.wait()
    fields = cl.shape[0] // ROWS
    even, _ = position()
    raw[...] = jnp.zeros(raw.shape, F32)
    for r in range(ROWS):
        own[r] = inc[pl.ds(r, LANES, stride=ROWS), :].T
        at = 8 * (STEPS + r)
        raw[at : at + fields, :] = cl[pl.ds(r, fields, stride=ROWS), :]
        raw[at + fields : at + 2 * fields, :] = ct[pl.ds(r, fields, stride=ROWS), :]
        w_out[r] = own[r, 0:STEPS, :]
        e_out[r] = own[r, LANES - STEPS : LANES, :]
    coef[...] = raw[...].T
    w_out[ROWS] = coef[0:STEPS, :]
    e_out[ROWS] = coef[LANES - STEPS : LANES, :]
    a_row = jnp.where(even, STEPS, 0)
    b_row = STEPS - a_row
    for out, first in ((b_out, b_row), (a_out, a_row)):
        for k in range(STEPS):
            out[k * LANES : (k + 1) * LANES, :] = own[first + k]
            at = STEPS * LANES + 8 * k
            out[at : at + 8, :] = raw[pl.ds(pl.multiple_of(8 * (STEPS + first + k), 8), 8), :]
    rim = jnp.concatenate([coef[0:STEPS, :], coef[LANES - STEPS : LANES, :]], 0)
    rim_out[STEPS] = rim
    a_out[STEPS * (LANES + 16) : STEPS * (LANES + 16) + 8, :] = rim
    for k in range(STEPS):
        rim_out[k, 0:STEPS, :] = own[b_row + k, 0:STEPS, :]
        rim_out[k, STEPS : 2 * STEPS, :] = own[b_row + k, LANES - STEPS : LANES, :]
        at = STEPS * (LANES + 8) + 8 * k
        a_out[at : at + STEPS, :] = own[a_row + k, 0:STEPS, :]
        a_out[at + STEPS : at + 2 * STEPS, :] = own[a_row + k, LANES - STEPS : LANES, :]
    for copy in copies[3:]:
        copy.wait()
    slots = columns.shape[1]
    lane = iota((1, slots), 1)
    limit = jnp.zeros((1, slots), jnp.int32)
    for d in range(owners):
        limit = jnp.where(lane // bucket == d, counts[d], limit)
    code = jnp.where(lane % bucket < limit, columns[...] * 4 + types[...], -1).astype(F32)
    for d in range(owners):
        at = d * bucket
        window = code[:, at // LANES * LANES : at // LANES * LANES + LANES]
        moved = pltpu.roll(window, (-at) % LANES, 1)
        slots_out[d, 2 * bucket : 2 * bucket + 8, :] = jnp.broadcast_to(moved, (8, LANES))


def edge_kernel(w_own, e_own, a_in, rim_b, w_out, e_out):
    even, pole = position()
    a_base, b_base, _, b_rows = halo_places(even, pole)
    sign = wind_sign(pole, (1, LANES))
    at = STEPS * (LANES + 8)
    for k in range(STEPS):
        rim = a_in[at + 8 * k : at + 8 * k + 8, :]
        w_out[a_base + k] = rim[0:STEPS]
        e_out[a_base + k] = rim[STEPS : 2 * STEPS]
        rim = rim_b[jnp.where(pole, STEPS - 1 - k, k)] * sign
        w_out[b_base + k] = rim[0:STEPS]
        e_out[b_base + k] = rim[STEPS : 2 * STEPS]
    for r in range(ROWS):
        w_out[STEPS + r] = w_own[r]
        e_out[STEPS + r] = e_own[r]
    at += 8 * STEPS
    plane = iota((8, LANES), 1) // 8
    tile = jnp.concatenate([w_own[ROWS], e_own[ROWS]], 0)
    from_a = pltpu.roll(a_in[at : at + 8, :], LANES // 2, 1)
    tile = jnp.where(plane // STEPS == a_base // STEPS, from_a, tile)
    for k in range(STEPS):
        shift = (8 * (b_base + k - STEPS - b_rows[k]) + 2 * LANES) % LANES
        tile = jnp.where(plane == b_base + k, pltpu.roll(rim_b[STEPS], shift, 1), tile)
    w_out[PLANES] = tile[0:STEPS]
    e_out[PLANES] = tile[STEPS : 2 * STEPS]


def coefs_wide(coef, a_in, b_in, from_west, from_east, raw, co_out, even, pole):
    a_base, b_base, _, _ = halo_places(even, pole)
    raw[...] = jnp.zeros(raw.shape, F32)
    for k in range(STEPS):
        kk = jnp.where(pole, STEPS - 1 - k, k)
        at = STEPS * LANES
        raw[pl.ds(pl.multiple_of(8 * (a_base + k), 8), 8), :] = a_in[at + 8 * k : at + 8 * k + 8, :]
        raw[pl.ds(pl.multiple_of(8 * (b_base + k), 8), 8), :] = b_in[pl.ds(pl.multiple_of(at + 8 * kk, 8), 8), :]
    co_out[8 : 8 + LANES, :] = raw[...].T + coef[...]
    co_out[8 - STEPS : 8, :] = from_west[PLANES]
    co_out[8 + LANES : 8 + LANES + STEPS, :] = from_east[PLANES]


def expand(co, cl, ct, cc):
    wide = jnp.concatenate([co[pl.ds(8 - STEPS + q, 8, stride=REGS), :] for q in range(REGS)], 0)
    high, low = split(wide)
    tall = 2 * LANES - 16
    row, col = (iota((tall, 2 * LANES), 0), iota((tall, 2 * LANES), 1))
    wanted = LANES - 16 + col // LANES * 4 + col % LANES // (LANES // 4)
    picks = [jnp.where(row == wanted + 8 * odd, 1.0, 0.0).astype(jnp.bfloat16) for odd in range(2)]
    for p in range(PLANES):
        first = LANES - 16 - p // 2 * 16
        pick = picks[p % 2][first : first + LANES, :]
        both = matmul(high, pick) + matmul(low, pick)
        a, b = (both[:, :LANES], both[:, LANES:])
        cl[p] = a
        ct[p] = b
        cc[p] = 1.0 - 2.0 * (a * a + b * b)


def diffuse(f, spare, cl, ct, cc, store):
    for step in range(STEPS):
        last = step == STEPS - 1

        def row(p, carry, f=f, spare=spare, last=last):
            regs = [pl.ds(8 * q, 8) for q in range(REGS)]
            here = [f[p, at, :] for at in regs]
            g = [cl[p, at, :] * x for at, x in zip(regs, here)]
            g = [pltpu.roll(g[-1], 1, 0)] + g + [pltpu.roll(g[0], 7, 0)]
            for q, at in enumerate(regs):
                sides = ct[p + 1, at, :] * f[p + 1, at, :] + ct[p - 1, at, :] * f[p - 1, at, :]
                new = cc[p, at, :] * here[q] + cl[p, at, :] * (g[q] + g[q + 2]) + ct[p, at, :] * sides
                if last:
                    store(p - STEPS, q, new)
                else:
                    spare[p, at, :] = new
            return carry

        lax.fori_loop(step + 1, PLANES - 1 - step, row, 0)
        f, spare = (spare, f)


def cell_of(n, rows):
    plane = (n * 482) >> 16
    rest = n - WIDE * plane
    column = (rest % 8) * REGS + rest // 8 - STEPS
    row = jnp.full(n.shape, -1, jnp.int32)
    for k, r in enumerate(rows):
        row = jnp.where(plane == k, r, row)
    inside = jnp.logical_and(jnp.logical_and(column >= 0, column < LANES), row >= 0)
    return jnp.where(inside, row * LANES + column, -2)


def scatter(adjoint, code_row, rows):
    high, low = split(adjoint)
    code = code_row.astype(jnp.int32)
    cell = jnp.where(code >= 0, code >> 2, -1)
    places = cell_of(iota((len(rows) * WIDE, LANES), 0), rows)
    hot = jnp.concatenate(
        [
            jnp.where(places == cell[:, t * LANES : (t + 1) * LANES], 1.0, 0.0).astype(jnp.bfloat16)
            for t in range(cell.shape[1] // LANES)
        ],
        1,
    )
    return halves(matmul(hot, jnp.concatenate([high, low], 1)))


def middle_kernel(
    own, coef, a_in, b_in, from_west, from_east, slots_in, operator,
    dep_out, adj_out, code_out, w_out, e_out, f_out, co,
    wide, raw, f, spare, cl, ct, cc, state,
):
    owners, bucket = (slots_in.shape[0], (slots_in.shape[1] - 8) // 2)
    slots = owners * bucket
    even, pole = position()
    a_base, b_base, _, _ = halo_places(even, pole)
    sign = wind_sign(pole, (1, LANES))
    inner = slice(8, 8 + LANES)
    coefs_wide(coef, a_in, b_in, from_west, from_east, raw, co, even, pole)
    expand(co, cl, ct, cc)
    for k in range(STEPS):
        wide[a_base + k, inner, :] = a_in[k * LANES : (k + 1) * LANES, :]
        at = pl.multiple_of(jnp.where(pole, STEPS - 1 - k, k) * LANES, LANES)
        wide[b_base + k, inner, :] = b_in[pl.ds(at, LANES), :] * sign
    for r in range(ROWS):
        wide[STEPS + r, inner, :] = own[r]
    for p in range(PLANES):
        wide[p, 8 - STEPS : 8, :] = from_west[p]
        wide[p, 8 + LANES : 8 + LANES + STEPS, :] = from_east[p]

    def interleave(p, carry):
        for q in range(REGS):
            f[p, pl.ds(8 * q, 8), :] = wide[p, pl.ds(8 - STEPS + q, 8, stride=REGS), :]
        return carry

    lax.fori_loop(0, PLANES, interleave, 0)

    def store(r, q, value):
        state[r, pl.ds(8 * q, 8), :] = value

    diffuse(f, spare, cl, ct, cc, store)

    lane = iota((1, LANES), 1)
    per_tile = LANES // bucket
    code_parts = []
    for t in range(slots // LANES):
        part = jnp.full((1, LANES), -1.0, F32)
        for n in range(per_tile):
            got = slots_in[t * per_tile + n, 2 * bucket : 2 * bucket + 1, :]
            part = jnp.where(lane // bucket == n, pltpu.roll(got, n * bucket, 1), part)
        code_parts.append(part)
        code_out[8 * t : 8 * t + 8, :] = jnp.broadcast_to(part, (8, LANES))
    code_row = jnp.concatenate(code_parts, 1)
    code = jnp.concatenate([jnp.broadcast_to(part, (LANES, LANES)).T for part in code_parts], 0)
    code = code.astype(jnp.int32)
    cell = jnp.where(code >= 0, code >> 2, -1)
    kind = jnp.where(code >= 0, code & 3, -1)

    depth = ROWS * WIDE
    padded = (depth + LANES - 1) // LANES * LANES
    places = cell_of(iota((1, padded), 1), range(ROWS))
    hot = jnp.concatenate(
        [
            jnp.where(places[:, t : t + LANES] == cell, 1.0, 0.0).astype(jnp.bfloat16)
            for t in range(0, padded, LANES)
        ],
        1,
    )
    cells = jnp.concatenate(split(state[...].reshape(depth, LANES)), 1)
    cells = jnp.concatenate([cells, jnp.zeros((padded - depth, 2 * LANES), jnp.bfloat16)], 0)
    column = halves(matmul(hot, cells))

    masks = [kind == n for n in range(3)]
    op_high, op_low = split(operator[...])
    zero = jnp.zeros((LANES, LANES), jnp.bfloat16)

    def by_kind(x):
        return jnp.concatenate([jnp.where(m, part, jnp.zeros_like(part)) for part in split(x) for m in masks], 1)

    forward = jnp.concatenate(
        [jnp.concatenate([op_high[n], op_low[n]], 1) for n in range(3)]
        + [jnp.concatenate([op_high[n], zero], 1) for n in range(3)],
        0,
    )
    model = halves(matmul(by_kind(column), forward))
    values = slots_in[:, 0:bucket, :].reshape(slots, LANES)
    weights = slots_in[:, bucket : 2 * bucket, :].reshape(slots, LANES)
    departures = jnp.where(code >= 0, values - model, 0.0)
    dep_out[...] = departures
    backward = jnp.concatenate(
        [
            jnp.concatenate([op_high[0], op_high[1], op_high[2]] * 2, 1),
            jnp.concatenate([op_low[0], op_low[1], op_low[2], zero, zero, zero], 1),
        ],
        0,
    )
    adjoint = halves(matmul(by_kind(weights * departures), backward, ((1,), (1,))))
    adj_out[...] = adjoint
    forcing = scatter(adjoint, code_row, range(ROWS))
    for r in range(ROWS):
        f_out[r] = forcing[r * WIDE : (r + 1) * WIDE]
    for r in range(ROWS):
        w_out[r] = f_out[r, pl.ds(8 * STEPS, STEPS, stride=8), :]
        e_out[r] = f_out[r, pl.ds(8 * (LANES - 7 * REGS) + 7, STEPS, stride=8), :]


def last_kernel(inc, f_in, cl, ct, cc, from_west, from_east, a_in, b_in, out, f, spare, wide):
    rims = 8 * ROWS
    slots = (a_in.shape[0] - rims) * LANES // (LANES + 8)
    even, pole = position()
    a_base, b_base, a_rows, b_rows = halo_places(even, pole)
    sign = wind_sign(pole, (1, LANES))
    west, east = (pl.ds(0, STEPS, stride=8), pl.ds(8 * (REGS - STEPS) + 7, STEPS, stride=8))

    def halo(ref, rows, base, scale):
        codes = [ref[rims + slots + 8 * t : rims + slots + 8 * t + 1, :] for t in range(slots // LANES)]
        got = scatter(ref[rims : rims + slots, :], jnp.concatenate(codes, 1), rows)
        for k in range(STEPS):
            f[base + k] = got[k * WIDE : (k + 1) * WIDE] * scale
            rim = ref[pl.ds(pl.multiple_of(8 * rows[k], 8), 8), :] * scale
            f[base + k, west, :] = rim[0:STEPS]
            f[base + k, east, :] = rim[STEPS : 2 * STEPS]

    halo(a_in, a_rows, a_base, 1.0)
    halo(b_in, b_rows, b_base, sign)
    for r in range(ROWS):
        f[STEPS + r] = f_in[r]
        f[STEPS + r, west, :] = from_west[r]
        f[STEPS + r, east, :] = from_east[r]

    def store(r, q, value):
        wide[r, pl.ds(8 - STEPS + q, 8, stride=REGS), :] = value

    diffuse(f, spare, cl, ct, cc, store)
    for r in range(ROWS):
        at = pl.ds(r, LANES, stride=ROWS)
        out[at, :] = inc[at, :] - wide[r, 8 : 8 + LANES, :].T


def call(kernel, outs, args, scratch=(), spaces=None, flops=0, limit=20):
    spaces = spaces or {}
    specs = [pl.BlockSpec(memory_space=spaces.get(n, VMEM)) for n in range(len(args))]
    size = 4 * sum(x.size for x in list(args) + list(outs))
    args = [pltpu.with_memory_space_constraint(x, HBM) if spaces.get(n) is HBM else x for n, x in enumerate(args)]
    return pl.pallas_call(
        kernel,
        out_shape=outs,
        in_specs=specs,
        out_specs=[pl.BlockSpec(memory_space=VMEM) for _ in outs],
        scratch_shapes=list(scratch),
        compiler_params=pltpu.CompilerParams(vmem_limit_bytes=limit * MIB),
        cost_estimate=pl.CostEstimate(flops=flops, bytes_accessed=size, transcendentals=0),
    )(*args)


def routes():
    lons, lats = (lax.axis_size("lon"), lax.axis_size("lat"))
    at = lambda lon, lat: lon % lons * lats + lat
    cells = [(lon, lat) for lon in range(lons) for lat in range(lats)]
    inner = [(at(o, a), at(o, a ^ 1)) for o, a in cells]
    outer = []
    for o, a in cells:
        if a in (0, lats - 1):
            outer.append((at(o, a), at(o + lons // 2, a)))
        else:
            outer.append((at(o, a), at(o, a - 1 if a % 2 == 0 else a + 1)))
    east = [(at(o, a), at(o + 1, a)) for o, a in cells]
    west = [(at(o, a), at(o - 1, a)) for o, a in cells]
    return inner, outer, east, west


def local(
    increment, coef_lon, coef_lat, obs_values, obs_weight, obs_operator, obs_columns, obs_types, obs_counts
):
    shape = lambda *dims: jax.ShapeDtypeStruct(dims, F32)
    inner, outer, east, west = routes()
    send = lambda x, route: lax.ppermute(x, ("lon", "lat"), route)
    lats = lax.axis_size("lat")
    slots = obs_values.shape[0]
    bucket = slots // lats
    tiles = slots // LANES
    fields = increment.shape[0]
    inc = increment.reshape(-1, LANES)
    cl = coef_lon.reshape(fields * ROWS, LANES)
    ct = coef_lat.reshape(fields * ROWS, LANES)

    own, coef, b_send, a_send, rim_send, w_own, e_own, slots_send = call(
        pack_kernel,
        [
            shape(ROWS, LANES, LANES),
            shape(LANES, LANES),
            shape(STEPS * (LANES + 8), LANES),
            shape(STEPS * (LANES + 16) + 8, LANES),
            shape(STEPS + 1, 8, LANES),
            shape(ROWS + 1, STEPS, LANES),
            shape(ROWS + 1, STEPS, LANES),
            shape(lats, 2 * bucket + 8, LANES),
        ],
        [
            inc,
            cl,
            ct,
            obs_values.reshape(lats, bucket, LANES),
            obs_weight.reshape(lats, bucket, LANES),
            obs_columns.reshape(1, slots),
            obs_types.reshape(1, slots),
            obs_counts,
        ],
        [
            VMEM(inc.shape, F32),
            VMEM(cl.shape, F32),
            VMEM(ct.shape, F32),
            VMEM((LANES, LANES), F32),
            VMEM((1, slots), jnp.int32),
            VMEM((1, slots), jnp.int32),
            pltpu.SMEM(obs_counts.shape, jnp.int32),
            pltpu.SemaphoreType.DMA((8,)),
        ],
        spaces={n: HBM for n in range(8)},
    )
    rim_b = send(rim_send, outer)
    a_in = send(a_send, inner)
    b_in = send(b_send, outer)
    slots_in = lax.all_to_all(slots_send, "lat", split_axis=0, concat_axis=0, tiled=True)
    edge = shape(PLANES + 1, STEPS, LANES)
    w_send, e_send = call(edge_kernel, [edge, edge], [w_own, e_own, a_in, rim_b])
    from_west = send(e_send, east)
    from_east = send(w_send, west)
    grid = VMEM((PLANES, WIDE, LANES), F32)
    planes = shape(PLANES, WIDE, LANES)
    departures, adjoint, code, w_send, e_send, forcing, co = call(
        middle_kernel,
        [
            shape(slots, LANES),
            shape(slots, LANES),
            shape(8 * tiles, LANES),
            shape(ROWS, STEPS, LANES),
            shape(ROWS, STEPS, LANES),
            shape(ROWS, WIDE, LANES),
            shape(PADDED, LANES),
        ],
        [own, coef, a_in, b_in, from_west, from_east, slots_in, obs_operator],
        [VMEM((PLANES, PADDED, LANES), F32), VMEM((LANES, LANES), F32)]
        + [grid] * 5
        + [VMEM((ROWS, WIDE, LANES), F32)],
        flops=10**8,
    )
    from_west = send(e_send, east)
    from_east = send(w_send, west)
    back = lax.all_to_all(
        departures.reshape(lats, bucket, LANES), "lat", split_axis=0, concat_axis=0, tiled=True
    )
    rims = jnp.concatenate([from_west, from_east], 1).reshape(8 * ROWS, LANES)
    payload = jnp.concatenate([rims, adjoint, code], 0)
    a_in = send(payload, inner)
    b_in = send(payload, outer)
    wl, wt, wc = call(expand, [planes, planes, planes], [co], flops=10**8)
    (gradient,) = call(
        last_kernel,
        [shape(*inc.shape)],
        [inc, forcing, wl, wt, wc, from_west, from_east, a_in, b_in],
        [grid] * 2 + [VMEM((ROWS, PADDED, LANES), F32)],
        flops=LONG,
    )
    gradient, back = lax.optimization_barrier((gradient, back))
    return (gradient.reshape(increment.shape), back.reshape(slots, LANES))


def solution(mesh):
    return jax.shard_map(
        local,
        mesh=mesh,
        in_specs=(
            P(None, None, "lat", "lon"),
            P(None, "lat", "lon"),
            P(None, "lat", "lon"),
            P(("lon", "lat"), None),
            P(("lon", "lat"), None),
            P(),
            P(("lon", "lat")),
            P(("lon", "lat")),
            P(("lon", "lat")),
        ),
        out_specs=(P(None, None, "lat", "lon"), P(("lon", "lat"), None)),
        check_vma=False,
    )
```

```python
import functools

import jax
import jax.numpy as jnp
from jax import lax
from jax.experimental import pallas as pl
from jax.experimental.pallas import tpu as pltpu
from jax.sharding import PartitionSpec as P

STEPS = 4
ROWS = 8
LANES = 128
PLANES = ROWS + 2 * STEPS
BODY = LANES // 8
RIM = 3
SIDE = 4 * RIM
VMEM = pltpu.VMEM
HBM = pltpu.HBM
MIB = 1 << 20
EDGE_COST = 10**10
EXPAND_COST = 10**8
STATE_COST = 10**9
SMOOTH_COST = 10**10
F32 = jnp.float32


def iota(shape, axis):
    return lax.broadcasted_iota(jnp.int32, shape, axis)


def position():
    lat, count = (lax.axis_index("lat"), lax.axis_size("lat"))
    return lat % 2 == 0, jnp.logical_or(lat == 0, lat == count - 1)


def halo_places(even, pole):
    a_base = jnp.where(even, PLANES - STEPS, 0)
    b_base = jnp.where(even, 0, PLANES - STEPS)
    a_rows = [jnp.where(even, k, STEPS + k) for k in range(STEPS)]
    b_rows = [
        jnp.where(
            pole,
            jnp.where(even, STEPS - 1 - k, ROWS - 1 - k),
            jnp.where(even, STEPS + k, k),
        )
        for k in range(STEPS)
    ]
    return a_base, b_base, a_rows, b_rows


def wind_sign(pole, shape):
    flipped = jnp.logical_and(iota(shape, len(shape) - 1) >= LANES // 2, pole)
    return jnp.where(flipped, -1.0, 1.0).astype(F32)


def split(x):
    high = x.astype(jnp.bfloat16)
    low = (x - high.astype(F32)).astype(jnp.bfloat16)
    return high, low


def matmul(a, b, dims=((1,), (0,))):
    return lax.dot_general(a, b, (dims, ((), ())), preferred_element_type=F32)


def halves(x):
    return x[:, :LANES] + x[:, LANES:]


def pack_kernel(
    inc_hbm, cl_hbm, ct_hbm, values, weights, columns_hbm, types_hbm, counts_hbm,
    own, coef, b_out, a_out, rim_b, rim_a, w_out, e_out, slots_out,
    inc, cl, ct, raw, columns, types, counts, sems,
):
    owners, bucket = (slots_out.shape[0], values.shape[1])
    moves = (
        (inc_hbm, inc),
        (cl_hbm, cl),
        (ct_hbm, ct),
        (columns_hbm, columns),
        (types_hbm, types),
        (counts_hbm, counts),
        (values, slots_out.at[:, pl.ds(0, bucket), :]),
        (weights, slots_out.at[:, pl.ds(bucket, bucket), :]),
    )
    copies = [pltpu.make_async_copy(src, dst, sems.at[n]) for n, (src, dst) in enumerate(moves)]
    for copy in copies:
        copy.start()
    for copy in copies[:3]:
        copy.wait()
    fields = cl.shape[0] // ROWS
    even, _ = position()
    raw[...] = jnp.zeros(raw.shape, F32)
    for r in range(ROWS):
        own[r] = inc[pl.ds(r, LANES, stride=ROWS), :].T
        at = 8 * (STEPS + r)
        raw[at : at + fields, :] = cl[pl.ds(r, fields, stride=ROWS), :]
        raw[at + fields : at + 2 * fields, :] = ct[pl.ds(r, fields, stride=ROWS), :]
        w_out[r] = own[r, 0:STEPS, :]
        e_out[r] = own[r, LANES - STEPS : LANES, :]
    coef[...] = raw[...].T
    w_out[ROWS] = coef[0:STEPS, :]
    e_out[ROWS] = coef[LANES - STEPS : LANES, :]
    a_row = jnp.where(even, STEPS, 0)
    b_row = STEPS - a_row
    for out, first in ((b_out, b_row), (a_out, a_row)):
        for k in range(STEPS):
            out[k] = own[first + k]
    for out, first in ((rim_b, b_row), (rim_a, a_row)):
        for k in range(STEPS):
            out[k, 0:STEPS, :] = own[first + k, 0:STEPS, :]
            out[k, STEPS : 2 * STEPS, :] = own[first + k, LANES - STEPS : LANES, :]
            out[STEPS + 1 + k] = raw[pl.ds(pl.multiple_of(8 * (STEPS + first + k), 8), 8), :]
        out[STEPS, 0:STEPS, :] = coef[0:STEPS, :]
        out[STEPS, STEPS : 2 * STEPS, :] = coef[LANES - STEPS : LANES, :]
    for copy in copies[3:]:
        copy.wait()
    slots = columns.shape[1]
    lane = iota((1, slots), 1)
    limit = jnp.zeros((1, slots), jnp.int32)
    for d in range(owners):
        limit = jnp.where(lane // bucket == d, counts[d], limit)
    code = jnp.where(lane % bucket < limit, columns[...] * 4 + types[...], -1).astype(F32)
    for d in range(owners):
        at = d * bucket
        window = code[:, at // LANES * LANES : at // LANES * LANES + LANES]
        moved = pltpu.roll(window, (-at) % LANES, 1)
        slots_out[d, 2 * bucket : 2 * bucket + 8, :] = jnp.broadcast_to(moved, (8, LANES))


def edge_kernel(w_own, e_own, coef, rim_a, rim_b, w_out, e_out, co, raw):
    even, pole = position()
    a_base, b_base, _, b_rows = halo_places(even, pole)
    sign = wind_sign(pole, (1, LANES))
    raw[...] = jnp.zeros(raw.shape, F32)
    for k in range(STEPS):
        kk = jnp.where(pole, STEPS - 1 - k, k)
        w_out[a_base + k] = rim_a[k, 0:STEPS, :]
        e_out[a_base + k] = rim_a[k, STEPS : 2 * STEPS, :]
        rim = rim_b[kk] * sign
        w_out[b_base + k] = rim[0:STEPS]
        e_out[b_base + k] = rim[STEPS : 2 * STEPS]
        raw[pl.ds(pl.multiple_of(8 * (a_base + k), 8), 8), :] = rim_a[STEPS + 1 + k]
        raw[pl.ds(pl.multiple_of(8 * (b_base + k), 8), 8), :] = rim_b[STEPS + 1 + kk]
    for r in range(ROWS):
        w_out[STEPS + r] = w_own[r]
        e_out[STEPS + r] = e_own[r]
    plane = iota((8, LANES), 1) // 8
    tile = jnp.concatenate([w_own[ROWS], e_own[ROWS]], 0)
    from_a = pltpu.roll(rim_a[STEPS], LANES // 2, 1)
    tile = jnp.where(plane // STEPS == a_base // STEPS, from_a, tile)
    for k in range(STEPS):
        shift = (8 * (b_base + k - STEPS - b_rows[k]) + 2 * LANES) % LANES
        tile = jnp.where(plane == b_base + k, pltpu.roll(rim_b[STEPS], shift, 1), tile)
    w_out[PLANES] = tile[0:STEPS]
    e_out[PLANES] = tile[STEPS : 2 * STEPS]
    co[...] = raw[...].T + coef[...]


def expand(co, cl, ct, cc, regs=BODY):
    high, low = split(jnp.concatenate([co[pl.ds(q, 8, stride=regs), :] for q in range(regs)], 0))
    tall = 2 * LANES - 16
    row, col = (iota((tall, 2 * LANES), 0), iota((tall, 2 * LANES), 1))
    wanted = LANES - 16 + col // LANES * 4 + col % LANES // (LANES // 4)
    picks = [jnp.where(row == wanted + 8 * odd, 1.0, 0.0).astype(jnp.bfloat16) for odd in range(2)]
    for p in range(PLANES):
        first = LANES - 16 - p // 2 * 16
        pick = picks[p % 2][first : first + LANES, :]
        both = matmul(high, pick) + matmul(low, pick)
        a, b = (both[:, :LANES], both[:, LANES:])
        cl[p] = a
        ct[p] = b
        cc[p] = 1.0 - 2.0 * (a * a + b * b)


def diffuse(f, spare, cl, ct, cc, store):
    regs = [pl.ds(8 * q, 8) for q in range(f.shape[1] // 8)]
    for step in range(STEPS):
        last = step == STEPS - 1

        def row(p, carry, f=f, spare=spare, last=last):
            here = [f[p, at, :] for at in regs]
            g = [cl[p, at, :] * x for at, x in zip(regs, here)]
            g = [pltpu.roll(g[-1], 1, 0)] + g + [pltpu.roll(g[0], 7, 0)]
            for q, at in enumerate(regs):
                sides = ct[p + 1, at, :] * f[p + 1, at, :] + ct[p - 1, at, :] * f[p - 1, at, :]
                new = cc[p, at, :] * here[q] + cl[p, at, :] * (g[q] + g[q + 2]) + ct[p, at, :] * sides
                if last:
                    store(p - STEPS, q, new)
                else:
                    spare[p, at, :] = new
            return carry

        lax.fori_loop(step + 1, PLANES - 1 - step, row, 0)
        f, spare = (spare, f)


def diffuse_rim(rim, f, spare, cl, ct, cc, west, east):
    for p in range(PLANES):
        rim[p, 0:STEPS, :] = west[p]
        rim[p, 2 * SIDE - STEPS : 2 * SIDE, :] = east[p]
        for q in range(RIM):
            f[p, 8 * q : 8 * q + 8, :] = rim[p, pl.ds(q, 8, stride=RIM), :]

    def store(r, q, value):
        rim[STEPS + r, pl.ds(q, 8, stride=RIM), :] = value

    diffuse(f, spare, cl, ct, cc, store)


def body_cell(n, rows):
    rest = n % LANES
    row = jnp.zeros(n.shape, jnp.int32)
    for k, r in enumerate(rows):
        row = jnp.where(n // LANES == k, r, row)
    return row * LANES + (rest % 8) * BODY + rest // 8


def edge_cell(n, rows):
    rest = n % 8
    row = jnp.zeros(n.shape, jnp.int32)
    for k, r in enumerate(rows):
        row = jnp.where(n // 8 == k, r, row)
    return row * LANES + jnp.where(rest < STEPS, rest, rest + LANES - 8)


def scatter(adjoint, code_row, cells):
    code = code_row.astype(jnp.int32)
    cell = jnp.where(code >= 0, code >> 2, -1)
    hot = jnp.concatenate(
        [
            jnp.where(cells == cell[:, t * LANES : (t + 1) * LANES], 1.0, 0.0).astype(jnp.bfloat16)
            for t in range(cell.shape[1] // LANES)
        ],
        1,
    )
    return halves(matmul(hot, jnp.concatenate(split(adjoint), 1)))


def payload_parts(ref):
    slots = ref.shape[0] * LANES // (LANES + 8)
    codes = [ref[slots + 8 * t : slots + 8 * t + 1, :] for t in range(slots // LANES)]
    return ref[0:slots, :], jnp.concatenate(codes, 1)


def state_kernel(own, a_in, b_in, cl, ct, cc, state, f, spare):
    even, pole = position()
    a_base, b_base, _, _ = halo_places(even, pole)
    sign = wind_sign(pole, (1, LANES))
    for q in range(BODY):
        at, to = (pl.ds(q, 8, stride=BODY), pl.ds(8 * q, 8))
        for k in range(STEPS):
            f[a_base + k, to, :] = a_in[k, at, :]
            f[b_base + k, to, :] = b_in[jnp.where(pole, STEPS - 1 - k, k), at, :] * sign
        for r in range(ROWS):
            f[STEPS + r, to, :] = own[r, at, :]

    def store(r, q, value):
        state[r, pl.ds(8 * q, 8), :] = value

    diffuse(f, spare, cl, ct, cc, store)


def observe_kernel(
    state_in, own, a_in, b_in, co, from_west, from_east, slots_in, operator,
    dep_out, pay_out, f_out, rl, rt, rc,
    rim, f, spare, co_rim, state,
):
    even, pole = position()
    a_base, b_base, _, _ = halo_places(even, pole)
    sign = wind_sign(pole, (1, LANES))
    co_rim[0:STEPS, :] = from_west[PLANES]
    co_rim[STEPS:SIDE, :] = co[0:8, :]
    co_rim[SIDE : 2 * SIDE - STEPS, :] = co[LANES - 8 : LANES, :]
    co_rim[2 * SIDE - STEPS : 2 * SIDE, :] = from_east[PLANES]
    expand(co_rim, rl, rt, rc, RIM)
    sides = ((slice(STEPS, SIDE), slice(0, 8)), (slice(SIDE, 2 * SIDE - STEPS), slice(LANES - 8, LANES)))
    for to, at in sides:
        for k in range(STEPS):
            rim[a_base + k, to, :] = a_in[k, at, :]
            rim[b_base + k, to, :] = b_in[jnp.where(pole, STEPS - 1 - k, k), at, :] * sign
        for r in range(ROWS):
            rim[STEPS + r, to, :] = own[r, at, :]
    diffuse_rim(rim, f, spare, rl, rt, rc, from_west, from_east)
    state[...] = state_in[...]
    for r in range(ROWS):
        state[r, pl.ds(0, STEPS, stride=8), :] = rim[STEPS + r, STEPS : 2 * STEPS, :]
        last = rim[STEPS + r, 2 * SIDE - 2 * STEPS : 2 * SIDE - STEPS, :]
        state[r, pl.ds(8 * (BODY - STEPS) + 7, STEPS, stride=8), :] = last

    owners, bucket = (slots_in.shape[0], (slots_in.shape[1] - 8) // 2)
    slots = owners * bucket
    lane = iota((1, LANES), 1)
    per_tile = LANES // bucket
    code_parts = []
    for t in range(slots // LANES):
        part = jnp.full((1, LANES), -1.0, F32)
        for n in range(per_tile):
            got = slots_in[t * per_tile + n, 2 * bucket : 2 * bucket + 1, :]
            part = jnp.where(lane // bucket == n, pltpu.roll(got, n * bucket, 1), part)
        code_parts.append(part)
        pay_out[slots + 8 * t : slots + 8 * t + 8, :] = jnp.broadcast_to(part, (8, LANES))
    code_row = jnp.concatenate(code_parts, 1)
    code = jnp.concatenate([jnp.broadcast_to(part, (LANES, LANES)).T for part in code_parts], 0)
    code = code.astype(jnp.int32)
    cell = jnp.where(code >= 0, code >> 2, -1)
    kind = jnp.where(code >= 0, code & 3, -1)

    depth = ROWS * LANES
    places = body_cell(iota((1, depth), 1), range(ROWS))
    hot = jnp.concatenate(
        [
            jnp.where(places[:, t : t + LANES] == cell, 1.0, 0.0).astype(jnp.bfloat16)
            for t in range(0, depth, LANES)
        ],
        1,
    )
    cells = jnp.concatenate(split(state[...].reshape(depth, LANES)), 1)
    column = halves(matmul(hot, cells))

    masks = [kind == n for n in range(3)]
    op_high, op_low = split(operator[...])
    zero = jnp.zeros((LANES, LANES), jnp.bfloat16)

    def by_kind(x):
        return jnp.concatenate([jnp.where(m, part, jnp.zeros_like(part)) for part in split(x) for m in masks], 1)

    forward = jnp.concatenate(
        [jnp.concatenate([op_high[n], op_low[n]], 1) for n in range(3)]
        + [jnp.concatenate([op_high[n], zero], 1) for n in range(3)],
        0,
    )
    model = halves(matmul(by_kind(column), forward))
    values = slots_in[:, 0:bucket, :].reshape(slots, LANES)
    weights = slots_in[:, bucket : 2 * bucket, :].reshape(slots, LANES)
    departures = jnp.where(code >= 0, values - model, 0.0)
    dep_out[...] = departures
    backward = jnp.concatenate(
        [
            jnp.concatenate([op_high[0], op_high[1], op_high[2]] * 2, 1),
            jnp.concatenate([op_low[0], op_low[1], op_low[2], zero, zero, zero], 1),
        ],
        0,
    )
    adjoint = halves(matmul(by_kind(weights * departures), backward, ((1,), (1,))))
    pay_out[0:slots, :] = adjoint
    f_out[...] = scatter(adjoint, code_row, body_cell(iota((depth, LANES), 0), range(ROWS))).reshape(f_out.shape)


def edge_forcing_kernel(f_in, a_in, b_in, w_out, e_out):
    even, pole = position()
    a_base, b_base, a_rows, b_rows = halo_places(even, pole)
    sign = wind_sign(pole, (1, LANES))
    for ref, rows, base, scale in ((a_in, a_rows, a_base, 1.0), (b_in, b_rows, b_base, sign)):
        got = scatter(*payload_parts(ref), edge_cell(iota((8 * STEPS, LANES), 0), rows)) * scale
        for k in range(STEPS):
            w_out[base + k] = got[8 * k : 8 * k + STEPS]
            e_out[base + k] = got[8 * k + STEPS : 8 * k + 8]
    for r in range(ROWS):
        w_out[STEPS + r] = f_in[r, pl.ds(0, STEPS, stride=8), :]
        e_out[STEPS + r] = f_in[r, pl.ds(8 * (BODY - STEPS) + 7, STEPS, stride=8), :]


def smooth_kernel(f_in, a_in, b_in, cl, ct, cc, smooth, rim, f, spare):
    even, pole = position()
    a_base, b_base, a_rows, b_rows = halo_places(even, pole)
    sign = wind_sign(pole, (1, LANES))
    for ref, rows, base, scale in ((a_in, a_rows, a_base, 1.0), (b_in, b_rows, b_base, sign)):
        got = scatter(*payload_parts(ref), body_cell(iota((STEPS * LANES, LANES), 0), rows)) * scale
        for k in range(STEPS):
            f[base + k] = got[k * LANES : (k + 1) * LANES]
    for r in range(ROWS):
        f[STEPS + r] = f_in[r]
    for p in range(PLANES):
        rim[p, 0:STEPS, :] = jnp.zeros((STEPS, LANES), F32)
        rim[p, STEPS:SIDE, :] = f[p, pl.ds(0, 8, stride=8), :]
        rim[p, SIDE : 2 * SIDE - STEPS, :] = f[p, pl.ds(8 * (BODY - 8) + 7, 8, stride=8), :]
        rim[p, 2 * SIDE - STEPS : 2 * SIDE, :] = jnp.zeros((STEPS, LANES), F32)

    def store(r, q, value):
        smooth[r, pl.ds(q, 8, stride=BODY), :] = value

    diffuse(f, spare, cl, ct, cc, store)


def last_kernel(inc, smooth, rim_in, from_west, from_east, rl, rt, rc, out, rim, f, spare, wide):
    rim[...] = rim_in[...]
    diffuse_rim(rim, f, spare, rl, rt, rc, from_west, from_east)
    for r in range(ROWS):
        wide[...] = smooth[r]
        wide[0:STEPS, :] = rim[STEPS + r, STEPS : 2 * STEPS, :]
        wide[LANES - STEPS : LANES, :] = rim[STEPS + r, 2 * SIDE - 2 * STEPS : 2 * SIDE - STEPS, :]
        at = pl.ds(r, LANES, stride=ROWS)
        out[at, :] = inc[at, :] - wide[...].T


def call(kernel, outs, args, scratch=(), spaces=None, flops=0, limit=20):
    spaces = spaces or {}
    specs = [pl.BlockSpec(memory_space=spaces.get(n, VMEM)) for n in range(len(args))]
    size = 4 * sum(x.size for x in list(args) + list(outs))
    args = [pltpu.with_memory_space_constraint(x, HBM) if spaces.get(n) is HBM else x for n, x in enumerate(args)]
    return pl.pallas_call(
        kernel,
        out_shape=outs,
        in_specs=specs,
        out_specs=[pl.BlockSpec(memory_space=VMEM) for _ in outs],
        scratch_shapes=list(scratch),
        compiler_params=pltpu.CompilerParams(vmem_limit_bytes=limit * MIB),
        cost_estimate=pl.CostEstimate(flops=flops, bytes_accessed=size, transcendentals=0),
    )(*args)


def routes():
    lons, lats = (lax.axis_size("lon"), lax.axis_size("lat"))
    at = lambda lon, lat: lon % lons * lats + lat
    cells = [(lon, lat) for lon in range(lons) for lat in range(lats)]
    inner = [(at(o, a), at(o, a ^ 1)) for o, a in cells]
    outer = []
    for o, a in cells:
        if a in (0, lats - 1):
            outer.append((at(o, a), at(o + lons // 2, a)))
        else:
            outer.append((at(o, a), at(o, a - 1 if a % 2 == 0 else a + 1)))
    east = [(at(o, a), at(o + 1, a)) for o, a in cells]
    west = [(at(o, a), at(o - 1, a)) for o, a in cells]
    return inner, outer, east, west


def local(
    increment, coef_lon, coef_lat, obs_values, obs_weight, obs_operator, obs_columns, obs_types, obs_counts
):
    shape = lambda *dims: jax.ShapeDtypeStruct(dims, F32)
    inner, outer, east, west = routes()
    send = lambda x, route: lax.ppermute(x, ("lon", "lat"), route)
    lats = lax.axis_size("lat")
    slots = obs_values.shape[0]
    bucket = slots // lats
    tiles = slots // LANES
    fields = increment.shape[0]
    inc = increment.reshape(-1, LANES)
    cl = coef_lon.reshape(fields * ROWS, LANES)
    ct = coef_lat.reshape(fields * ROWS, LANES)

    own, coef, b_send, a_send, rim_b, rim_a, w_own, e_own, slots_send = call(
        pack_kernel,
        [
            shape(ROWS, LANES, LANES),
            shape(LANES, LANES),
            shape(STEPS, LANES, LANES),
            shape(STEPS, LANES, LANES),
            shape(2 * STEPS + 1, 8, LANES),
            shape(2 * STEPS + 1, 8, LANES),
            shape(ROWS + 1, STEPS, LANES),
            shape(ROWS + 1, STEPS, LANES),
            shape(lats, 2 * bucket + 8, LANES),
        ],
        [
            inc,
            cl,
            ct,
            obs_values.reshape(lats, bucket, LANES),
            obs_weight.reshape(lats, bucket, LANES),
            obs_columns.reshape(1, slots),
            obs_types.reshape(1, slots),
            obs_counts,
        ],
        [
            VMEM(inc.shape, F32),
            VMEM(cl.shape, F32),
            VMEM(ct.shape, F32),
            VMEM((LANES, LANES), F32),
            VMEM((1, slots), jnp.int32),
            VMEM((1, slots), jnp.int32),
            pltpu.SMEM(obs_counts.shape, jnp.int32),
            pltpu.SemaphoreType.DMA((8,)),
        ],
        spaces={n: HBM for n in range(8)},
    )
    rim_a = send(rim_a, inner)
    a_in = send(a_send, inner)
    rim_b = send(rim_b, outer)
    b_in = send(b_send, outer)
    slots_send, _ = lax.optimization_barrier((slots_send, a_in))
    slots_in = lax.all_to_all(slots_send, "lat", split_axis=0, concat_axis=0, tiled=True)
    edge = shape(PLANES + 1, STEPS, LANES)
    block = shape(ROWS, LANES, LANES)
    planes = shape(PLANES, LANES, LANES)
    ends = shape(PLANES, 2 * SIDE, LANES)
    body_buffers = [VMEM(planes.shape, F32)] * 2
    rim_buffers = [VMEM(ends.shape, F32)] * 3
    w_send, e_send, co = call(
        edge_kernel,
        [edge, edge, shape(LANES, LANES)],
        [w_own, e_own, coef, rim_a, rim_b],
        [VMEM((LANES, LANES), F32)],
        flops=EDGE_COST,
    )
    from_west = send(e_send, east)
    from_east = send(w_send, west)
    wl, wt, wc = call(expand, [planes, planes, planes], [co], flops=EXPAND_COST)
    (state,) = call(state_kernel, [block], [own, a_in, b_in, wl, wt, wc], body_buffers, flops=STATE_COST)
    departures, payload, forcing, rl, rt, rc = call(
        observe_kernel,
        [shape(slots, LANES), shape(slots + 8 * tiles, LANES), block, ends, ends, ends],
        [state, own, a_in, b_in, co, from_west, from_east, slots_in, obs_operator],
        rim_buffers + [VMEM((2 * SIDE, LANES), F32), VMEM(block.shape, F32)],
        flops=10**8,
    )
    a_in = send(payload, inner)
    b_in = send(payload, outer)
    back = lax.all_to_all(
        departures.reshape(lats, bucket, LANES), "lat", split_axis=0, concat_axis=0, tiled=True
    )
    co, _ = lax.optimization_barrier((co, payload))
    wl, wt, wc = call(expand, [planes, planes, planes], [co], flops=EXPAND_COST)
    edge = shape(PLANES, STEPS, LANES)
    w_send, e_send = call(edge_forcing_kernel, [edge, edge], [forcing, a_in, b_in], flops=10**8)
    from_west = send(e_send, east)
    from_east = send(w_send, west)
    smooth, rim = call(
        smooth_kernel, [block, ends], [forcing, a_in, b_in, wl, wt, wc], body_buffers, flops=SMOOTH_COST
    )
    (gradient,) = call(
        last_kernel,
        [shape(*inc.shape)],
        [inc, smooth, rim, from_west, from_east, rl, rt, rc],
        rim_buffers + [VMEM((LANES, LANES), F32)],
        flops=10**8,
    )
    gradient, back = lax.optimization_barrier((gradient, back))
    return (gradient.reshape(increment.shape), back.reshape(slots, LANES))


def solution(mesh):
    return jax.shard_map(
        local,
        mesh=mesh,
        in_specs=(
            P(None, None, "lat", "lon"),
            P(None, "lat", "lon"),
            P(None, "lat", "lon"),
            P(("lon", "lat"), None),
            P(("lon", "lat"), None),
            P(),
            P(("lon", "lat")),
            P(("lon", "lat")),
            P(("lon", "lat")),
        ),
        out_specs=(P(None, None, "lat", "lon"), P(("lon", "lat"), None)),
        check_vma=False,
    )
```

```python
import functools

import jax
import jax.numpy as jnp
from jax import lax
from jax.experimental import pallas as pl
from jax.experimental.pallas import tpu as pltpu
from jax.sharding import PartitionSpec as P

STEPS = 4
ROWS = 8
LANES = 128
PLANES = ROWS + 2 * STEPS
BODY = LANES // 8
RIM = 3
SIDE = 4 * RIM
VMEM = pltpu.VMEM
HBM = pltpu.HBM
MIB = 1 << 20
RIM_UNROLL = True
BODY_UNROLL = 2
EDGE_COST = 10**10
EXPAND_COST = 10**8
STATE_COST = 10**9
SMOOTH_COST = 10**10
F32 = jnp.float32


def iota(shape, axis):
    return lax.broadcasted_iota(jnp.int32, shape, axis)


def position():
    lat, count = (lax.axis_index("lat"), lax.axis_size("lat"))
    return lat % 2 == 0, jnp.logical_or(lat == 0, lat == count - 1)


def halo_places(even, pole):
    a_base = jnp.where(even, PLANES - STEPS, 0)
    b_base = jnp.where(even, 0, PLANES - STEPS)
    a_rows = [jnp.where(even, k, STEPS + k) for k in range(STEPS)]
    b_rows = [
        jnp.where(
            pole,
            jnp.where(even, STEPS - 1 - k, ROWS - 1 - k),
            jnp.where(even, STEPS + k, k),
        )
        for k in range(STEPS)
    ]
    return a_base, b_base, a_rows, b_rows


def wind_sign(pole, shape):
    flipped = jnp.logical_and(iota(shape, len(shape) - 1) >= LANES // 2, pole)
    return jnp.where(flipped, -1.0, 1.0).astype(F32)


def split(x):
    high = x.astype(jnp.bfloat16)
    low = (x - high.astype(F32)).astype(jnp.bfloat16)
    return high, low


def matmul(a, b, dims=((1,), (0,))):
    return lax.dot_general(a, b, (dims, ((), ())), preferred_element_type=F32)


def halves(x):
    return x[:, :LANES] + x[:, LANES:]


def pack_kernel(
    inc_hbm, cl_hbm, ct_hbm, values, weights, columns_hbm, types_hbm, counts_hbm,
    own, coef, b_out, a_out, rim_b, rim_a, w_out, e_out, slots_out,
    inc, cl, ct, raw, columns, types, counts, staged, sems,
):
    owners, bucket = (slots_out.shape[0], values.shape[1])
    moves = (
        (columns_hbm, columns),
        (types_hbm, types),
        (counts_hbm, counts),
        (inc_hbm, inc),
        (cl_hbm, cl),
        (ct_hbm, ct),
        (values, staged.at[:, pl.ds(0, bucket), :]),
        (weights, staged.at[:, pl.ds(bucket, bucket), :]),
        (staged, slots_out),
    )
    copies = [pltpu.make_async_copy(src, dst, sems.at[n]) for n, (src, dst) in enumerate(moves)]
    for copy in copies[:8]:
        copy.start()
    for copy in copies[:3]:
        copy.wait()
    slots = columns.shape[1]
    lane = iota((1, slots), 1)
    limit = jnp.zeros((1, slots), jnp.int32)
    for d in range(owners):
        limit = jnp.where(lane // bucket == d, counts[d], limit)
    code = jnp.where(lane % bucket < limit, columns[...] * 4 + types[...], -1).astype(F32)
    for d in range(owners):
        at = d * bucket
        window = code[:, at // LANES * LANES : at // LANES * LANES + LANES]
        moved = pltpu.roll(window, (-at) % LANES, 1)
        staged[d, 2 * bucket : 2 * bucket + 8, :] = jnp.broadcast_to(moved, (8, LANES))
    for copy in copies[3:8]:
        copy.wait()
    copies[8].start()
    fields = cl.shape[0] // ROWS
    even, _ = position()
    raw[...] = jnp.zeros(raw.shape, F32)
    for r in range(ROWS):
        own[r] = inc[pl.ds(r, LANES, stride=ROWS), :].T
        at = 8 * (STEPS + r)
        raw[at : at + fields, :] = cl[pl.ds(r, fields, stride=ROWS), :]
        raw[at + fields : at + 2 * fields, :] = ct[pl.ds(r, fields, stride=ROWS), :]
        w_out[r] = own[r, 0:STEPS, :]
        e_out[r] = own[r, LANES - STEPS : LANES, :]
    coef[...] = raw[...].T
    w_out[ROWS] = coef[0:STEPS, :]
    e_out[ROWS] = coef[LANES - STEPS : LANES, :]
    a_row = jnp.where(even, STEPS, 0)
    b_row = STEPS - a_row
    for out, first in ((b_out, b_row), (a_out, a_row)):
        for k in range(STEPS):
            out[k] = own[first + k]
    for out, first in ((rim_b, b_row), (rim_a, a_row)):
        for k in range(STEPS):
            out[k, 0:STEPS, :] = own[first + k, 0:STEPS, :]
            out[k, STEPS : 2 * STEPS, :] = own[first + k, LANES - STEPS : LANES, :]
            out[STEPS + 1 + k] = raw[pl.ds(pl.multiple_of(8 * (STEPS + first + k), 8), 8), :]
        out[STEPS, 0:STEPS, :] = coef[0:STEPS, :]
        out[STEPS, STEPS : 2 * STEPS, :] = coef[LANES - STEPS : LANES, :]
    copies[8].wait()


def edge_kernel(w_own, e_own, coef, rim_a, rim_b, w_out, e_out, co, raw):
    even, pole = position()
    a_base, b_base, _, b_rows = halo_places(even, pole)
    sign = wind_sign(pole, (1, LANES))
    raw[...] = jnp.zeros(raw.shape, F32)
    for k in range(STEPS):
        kk = jnp.where(pole, STEPS - 1 - k, k)
        w_out[a_base + k] = rim_a[k, 0:STEPS, :]
        e_out[a_base + k] = rim_a[k, STEPS : 2 * STEPS, :]
        rim = rim_b[kk] * sign
        w_out[b_base + k] = rim[0:STEPS]
        e_out[b_base + k] = rim[STEPS : 2 * STEPS]
        raw[pl.ds(pl.multiple_of(8 * (a_base + k), 8), 8), :] = rim_a[STEPS + 1 + k]
        raw[pl.ds(pl.multiple_of(8 * (b_base + k), 8), 8), :] = rim_b[STEPS + 1 + kk]
    for r in range(ROWS):
        w_out[STEPS + r] = w_own[r]
        e_out[STEPS + r] = e_own[r]
    plane = iota((8, LANES), 1) // 8
    tile = jnp.concatenate([w_own[ROWS], e_own[ROWS]], 0)
    from_a = pltpu.roll(rim_a[STEPS], LANES // 2, 1)
    tile = jnp.where(plane // STEPS == a_base // STEPS, from_a, tile)
    for k in range(STEPS):
        shift = (8 * (b_base + k - STEPS - b_rows[k]) + 2 * LANES) % LANES
        tile = jnp.where(plane == b_base + k, pltpu.roll(rim_b[STEPS], shift, 1), tile)
    w_out[PLANES] = tile[0:STEPS]
    e_out[PLANES] = tile[STEPS : 2 * STEPS]
    co[...] = raw[...].T + coef[...]


def expand(co, cl, ct, cc, regs=BODY):
    high, low = split(jnp.concatenate([co[pl.ds(q, 8, stride=regs), :] for q in range(regs)], 0))
    tall = 2 * LANES - 16
    row, col = (iota((tall, 2 * LANES), 0), iota((tall, 2 * LANES), 1))
    wanted = LANES - 16 + col // LANES * 4 + col % LANES // (LANES // 4)
    picks = [jnp.where(row == wanted + 8 * odd, 1.0, 0.0).astype(jnp.bfloat16) for odd in range(2)]
    for p in range(PLANES):
        first = LANES - 16 - p // 2 * 16
        pick = picks[p % 2][first : first + LANES, :]
        both = matmul(high, pick) + matmul(low, pick)
        a, b = (both[:, :LANES], both[:, LANES:])
        cl[p] = a
        ct[p] = b
        cc[p] = 1.0 - 2.0 * (a * a + b * b)


def diffuse(f, spare, cl, ct, cc, store, unroll=1):
    regs = [pl.ds(8 * q, 8) for q in range(f.shape[1] // 8)]
    for step in range(STEPS):
        last = step == STEPS - 1

        def row(p, carry, f=f, spare=spare, last=last):
            here = [f[p, at, :] for at in regs]
            g = [cl[p, at, :] * x for at, x in zip(regs, here)]
            g = [pltpu.roll(g[-1], 1, 0)] + g + [pltpu.roll(g[0], 7, 0)]
            for q, at in enumerate(regs):
                sides = ct[p + 1, at, :] * f[p + 1, at, :] + ct[p - 1, at, :] * f[p - 1, at, :]
                new = cc[p, at, :] * here[q] + cl[p, at, :] * (g[q] + g[q + 2]) + ct[p, at, :] * sides
                if last:
                    store(p - STEPS, q, new)
                else:
                    spare[p, at, :] = new
            return carry

        lax.fori_loop(step + 1, PLANES - 1 - step, row, 0, unroll=unroll)
        f, spare = (spare, f)


def diffuse_rim(rim, f, spare, cl, ct, cc, west, east):
    for p in range(PLANES):
        rim[p, 0:STEPS, :] = west[p]
        rim[p, 2 * SIDE - STEPS : 2 * SIDE, :] = east[p]
        for q in range(RIM):
            f[p, 8 * q : 8 * q + 8, :] = rim[p, pl.ds(q, 8, stride=RIM), :]

    def store(r, q, value):
        rim[STEPS + r, pl.ds(q, 8, stride=RIM), :] = value

    diffuse(f, spare, cl, ct, cc, store, RIM_UNROLL)


def body_cell(n, rows):
    rest = n % LANES
    row = jnp.zeros(n.shape, jnp.int32)
    for k, r in enumerate(rows):
        row = jnp.where(n // LANES == k, r, row)
    return row * LANES + (rest % 8) * BODY + rest // 8


def edge_cell(n, rows):
    rest = n % 8
    row = jnp.zeros(n.shape, jnp.int32)
    for k, r in enumerate(rows):
        row = jnp.where(n // 8 == k, r, row)
    return row * LANES + jnp.where(rest < STEPS, rest, rest + LANES - 8)


def scatter(adjoint, code_row, cells):
    code = code_row.astype(jnp.int32)
    cell = jnp.where(code >= 0, code >> 2, -1)
    hot = jnp.concatenate(
        [
            jnp.where(cells == cell[:, t * LANES : (t + 1) * LANES], 1.0, 0.0).astype(jnp.bfloat16)
            for t in range(cell.shape[1] // LANES)
        ],
        1,
    )
    return halves(matmul(hot, jnp.concatenate(split(adjoint), 1)))


def payload_parts(ref):
    slots = ref.shape[0] * LANES // (LANES + 8)
    codes = [ref[slots + 8 * t : slots + 8 * t + 1, :] for t in range(slots // LANES)]
    return ref[0:slots, :], jnp.concatenate(codes, 1)


def state_kernel(own, a_in, b_in, cl, ct, cc, state, f, spare):
    even, pole = position()
    a_base, b_base, _, _ = halo_places(even, pole)
    sign = wind_sign(pole, (1, LANES))
    for q in range(BODY):
        at, to = (pl.ds(q, 8, stride=BODY), pl.ds(8 * q, 8))
        for k in range(STEPS):
            f[a_base + k, to, :] = a_in[k, at, :]
            f[b_base + k, to, :] = b_in[jnp.where(pole, STEPS - 1 - k, k), at, :] * sign
        for r in range(ROWS):
            f[STEPS + r, to, :] = own[r, at, :]

    def store(r, q, value):
        state[r, pl.ds(8 * q, 8), :] = value

    diffuse(f, spare, cl, ct, cc, store, BODY_UNROLL)


def observe_kernel(
    state_in, own, a_in, b_in, co, from_west, from_east, slots_in, operator,
    dep_out, pay_out, f_out, rl, rt, rc,
    rim, f, spare, co_rim, state,
):
    even, pole = position()
    a_base, b_base, _, _ = halo_places(even, pole)
    sign = wind_sign(pole, (1, LANES))
    co_rim[0:STEPS, :] = from_west[PLANES]
    co_rim[STEPS:SIDE, :] = co[0:8, :]
    co_rim[SIDE : 2 * SIDE - STEPS, :] = co[LANES - 8 : LANES, :]
    co_rim[2 * SIDE - STEPS : 2 * SIDE, :] = from_east[PLANES]
    expand(co_rim, rl, rt, rc, RIM)
    sides = ((slice(STEPS, SIDE), slice(0, 8)), (slice(SIDE, 2 * SIDE - STEPS), slice(LANES - 8, LANES)))
    for to, at in sides:
        for k in range(STEPS):
            rim[a_base + k, to, :] = a_in[k, at, :]
            rim[b_base + k, to, :] = b_in[jnp.where(pole, STEPS - 1 - k, k), at, :] * sign
        for r in range(ROWS):
            rim[STEPS + r, to, :] = own[r, at, :]
    diffuse_rim(rim, f, spare, rl, rt, rc, from_west, from_east)
    state[...] = state_in[...]
    for r in range(ROWS):
        state[r, pl.ds(0, STEPS, stride=8), :] = rim[STEPS + r, STEPS : 2 * STEPS, :]
        last = rim[STEPS + r, 2 * SIDE - 2 * STEPS : 2 * SIDE - STEPS, :]
        state[r, pl.ds(8 * (BODY - STEPS) + 7, STEPS, stride=8), :] = last

    owners, bucket = (slots_in.shape[0], (slots_in.shape[1] - 8) // 2)
    slots = owners * bucket
    lane = iota((1, LANES), 1)
    per_tile = LANES // bucket
    code_parts = []
    for t in range(slots // LANES):
        part = jnp.full((1, LANES), -1.0, F32)
        for n in range(per_tile):
            got = slots_in[t * per_tile + n, 2 * bucket : 2 * bucket + 1, :]
            part = jnp.where(lane // bucket == n, pltpu.roll(got, n * bucket, 1), part)
        code_parts.append(part)
        pay_out[slots + 8 * t : slots + 8 * t + 8, :] = jnp.broadcast_to(part, (8, LANES))
    code_row = jnp.concatenate(code_parts, 1)
    code = jnp.concatenate([jnp.broadcast_to(part, (LANES, LANES)).T for part in code_parts], 0)
    code = code.astype(jnp.int32)
    cell = jnp.where(code >= 0, code >> 2, -1)
    kind = jnp.where(code >= 0, code & 3, -1)

    depth = ROWS * LANES
    places = body_cell(iota((1, depth), 1), range(ROWS))
    hot = jnp.concatenate(
        [
            jnp.where(places[:, t : t + LANES] == cell, 1.0, 0.0).astype(jnp.bfloat16)
            for t in range(0, depth, LANES)
        ],
        1,
    )
    cells = jnp.concatenate(split(state[...].reshape(depth, LANES)), 1)
    column = halves(matmul(hot, cells))

    masks = [kind == n for n in range(3)]
    op_high, op_low = split(operator[...])
    zero = jnp.zeros((LANES, LANES), jnp.bfloat16)

    def by_kind(x):
        return jnp.concatenate([jnp.where(m, part, jnp.zeros_like(part)) for part in split(x) for m in masks], 1)

    forward = jnp.concatenate(
        [jnp.concatenate([op_high[n], op_low[n]], 1) for n in range(3)]
        + [jnp.concatenate([op_high[n], zero], 1) for n in range(3)],
        0,
    )
    model = halves(matmul(by_kind(column), forward))
    values = slots_in[:, 0:bucket, :].reshape(slots, LANES)
    weights = slots_in[:, bucket : 2 * bucket, :].reshape(slots, LANES)
    departures = jnp.where(code >= 0, values - model, 0.0)
    dep_out[...] = departures
    backward = jnp.concatenate(
        [
            jnp.concatenate([op_high[0], op_high[1], op_high[2]] * 2, 1),
            jnp.concatenate([op_low[0], op_low[1], op_low[2], zero, zero, zero], 1),
        ],
        0,
    )
    adjoint = halves(matmul(by_kind(weights * departures), backward, ((1,), (1,))))
    pay_out[0:slots, :] = adjoint
    f_out[...] = scatter(adjoint, code_row, body_cell(iota((depth, LANES), 0), range(ROWS))).reshape(f_out.shape)


def edge_forcing_kernel(f_in, a_in, b_in, w_out, e_out):
    even, pole = position()
    a_base, b_base, a_rows, b_rows = halo_places(even, pole)
    sign = wind_sign(pole, (1, LANES))
    for ref, rows, base, scale in ((a_in, a_rows, a_base, 1.0), (b_in, b_rows, b_base, sign)):
        got = scatter(*payload_parts(ref), edge_cell(iota((8 * STEPS, LANES), 0), rows)) * scale
        for k in range(STEPS):
            w_out[base + k] = got[8 * k : 8 * k + STEPS]
            e_out[base + k] = got[8 * k + STEPS : 8 * k + 8]
    for r in range(ROWS):
        w_out[STEPS + r] = f_in[r, pl.ds(0, STEPS, stride=8), :]
        e_out[STEPS + r] = f_in[r, pl.ds(8 * (BODY - STEPS) + 7, STEPS, stride=8), :]


def smooth_kernel(f_in, a_in, b_in, cl, ct, cc, smooth, rim, f, spare):
    even, pole = position()
    a_base, b_base, a_rows, b_rows = halo_places(even, pole)
    sign = wind_sign(pole, (1, LANES))
    for ref, rows, base, scale in ((a_in, a_rows, a_base, 1.0), (b_in, b_rows, b_base, sign)):
        got = scatter(*payload_parts(ref), body_cell(iota((STEPS * LANES, LANES), 0), rows)) * scale
        for k in range(STEPS):
            f[base + k] = got[k * LANES : (k + 1) * LANES]
    for r in range(ROWS):
        f[STEPS + r] = f_in[r]
    for p in range(PLANES):
        rim[p, 0:STEPS, :] = jnp.zeros((STEPS, LANES), F32)
        rim[p, STEPS:SIDE, :] = f[p, pl.ds(0, 8, stride=8), :]
        rim[p, SIDE : 2 * SIDE - STEPS, :] = f[p, pl.ds(8 * (BODY - 8) + 7, 8, stride=8), :]
        rim[p, 2 * SIDE - STEPS : 2 * SIDE, :] = jnp.zeros((STEPS, LANES), F32)

    def store(r, q, value):
        smooth[r, pl.ds(q, 8, stride=BODY), :] = value

    diffuse(f, spare, cl, ct, cc, store, BODY_UNROLL)


def last_kernel(inc, smooth, rim_in, from_west, from_east, rl, rt, rc, back, out, dep_out, rim, f, spare, wide):
    dep_out[...] = back[...]
    rim[...] = rim_in[...]
    diffuse_rim(rim, f, spare, rl, rt, rc, from_west, from_east)
    for r in range(ROWS):
        wide[...] = smooth[r]
        wide[0:STEPS, :] = rim[STEPS + r, STEPS : 2 * STEPS, :]
        wide[LANES - STEPS : LANES, :] = rim[STEPS + r, 2 * SIDE - 2 * STEPS : 2 * SIDE - STEPS, :]
        at = pl.ds(r, LANES, stride=ROWS)
        out[at, :] = inc[at, :] - wide[...].T


def call(kernel, outs, args, scratch=(), spaces=None, out_spaces=None, flops=0, limit=20):
    spaces = spaces or {}
    specs = [pl.BlockSpec(memory_space=spaces.get(n, VMEM)) for n in range(len(args))]
    size = 4 * sum(x.size for x in list(args) + list(outs))
    args = [pltpu.with_memory_space_constraint(x, HBM) if spaces.get(n) is HBM else x for n, x in enumerate(args)]
    return pl.pallas_call(
        kernel,
        out_shape=outs,
        in_specs=specs,
        out_specs=[pl.BlockSpec(memory_space=(out_spaces or {}).get(n, VMEM)) for n in range(len(outs))],
        scratch_shapes=list(scratch),
        compiler_params=pltpu.CompilerParams(vmem_limit_bytes=limit * MIB),
        cost_estimate=pl.CostEstimate(flops=flops, bytes_accessed=size, transcendentals=0),
    )(*args)


def routes():
    lons, lats = (lax.axis_size("lon"), lax.axis_size("lat"))
    at = lambda lon, lat: lon % lons * lats + lat
    cells = [(lon, lat) for lon in range(lons) for lat in range(lats)]
    inner = [(at(o, a), at(o, a ^ 1)) for o, a in cells]
    outer = []
    for o, a in cells:
        if a in (0, lats - 1):
            outer.append((at(o, a), at(o + lons // 2, a)))
        else:
            outer.append((at(o, a), at(o, a - 1 if a % 2 == 0 else a + 1)))
    east = [(at(o, a), at(o + 1, a)) for o, a in cells]
    west = [(at(o, a), at(o - 1, a)) for o, a in cells]
    return inner, outer, east, west


def local(
    increment, coef_lon, coef_lat, obs_values, obs_weight, obs_operator, obs_columns, obs_types, obs_counts
):
    shape = lambda *dims: jax.ShapeDtypeStruct(dims, F32)
    inner, outer, east, west = routes()
    send = lambda x, route: lax.ppermute(x, ("lon", "lat"), route)
    lats = lax.axis_size("lat")
    slots = obs_values.shape[0]
    bucket = slots // lats
    tiles = slots // LANES
    fields = increment.shape[0]
    inc = increment.reshape(-1, LANES)
    cl = coef_lon.reshape(fields * ROWS, LANES)
    ct = coef_lat.reshape(fields * ROWS, LANES)

    own, coef, b_send, a_send, rim_b, rim_a, w_own, e_own, slots_send = call(
        pack_kernel,
        [
            shape(ROWS, LANES, LANES),
            shape(LANES, LANES),
            shape(STEPS, LANES, LANES),
            shape(STEPS, LANES, LANES),
            shape(2 * STEPS + 1, 8, LANES),
            shape(2 * STEPS + 1, 8, LANES),
            shape(ROWS + 1, STEPS, LANES),
            shape(ROWS + 1, STEPS, LANES),
            shape(lats, 2 * bucket + 8, LANES),
        ],
        [
            inc,
            cl,
            ct,
            obs_values.reshape(lats, bucket, LANES),
            obs_weight.reshape(lats, bucket, LANES),
            obs_columns.reshape(1, slots),
            obs_types.reshape(1, slots),
            obs_counts,
        ],
        [
            VMEM(inc.shape, F32),
            VMEM(cl.shape, F32),
            VMEM(ct.shape, F32),
            VMEM((LANES, LANES), F32),
            VMEM((1, slots), jnp.int32),
            VMEM((1, slots), jnp.int32),
            pltpu.SMEM(obs_counts.shape, jnp.int32),
            VMEM((lats, 2 * bucket + 8, LANES), F32),
            pltpu.SemaphoreType.DMA((9,)),
        ],
        spaces={n: HBM for n in range(8)},
        out_spaces={8: pl.ANY},
    )
    rim_a = send(rim_a, inner)
    a_in = send(a_send, inner)
    rim_b = send(rim_b, outer)
    b_in = send(b_send, outer)
    slots_send, _ = lax.optimization_barrier((slots_send, a_in))
    slots_in = lax.all_to_all(slots_send, "lat", split_axis=0, concat_axis=0, tiled=True)
    edge = shape(PLANES + 1, STEPS, LANES)
    block = shape(ROWS, LANES, LANES)
    planes = shape(PLANES, LANES, LANES)
    ends = shape(PLANES, 2 * SIDE, LANES)
    body_buffers = [VMEM(planes.shape, F32)] * 2
    rim_buffers = [VMEM(ends.shape, F32)] * 3
    w_send, e_send, co = call(
        edge_kernel,
        [edge, edge, shape(LANES, LANES)],
        [w_own, e_own, coef, rim_a, rim_b],
        [VMEM((LANES, LANES), F32)],
        flops=EDGE_COST,
    )
    from_west = send(e_send, east)
    from_east = send(w_send, west)
    wl, wt, wc = call(expand, [planes, planes, planes], [co], flops=EXPAND_COST)
    (state,) = call(state_kernel, [block], [own, a_in, b_in, wl, wt, wc], body_buffers, flops=STATE_COST)
    departures, payload, forcing, rl, rt, rc = call(
        observe_kernel,
        [shape(slots, LANES), shape(slots + 8 * tiles, LANES), block, ends, ends, ends],
        [state, own, a_in, b_in, co, from_west, from_east, slots_in, obs_operator],
        rim_buffers + [VMEM((2 * SIDE, LANES), F32), VMEM(block.shape, F32)],
        flops=10**8,
    )
    a_in = send(payload, inner)
    b_in = send(payload, outer)
    back = lax.all_to_all(
        departures.reshape(lats, bucket, LANES), "lat", split_axis=0, concat_axis=0, tiled=True
    )
    co, _ = lax.optimization_barrier((co, payload))
    wl, wt, wc = call(expand, [planes, planes, planes], [co], flops=EXPAND_COST)
    edge = shape(PLANES, STEPS, LANES)
    w_send, e_send = call(edge_forcing_kernel, [edge, edge], [forcing, a_in, b_in], flops=10**8)
    from_west = send(e_send, east)
    from_east = send(w_send, west)
    smooth, rim = call(
        smooth_kernel, [block, ends], [forcing, a_in, b_in, wl, wt, wc], body_buffers, flops=SMOOTH_COST
    )
    gradient, departures = call(
        last_kernel,
        [shape(*inc.shape), shape(slots, LANES)],
        [inc, smooth, rim, from_west, from_east, rl, rt, rc, back.reshape(slots, LANES)],
        rim_buffers + [VMEM((LANES, LANES), F32)],
        flops=10**8,
    )
    return (gradient.reshape(increment.shape), departures)


def solution(mesh):
    return jax.shard_map(
        local,
        mesh=mesh,
        in_specs=(
            P(None, None, "lat", "lon"),
            P(None, "lat", "lon"),
            P(None, "lat", "lon"),
            P(("lon", "lat"), None),
            P(("lon", "lat"), None),
            P(),
            P(("lon", "lat")),
            P(("lon", "lat")),
            P(("lon", "lat")),
        ),
        out_specs=(P(None, None, "lat", "lon"), P(("lon", "lat"), None)),
        check_vma=False,
    )
```

```python
import functools

import jax
import jax.numpy as jnp
from jax import lax
from jax.experimental import pallas as pl
from jax.experimental.pallas import tpu as pltpu
from jax.sharding import PartitionSpec as P

STEPS = 4
ROWS = 8
LANES = 128
PLANES = ROWS + 2 * STEPS
BODY = LANES // 8
RIM = 3
SIDE = 4 * RIM
VMEM = pltpu.VMEM
HBM = pltpu.HBM
MIB = 1 << 20
RIM_UNROLL = True
BODY_UNROLL = 2
EDGE_COST = 10**10
EXPAND_COST = 10**8
STATE_COST = 10**9
SMOOTH_COST = 10**10
F32 = jnp.float32


def iota(shape, axis):
    return lax.broadcasted_iota(jnp.int32, shape, axis)


def position():
    lat, count = (lax.axis_index("lat"), lax.axis_size("lat"))
    return lat % 2 == 0, jnp.logical_or(lat == 0, lat == count - 1)


def halo_places(even, pole):
    a_base = jnp.where(even, PLANES - STEPS, 0)
    b_base = jnp.where(even, 0, PLANES - STEPS)
    a_rows = [jnp.where(even, k, STEPS + k) for k in range(STEPS)]
    b_rows = [
        jnp.where(
            pole,
            jnp.where(even, STEPS - 1 - k, ROWS - 1 - k),
            jnp.where(even, STEPS + k, k),
        )
        for k in range(STEPS)
    ]
    return a_base, b_base, a_rows, b_rows


def wind_sign(pole, shape):
    flipped = jnp.logical_and(iota(shape, len(shape) - 1) >= LANES // 2, pole)
    return jnp.where(flipped, -1.0, 1.0).astype(F32)


def split(x):
    high = x.astype(jnp.bfloat16)
    low = (x - high.astype(F32)).astype(jnp.bfloat16)
    return high, low


def matmul(a, b, dims=((1,), (0,))):
    return lax.dot_general(a, b, (dims, ((), ())), preferred_element_type=F32)


def halves(x):
    return x[:, :LANES] + x[:, LANES:]


def pack_kernel(
    inc_hbm, cl_hbm, ct_hbm, values, weights, columns_hbm, types_hbm, counts_hbm,
    own, coef, b_out, a_out, rim_b, rim_a, w_out, e_out, slots_out,
    inc, cl, ct, raw, columns, types, counts, staged, sems,
):
    owners, bucket = (slots_out.shape[0], values.shape[1])
    moves = (
        (columns_hbm, columns),
        (types_hbm, types),
        (counts_hbm, counts),
        (inc_hbm, inc),
        (cl_hbm, cl),
        (ct_hbm, ct),
        (values, staged.at[:, pl.ds(0, bucket), :]),
        (weights, staged.at[:, pl.ds(bucket, bucket), :]),
        (staged, slots_out),
    )
    copies = [pltpu.make_async_copy(src, dst, sems.at[n]) for n, (src, dst) in enumerate(moves)]
    for copy in copies[:8]:
        copy.start()
    for copy in copies[:3]:
        copy.wait()
    slots = columns.shape[1]
    lane = iota((1, slots), 1)
    limit = jnp.zeros((1, slots), jnp.int32)
    for d in range(owners):
        limit = jnp.where(lane // bucket == d, counts[d], limit)
    code = jnp.where(lane % bucket < limit, columns[...] * 4 + types[...], -1).astype(F32)
    for d in range(owners):
        at = d * bucket
        window = code[:, at // LANES * LANES : at // LANES * LANES + LANES]
        moved = pltpu.roll(window, (-at) % LANES, 1)
        staged[d, 2 * bucket : 2 * bucket + 8, :] = jnp.broadcast_to(moved, (8, LANES))
    for copy in copies[3:8]:
        copy.wait()
    copies[8].start()
    fields = cl.shape[0] // ROWS
    even, _ = position()
    raw[...] = jnp.zeros(raw.shape, F32)
    for r in range(ROWS):
        own[r] = inc[pl.ds(r, LANES, stride=ROWS), :].T
        at = 8 * (STEPS + r)
        raw[at : at + fields, :] = cl[pl.ds(r, fields, stride=ROWS), :]
        raw[at + fields : at + 2 * fields, :] = ct[pl.ds(r, fields, stride=ROWS), :]
        w_out[r] = own[r, 0:STEPS, :]
        e_out[r] = own[r, LANES - STEPS : LANES, :]
    coef[...] = raw[...].T
    w_out[ROWS] = coef[0:STEPS, :]
    e_out[ROWS] = coef[LANES - STEPS : LANES, :]
    a_row = jnp.where(even, STEPS, 0)
    b_row = STEPS - a_row
    for out, first in ((b_out, b_row), (a_out, a_row)):
        for k in range(STEPS):
            out[k] = own[first + k]
    for out, first in ((rim_b, b_row), (rim_a, a_row)):
        for k in range(STEPS):
            out[k, 0:STEPS, :] = own[first + k, 0:STEPS, :]
            out[k, STEPS : 2 * STEPS, :] = own[first + k, LANES - STEPS : LANES, :]
            out[STEPS + 1 + k] = raw[pl.ds(pl.multiple_of(8 * (STEPS + first + k), 8), 8), :]
        out[STEPS, 0:STEPS, :] = coef[0:STEPS, :]
        out[STEPS, STEPS : 2 * STEPS, :] = coef[LANES - STEPS : LANES, :]
    copies[8].wait()


def edge_kernel(w_own, e_own, coef, rim_a, rim_b, w_out, e_out, co, raw):
    even, pole = position()
    a_base, b_base, _, b_rows = halo_places(even, pole)
    sign = wind_sign(pole, (1, LANES))
    raw[...] = jnp.zeros(raw.shape, F32)
    for k in range(STEPS):
        kk = jnp.where(pole, STEPS - 1 - k, k)
        w_out[a_base + k] = rim_a[k, 0:STEPS, :]
        e_out[a_base + k] = rim_a[k, STEPS : 2 * STEPS, :]
        rim = rim_b[kk] * sign
        w_out[b_base + k] = rim[0:STEPS]
        e_out[b_base + k] = rim[STEPS : 2 * STEPS]
        raw[pl.ds(pl.multiple_of(8 * (a_base + k), 8), 8), :] = rim_a[STEPS + 1 + k]
        raw[pl.ds(pl.multiple_of(8 * (b_base + k), 8), 8), :] = rim_b[STEPS + 1 + kk]
    for r in range(ROWS):
        w_out[STEPS + r] = w_own[r]
        e_out[STEPS + r] = e_own[r]
    plane = iota((8, LANES), 1) // 8
    tile = jnp.concatenate([w_own[ROWS], e_own[ROWS]], 0)
    from_a = pltpu.roll(rim_a[STEPS], LANES // 2, 1)
    tile = jnp.where(plane // STEPS == a_base // STEPS, from_a, tile)
    for k in range(STEPS):
        shift = (8 * (b_base + k - STEPS - b_rows[k]) + 2 * LANES) % LANES
        tile = jnp.where(plane == b_base + k, pltpu.roll(rim_b[STEPS], shift, 1), tile)
    w_out[PLANES] = tile[0:STEPS]
    e_out[PLANES] = tile[STEPS : 2 * STEPS]
    co[...] = raw[...].T + coef[...]


def expand(co, cl, ct, cc):
    parts = split(jnp.concatenate([co[pl.ds(q, 8, stride=BODY), :] for q in range(BODY)], 0))
    both_parts = jnp.concatenate(parts, 1)
    tall = 2 * LANES - 16
    row, col = (iota((tall, 2 * LANES), 0), iota((tall, 2 * LANES), 1))
    wanted = LANES - 16 + col // LANES * 4 + col % LANES // (LANES // 4)
    picks = [jnp.where(row == wanted + 8 * odd, 1.0, 0.0).astype(jnp.bfloat16) for odd in range(2)]
    for p in range(PLANES):
        first = LANES - 16 - p // 2 * 16
        pick = picks[p % 2][first : first + LANES, :]
        both = matmul(both_parts, jnp.concatenate([pick, pick], 0))
        a, b = (both[:, :LANES], both[:, LANES:])
        cl[p] = a
        ct[p] = b
        cc[p] = 1.0 - 2.0 * (a * a + b * b)


def expand_rim(co, cl, ct, cc):
    wide = jnp.concatenate([co[pl.ds(q, 8, stride=RIM), :] for q in range(RIM)], 0)
    tall = jnp.concatenate([pltpu.roll(wide, (-8 * p) % LANES, 1) for p in range(PLANES)], 0)
    row, col = (iota((LANES, 2 * LANES), 0), iota((LANES, 2 * LANES), 1))
    pick = jnp.where(row == col // LANES * 4 + col % LANES // (LANES // 4), 1.0, 0.0).astype(jnp.bfloat16)
    both = matmul(jnp.concatenate(split(tall), 1), jnp.concatenate([pick, pick], 0))
    for p in range(PLANES):
        a = both[2 * SIDE * p : 2 * SIDE * (p + 1), :LANES]
        b = both[2 * SIDE * p : 2 * SIDE * (p + 1), LANES:]
        cl[p] = a
        ct[p] = b
        cc[p] = 1.0 - 2.0 * (a * a + b * b)


def relax(p, f, cl, ct, cc, emit):
    regs = [pl.ds(8 * q, 8) for q in range(f.shape[1] // 8)]
    here = [f[p, at, :] for at in regs]
    g = [cl[p, at, :] * x for at, x in zip(regs, here)]
    g = [pltpu.roll(g[-1], 1, 0)] + g + [pltpu.roll(g[0], 7, 0)]
    for q, at in enumerate(regs):
        sides = ct[p + 1, at, :] * f[p + 1, at, :] + ct[p - 1, at, :] * f[p - 1, at, :]
        emit(q, at, cc[p, at, :] * here[q] + cl[p, at, :] * (g[q] + g[q + 2]) + ct[p, at, :] * sides)


def diffuse(f, spare, cl, ct, cc, store, unroll=1):
    for step in range(STEPS):

        def row(p, carry, f=f, spare=spare, last=step == STEPS - 1):
            def emit(q, at, new):
                if last:
                    store(p - STEPS, q, new)
                else:
                    spare[p, at, :] = new

            relax(p, f, cl, ct, cc, emit)
            return carry

        lax.fori_loop(step + 1, PLANES - 1 - step, row, 0, unroll=unroll)
        f, spare = (spare, f)


def diffuse_rim(rim, f, spare, cl, ct, cc, west, east):
    for p in range(PLANES):
        rim[p, 0:STEPS, :] = west[p]
        rim[p, 2 * SIDE - STEPS : 2 * SIDE, :] = east[p]
        for q in range(RIM):
            f[p, 8 * q : 8 * q + 8, :] = rim[p, pl.ds(q, 8, stride=RIM), :]

    def store(r, q, value):
        rim[STEPS + r, pl.ds(q, 8, stride=RIM), :] = value

    diffuse(f, spare, cl, ct, cc, store, RIM_UNROLL)


def body_cell(n, rows):
    rest = n % LANES
    row = jnp.zeros(n.shape, jnp.int32)
    for k, r in enumerate(rows):
        row = jnp.where(n // LANES == k, r, row)
    return row * LANES + (rest % 8) * BODY + rest // 8


def edge_cell(n, rows):
    rest = n % 8
    row = jnp.zeros(n.shape, jnp.int32)
    for k, r in enumerate(rows):
        row = jnp.where(n // 8 == k, r, row)
    return row * LANES + jnp.where(rest < STEPS, rest, rest + LANES - 8)


def scatter(adjoint, code_row, cells):
    code = code_row.astype(jnp.int32)
    cell = jnp.where(code >= 0, code >> 2, -1)
    hot = jnp.concatenate(
        [
            jnp.where(cells == cell[:, t * LANES : (t + 1) * LANES], 1.0, 0.0).astype(jnp.bfloat16)
            for t in range(cell.shape[1] // LANES)
        ],
        1,
    )
    return halves(matmul(hot, jnp.concatenate(split(adjoint), 1)))


def payload_parts(ref):
    slots = ref.shape[0] * LANES // (LANES + 8)
    codes = [ref[slots + 8 * t : slots + 8 * t + 1, :] for t in range(slots // LANES)]
    return ref[0:slots, :], jnp.concatenate(codes, 1)


def near_half_kernel(own, a_in, cl, ct, cc, part, strips, f, spare):
    even, pole = position()
    a_base, _, _, _ = halo_places(even, pole)
    for q in range(BODY):
        at, to = (pl.ds(q, 8, stride=BODY), pl.ds(8 * q, 8))
        for k in range(STEPS):
            f[a_base + k, to, :] = a_in[k, at, :]
        for r in range(ROWS):
            f[STEPS + r, to, :] = own[r, at, :]
    for step in range(STEPS):
        low = jnp.where(even, STEPS + 1 + step, 1 + step)

        def row(i, carry, f=f, spare=spare, low=low, last=step == STEPS - 1):
            def emit(q, at, new):
                if last:
                    part[i, at, :] = new
                else:
                    spare[low + i, at, :] = new

            relax(low + i, f, cl, ct, cc, emit)
            return carry

        lax.fori_loop(0, ROWS + 2 - 2 * step, row, 0, unroll=BODY_UNROLL)
        if step < STEPS - 1:
            first = jnp.where(even, STEPS + 1 + step, ROWS + 1 - step)
            strips[step, 0] = spare[first]
            strips[step, 1] = spare[first + 1]
        f, spare = (spare, f)


def far_half_kernel(own, b_in, strips, cl, ct, cc, part, f, spare):
    even, pole = position()
    _, b_base, _, _ = halo_places(even, pole)
    sign = wind_sign(pole, (1, LANES))
    first = jnp.where(even, 0, ROWS - 2)
    for q in range(BODY):
        at, to = (pl.ds(q, 8, stride=BODY), pl.ds(8 * q, 8))
        for k in range(STEPS):
            f[b_base + k, to, :] = b_in[jnp.where(pole, STEPS - 1 - k, k), at, :] * sign
        for i in range(2):
            f[STEPS + first + i, to, :] = own[first + i, at, :]
    for step in range(STEPS):
        low = jnp.where(even, 1 + step, PLANES - 1 - STEPS - step)

        def row(i, carry, f=f, spare=spare, low=low, last=step == STEPS - 1):
            def emit(q, at, new):
                if last:
                    part[i, at, :] = new
                else:
                    spare[low + i, at, :] = new

            relax(low + i, f, cl, ct, cc, emit)
            return carry

        lax.fori_loop(0, STEPS, row, 0, unroll=BODY_UNROLL)
        if step < STEPS - 1:
            first = jnp.where(even, STEPS + 1 + step, ROWS + 1 - step)
            spare[first] = strips[step, 0]
            spare[first + 1] = strips[step, 1]
        f, spare = (spare, f)


def gather_kernel(near_half, far_half, slots_in, operator, column, code_out, row_out, forward, backward):
    owners, bucket = (slots_in.shape[0], (slots_in.shape[1] - 8) // 2)
    slots = owners * bucket
    even, _ = position()
    lane = iota((1, LANES), 1)
    per_tile = LANES // bucket
    code_parts = []
    for t in range(slots // LANES):
        part = jnp.full((1, LANES), -1.0, F32)
        for n in range(per_tile):
            got = slots_in[t * per_tile + n, 2 * bucket : 2 * bucket + 1, :]
            part = jnp.where(lane // bucket == n, pltpu.roll(got, n * bucket, 1), part)
        code_parts.append(part)
        row_out[8 * t : 8 * t + 8, :] = jnp.broadcast_to(part, (8, LANES))
    code = jnp.concatenate([jnp.broadcast_to(part, (LANES, LANES)).T for part in code_parts], 0)
    code = code.astype(jnp.int32)
    code_out[...] = code
    cell = jnp.where(code >= 0, code >> 2, -1)
    half = STEPS * LANES
    near_row = jnp.where(even, ROWS - STEPS, 0)
    places = iota((1, half), 1)
    ends = (places % 8 == 0) & (places % LANES < 8 * STEPS) | (places % 8 == 7) & (places % LANES >= LANES - 8 * STEPS)
    total = None
    for ref, first in ((near_half, near_row), (far_half, ROWS - STEPS - near_row)):
        cells = jnp.where(ends, -2, body_cell(places, [first + k for k in range(STEPS)]))
        hot = jnp.concatenate(
            [
                jnp.where(cells[:, t : t + LANES] == cell, 1.0, 0.0).astype(jnp.bfloat16)
                for t in range(0, half, LANES)
            ],
            1,
        )
        got = matmul(hot, jnp.concatenate(split(ref[...].reshape(half, LANES)), 1))
        total = got if total is None else total + got
    column[...] = halves(total)
    op_high, op_low = split(operator[...])
    zero = jnp.zeros((LANES, LANES), jnp.bfloat16)
    forward[...] = jnp.concatenate(
        [jnp.concatenate([op_high[n], op_low[n]], 1) for n in range(3)]
        + [jnp.concatenate([op_high[n], zero], 1) for n in range(3)],
        0,
    )
    backward[...] = jnp.concatenate(
        [
            jnp.concatenate([op_high[0], op_high[1], op_high[2]] * 2, 1),
            jnp.concatenate([op_low[0], op_low[1], op_low[2], zero, zero, zero], 1),
        ],
        0,
    )


def observe_kernel(
    column_in, code_in, row_in, forward, backward, own, a_in, b_in, co, from_west, from_east, slots_in,
    dep_out, pay_out, f_out, rl, rt, rc,
    rim, f, spare, co_rim, ends,
):
    even, pole = position()
    a_base, b_base, _, _ = halo_places(even, pole)
    sign = wind_sign(pole, (1, LANES))
    co_rim[0:STEPS, :] = from_west[PLANES]
    co_rim[STEPS:SIDE, :] = co[0:8, :]
    co_rim[SIDE : 2 * SIDE - STEPS, :] = co[LANES - 8 : LANES, :]
    co_rim[2 * SIDE - STEPS : 2 * SIDE, :] = from_east[PLANES]
    expand_rim(co_rim, rl, rt, rc)
    sides = ((slice(STEPS, SIDE), slice(0, 8)), (slice(SIDE, 2 * SIDE - STEPS), slice(LANES - 8, LANES)))
    for to, at in sides:
        for k in range(STEPS):
            rim[a_base + k, to, :] = a_in[k, at, :]
            rim[b_base + k, to, :] = b_in[jnp.where(pole, STEPS - 1 - k, k), at, :] * sign
        for r in range(ROWS):
            rim[STEPS + r, to, :] = own[r, at, :]
    diffuse_rim(rim, f, spare, rl, rt, rc, from_west, from_east)
    slots = column_in.shape[0]
    bucket = (slots_in.shape[1] - 8) // 2
    code = code_in[...]
    cell = jnp.where(code >= 0, code >> 2, -1)
    kind = jnp.where(code >= 0, code & 3, -1)
    for r in range(ROWS):
        ends[8 * r : 8 * r + STEPS, :] = rim[STEPS + r, STEPS : 2 * STEPS, :]
        ends[8 * r + STEPS : 8 * r + 8, :] = rim[STEPS + r, 2 * SIDE - 2 * STEPS : 2 * SIDE - STEPS, :]
    ends[8 * ROWS : LANES, :] = jnp.zeros((LANES - 8 * ROWS, LANES), F32)
    hot = jnp.where(edge_cell(iota((1, LANES), 1), range(ROWS)) == cell, 1.0, 0.0).astype(jnp.bfloat16)
    column = column_in[...] + halves(matmul(hot, jnp.concatenate(split(ends[...]), 1)))

    masks = [kind == n for n in range(3)]

    def by_kind(x):
        return jnp.concatenate([jnp.where(m, part, jnp.zeros_like(part)) for part in split(x) for m in masks], 1)

    model = halves(matmul(by_kind(column), forward[...]))
    values = slots_in[:, 0:bucket, :].reshape(slots, LANES)
    weights = slots_in[:, bucket : 2 * bucket, :].reshape(slots, LANES)
    departures = jnp.where(code >= 0, values - model, 0.0)
    dep_out[...] = departures
    adjoint = halves(matmul(by_kind(weights * departures), backward[...], ((1,), (1,))))
    pay_out[0:slots, :] = adjoint
    pay_out[slots:, :] = row_in[...]
    code_row = jnp.concatenate([row_in[8 * t : 8 * t + 1, :] for t in range(slots // LANES)], 1)
    depth = ROWS * LANES
    f_out[...] = scatter(adjoint, code_row, body_cell(iota((depth, LANES), 0), range(ROWS))).reshape(f_out.shape)


def edge_forcing_kernel(f_in, a_in, b_in, w_out, e_out):
    even, pole = position()
    a_base, b_base, a_rows, b_rows = halo_places(even, pole)
    sign = wind_sign(pole, (1, LANES))
    for ref, rows, base, scale in ((a_in, a_rows, a_base, 1.0), (b_in, b_rows, b_base, sign)):
        got = scatter(*payload_parts(ref), edge_cell(iota((8 * STEPS, LANES), 0), rows)) * scale
        for k in range(STEPS):
            w_out[base + k] = got[8 * k : 8 * k + STEPS]
            e_out[base + k] = got[8 * k + STEPS : 8 * k + 8]
    for r in range(ROWS):
        w_out[STEPS + r] = f_in[r, pl.ds(0, STEPS, stride=8), :]
        e_out[STEPS + r] = f_in[r, pl.ds(8 * (BODY - STEPS) + 7, STEPS, stride=8), :]


def smooth_kernel(f_in, a_in, b_in, cl, ct, cc, smooth, rim, f, spare):
    even, pole = position()
    a_base, b_base, a_rows, b_rows = halo_places(even, pole)
    sign = wind_sign(pole, (1, LANES))
    for ref, rows, base, scale in ((a_in, a_rows, a_base, 1.0), (b_in, b_rows, b_base, sign)):
        got = scatter(*payload_parts(ref), body_cell(iota((STEPS * LANES, LANES), 0), rows)) * scale
        for k in range(STEPS):
            f[base + k] = got[k * LANES : (k + 1) * LANES]
    for r in range(ROWS):
        f[STEPS + r] = f_in[r]
    for p in range(PLANES):
        rim[p, 0:STEPS, :] = jnp.zeros((STEPS, LANES), F32)
        rim[p, STEPS:SIDE, :] = f[p, pl.ds(0, 8, stride=8), :]
        rim[p, SIDE : 2 * SIDE - STEPS, :] = f[p, pl.ds(8 * (BODY - 8) + 7, 8, stride=8), :]
        rim[p, 2 * SIDE - STEPS : 2 * SIDE, :] = jnp.zeros((STEPS, LANES), F32)

    def store(r, q, value):
        smooth[r, pl.ds(q, 8, stride=BODY), :] = value

    diffuse(f, spare, cl, ct, cc, store, BODY_UNROLL)


def last_kernel(inc, smooth, rim_in, from_west, from_east, rl, rt, rc, back, out, dep_out, rim, f, spare, wide):
    dep_out[...] = back[...]
    rim[...] = rim_in[...]
    diffuse_rim(rim, f, spare, rl, rt, rc, from_west, from_east)
    for r in range(ROWS):
        wide[...] = smooth[r]
        wide[0:STEPS, :] = rim[STEPS + r, STEPS : 2 * STEPS, :]
        wide[LANES - STEPS : LANES, :] = rim[STEPS + r, 2 * SIDE - 2 * STEPS : 2 * SIDE - STEPS, :]
        at = pl.ds(r, LANES, stride=ROWS)
        out[at, :] = inc[at, :] - wide[...].T


def call(kernel, outs, args, scratch=(), spaces=None, out_spaces=None, flops=0, limit=20):
    spaces = spaces or {}
    specs = [pl.BlockSpec(memory_space=spaces.get(n, VMEM)) for n in range(len(args))]
    size = 4 * sum(x.size for x in list(args) + list(outs))
    args = [pltpu.with_memory_space_constraint(x, HBM) if spaces.get(n) is HBM else x for n, x in enumerate(args)]
    return pl.pallas_call(
        kernel,
        out_shape=outs,
        in_specs=specs,
        out_specs=[pl.BlockSpec(memory_space=(out_spaces or {}).get(n, VMEM)) for n in range(len(outs))],
        scratch_shapes=list(scratch),
        compiler_params=pltpu.CompilerParams(vmem_limit_bytes=limit * MIB),
        cost_estimate=pl.CostEstimate(flops=flops, bytes_accessed=size, transcendentals=0),
    )(*args)


def routes():
    lons, lats = (lax.axis_size("lon"), lax.axis_size("lat"))
    at = lambda lon, lat: lon % lons * lats + lat
    cells = [(lon, lat) for lon in range(lons) for lat in range(lats)]
    inner = [(at(o, a), at(o, a ^ 1)) for o, a in cells]
    outer = []
    for o, a in cells:
        if a in (0, lats - 1):
            outer.append((at(o, a), at(o + lons // 2, a)))
        else:
            outer.append((at(o, a), at(o, a - 1 if a % 2 == 0 else a + 1)))
    east = [(at(o, a), at(o + 1, a)) for o, a in cells]
    west = [(at(o, a), at(o - 1, a)) for o, a in cells]
    return inner, outer, east, west


def local(
    increment, coef_lon, coef_lat, obs_values, obs_weight, obs_operator, obs_columns, obs_types, obs_counts
):
    shape = lambda *dims: jax.ShapeDtypeStruct(dims, F32)
    inner, outer, east, west = routes()
    send = lambda x, route: lax.ppermute(x, ("lon", "lat"), route)
    lats = lax.axis_size("lat")
    slots = obs_values.shape[0]
    bucket = slots // lats
    tiles = slots // LANES
    fields = increment.shape[0]
    inc = increment.reshape(-1, LANES)
    cl = coef_lon.reshape(fields * ROWS, LANES)
    ct = coef_lat.reshape(fields * ROWS, LANES)

    own, coef, b_send, a_send, rim_b, rim_a, w_own, e_own, slots_send = call(
        pack_kernel,
        [
            shape(ROWS, LANES, LANES),
            shape(LANES, LANES),
            shape(STEPS, LANES, LANES),
            shape(STEPS, LANES, LANES),
            shape(2 * STEPS + 1, 8, LANES),
            shape(2 * STEPS + 1, 8, LANES),
            shape(ROWS + 1, STEPS, LANES),
            shape(ROWS + 1, STEPS, LANES),
            shape(lats, 2 * bucket + 8, LANES),
        ],
        [
            inc,
            cl,
            ct,
            obs_values.reshape(lats, bucket, LANES),
            obs_weight.reshape(lats, bucket, LANES),
            obs_columns.reshape(1, slots),
            obs_types.reshape(1, slots),
            obs_counts,
        ],
        [
            VMEM(inc.shape, F32),
            VMEM(cl.shape, F32),
            VMEM(ct.shape, F32),
            VMEM((LANES, LANES), F32),
            VMEM((1, slots), jnp.int32),
            VMEM((1, slots), jnp.int32),
            pltpu.SMEM(obs_counts.shape, jnp.int32),
            VMEM((lats, 2 * bucket + 8, LANES), F32),
            pltpu.SemaphoreType.DMA((9,)),
        ],
        spaces={n: HBM for n in range(8)},
        out_spaces={8: pl.ANY},
    )
    rim_a = send(rim_a, inner)
    a_in = send(a_send, inner)
    rim_b = send(rim_b, outer)
    b_in = send(b_send, outer)
    slots_send, _ = lax.optimization_barrier((slots_send, a_in))
    slots_in = lax.all_to_all(slots_send, "lat", split_axis=0, concat_axis=0, tiled=True)
    edge = shape(PLANES + 1, STEPS, LANES)
    block = shape(ROWS, LANES, LANES)
    planes = shape(PLANES, LANES, LANES)
    ends = shape(PLANES, 2 * SIDE, LANES)
    body_buffers = [VMEM(planes.shape, F32)] * 2
    rim_buffers = [VMEM(ends.shape, F32)] * 3
    w_send, e_send, co = call(
        edge_kernel,
        [edge, edge, shape(LANES, LANES)],
        [w_own, e_own, coef, rim_a, rim_b],
        [VMEM((LANES, LANES), F32)],
        flops=EDGE_COST,
    )
    from_west = send(e_send, east)
    from_east = send(w_send, west)
    wl, wt, wc = call(expand, [planes, planes, planes], [co], flops=EXPAND_COST)
    half = shape(STEPS, LANES, LANES)
    near_half, strips = call(
        near_half_kernel,
        [half, shape(STEPS - 1, 2, LANES, LANES)],
        [own, a_in, wl, wt, wc],
        body_buffers,
        flops=STATE_COST,
    )
    (far_half,) = call(
        far_half_kernel, [half], [own, b_in, strips, wl, wt, wc], body_buffers, flops=10**8
    )
    column, code, code_row, forward, backward = call(
        gather_kernel,
        [
            shape(slots, LANES),
            jax.ShapeDtypeStruct((slots, LANES), jnp.int32),
            shape(8 * tiles, LANES),
            jax.ShapeDtypeStruct((6 * LANES, 2 * LANES), jnp.bfloat16),
            jax.ShapeDtypeStruct((2 * LANES, 6 * LANES), jnp.bfloat16),
        ],
        [near_half, far_half, slots_in, obs_operator],
        flops=10**8,
    )
    departures, payload, forcing, rl, rt, rc = call(
        observe_kernel,
        [shape(slots, LANES), shape(slots + 8 * tiles, LANES), block, ends, ends, ends],
        [column, code, code_row, forward, backward, own, a_in, b_in, co, from_west, from_east, slots_in],
        rim_buffers + [VMEM((2 * SIDE, LANES), F32), VMEM((LANES, LANES), F32)],
        flops=10**8,
    )
    a_in = send(payload, inner)
    b_in = send(payload, outer)
    back = lax.all_to_all(
        departures.reshape(lats, bucket, LANES), "lat", split_axis=0, concat_axis=0, tiled=True
    )
    co, _ = lax.optimization_barrier((co, payload))
    wl, wt, wc = call(expand, [planes, planes, planes], [co], flops=EXPAND_COST)
    edge = shape(PLANES, STEPS, LANES)
    w_send, e_send = call(edge_forcing_kernel, [edge, edge], [forcing, a_in, b_in], flops=10**8)
    from_west = send(e_send, east)
    from_east = send(w_send, west)
    smooth, rim = call(
        smooth_kernel, [block, ends], [forcing, a_in, b_in, wl, wt, wc], body_buffers, flops=SMOOTH_COST
    )
    gradient, departures = call(
        last_kernel,
        [shape(*inc.shape), shape(slots, LANES)],
        [inc, smooth, rim, from_west, from_east, rl, rt, rc, back.reshape(slots, LANES)],
        rim_buffers + [VMEM((LANES, LANES), F32)],
        flops=10**8,
    )
    return (gradient.reshape(increment.shape), departures)


def solution(mesh):
    return jax.shard_map(
        local,
        mesh=mesh,
        in_specs=(
            P(None, None, "lat", "lon"),
            P(None, "lat", "lon"),
            P(None, "lat", "lon"),
            P(("lon", "lat"), None),
            P(("lon", "lat"), None),
            P(),
            P(("lon", "lat")),
            P(("lon", "lat")),
            P(("lon", "lat")),
        ),
        out_specs=(P(None, None, "lat", "lon"), P(("lon", "lat"), None)),
        check_vma=False,
    )
```

```python
import functools

import jax
import jax.numpy as jnp
from jax import lax
from jax.experimental import pallas as pl
from jax.experimental.pallas import tpu as pltpu
from jax.sharding import PartitionSpec as P

STEPS = 4
ROWS = 8
LANES = 128
PLANES = ROWS + 2 * STEPS
BODY = LANES // 8
RIM = 3
SIDE = 4 * RIM
VMEM = pltpu.VMEM
HBM = pltpu.HBM
MIB = 1 << 20
RIM_UNROLL = True
BODY_UNROLL = 2
EDGE_COST = 10**10
EXPAND_COST = 10**8
STATE_COST = 10**9
SMOOTH_COST = 10**10
F32 = jnp.float32


def iota(shape, axis):
    return lax.broadcasted_iota(jnp.int32, shape, axis)


def position():
    lat, count = (lax.axis_index("lat"), lax.axis_size("lat"))
    return lat % 2 == 0, jnp.logical_or(lat == 0, lat == count - 1)


def halo_places(even, pole):
    a_base = jnp.where(even, PLANES - STEPS, 0)
    b_base = jnp.where(even, 0, PLANES - STEPS)
    a_rows = [jnp.where(even, k, STEPS + k) for k in range(STEPS)]
    b_rows = [
        jnp.where(
            pole,
            jnp.where(even, STEPS - 1 - k, ROWS - 1 - k),
            jnp.where(even, STEPS + k, k),
        )
        for k in range(STEPS)
    ]
    return a_base, b_base, a_rows, b_rows


def wind_sign(pole, shape):
    flipped = jnp.logical_and(iota(shape, len(shape) - 1) >= LANES // 2, pole)
    return jnp.where(flipped, -1.0, 1.0).astype(F32)


def split(x):
    high = x.astype(jnp.bfloat16)
    low = (x - high.astype(F32)).astype(jnp.bfloat16)
    return high, low


def matmul(a, b, dims=((1,), (0,))):
    return lax.dot_general(a, b, (dims, ((), ())), preferred_element_type=F32)


def halves(x):
    return x[:, :LANES] + x[:, LANES:]


def pack_kernel(
    inc_hbm, cl_hbm, ct_hbm, values, weights, columns_hbm, types_hbm, counts_hbm,
    own, coef, b_out, a_out, rim_b, w_out, e_out, slots_out,
    inc, cl, ct, raw, columns, types, counts, staged, sems,
):
    owners, bucket = (slots_out.shape[0], values.shape[1])
    moves = (
        (columns_hbm, columns),
        (types_hbm, types),
        (counts_hbm, counts),
        (inc_hbm, inc),
        (cl_hbm, cl),
        (ct_hbm, ct),
        (values, staged.at[:, pl.ds(0, bucket), :]),
        (weights, staged.at[:, pl.ds(bucket, bucket), :]),
        (staged, slots_out),
    )
    copies = [pltpu.make_async_copy(src, dst, sems.at[n]) for n, (src, dst) in enumerate(moves)]
    for copy in copies[:8]:
        copy.start()
    for copy in copies[:3]:
        copy.wait()
    slots = columns.shape[1]
    lane = iota((1, slots), 1)
    limit = jnp.zeros((1, slots), jnp.int32)
    for d in range(owners):
        limit = jnp.where(lane // bucket == d, counts[d], limit)
    code = jnp.where(lane % bucket < limit, columns[...] * 4 + types[...], -1).astype(F32)
    for d in range(owners):
        at = d * bucket
        window = code[:, at // LANES * LANES : at // LANES * LANES + LANES]
        moved = pltpu.roll(window, (-at) % LANES, 1)
        staged[d, 2 * bucket : 2 * bucket + 8, :] = jnp.broadcast_to(moved, (8, LANES))
    for copy in copies[3:8]:
        copy.wait()
    copies[8].start()
    fields = cl.shape[0] // ROWS
    even, _ = position()
    raw[...] = jnp.zeros(raw.shape, F32)
    for r in range(ROWS):
        own[r] = inc[pl.ds(r, LANES, stride=ROWS), :].T
        at = 8 * (STEPS + r)
        raw[at : at + fields, :] = cl[pl.ds(r, fields, stride=ROWS), :]
        raw[at + fields : at + 2 * fields, :] = ct[pl.ds(r, fields, stride=ROWS), :]
        w_out[r] = own[r, 0:STEPS, :]
        e_out[r] = own[r, LANES - STEPS : LANES, :]
    coef[...] = raw[...].T
    w_out[ROWS] = coef[0:STEPS, :]
    e_out[ROWS] = coef[LANES - STEPS : LANES, :]
    a_row = jnp.where(even, STEPS, 0)
    b_row = STEPS - a_row
    for out, first in ((b_out, b_row), (a_out, a_row)):
        for k in range(STEPS):
            out[k, 0:LANES, :] = own[first + k]
    ends = jnp.concatenate([coef[0:STEPS, :], coef[LANES - STEPS : LANES, :]], 0)
    rim_b[STEPS] = ends
    for k in range(STEPS):
        rim_b[k, 0:STEPS, :] = own[b_row + k, 0:STEPS, :]
        rim_b[k, STEPS : 2 * STEPS, :] = own[b_row + k, LANES - STEPS : LANES, :]
        rim_b[STEPS + 1 + k] = raw[pl.ds(pl.multiple_of(8 * (STEPS + b_row + k), 8), 8), :]
        a_out[k, LANES : LANES + 8, :] = raw[pl.ds(pl.multiple_of(8 * (STEPS + a_row + k), 8), 8), :]
        a_out[k, LANES + 8 : LANES + 16, :] = ends
    copies[8].wait()


def edge_kernel(w_own, e_own, coef, a_in, rim_b, w_out, e_out, co, raw):
    even, pole = position()
    a_base, b_base, _, b_rows = halo_places(even, pole)
    sign = wind_sign(pole, (1, LANES))
    raw[...] = jnp.zeros(raw.shape, F32)
    for k in range(STEPS):
        kk = jnp.where(pole, STEPS - 1 - k, k)
        w_out[a_base + k] = a_in[k, 0:STEPS, :]
        e_out[a_base + k] = a_in[k, LANES - STEPS : LANES, :]
        rim = rim_b[kk] * sign
        w_out[b_base + k] = rim[0:STEPS]
        e_out[b_base + k] = rim[STEPS : 2 * STEPS]
        raw[pl.ds(pl.multiple_of(8 * (a_base + k), 8), 8), :] = a_in[k, LANES : LANES + 8, :]
        raw[pl.ds(pl.multiple_of(8 * (b_base + k), 8), 8), :] = rim_b[STEPS + 1 + kk]
    for r in range(ROWS):
        w_out[STEPS + r] = w_own[r]
        e_out[STEPS + r] = e_own[r]
    plane = iota((8, LANES), 1) // 8
    tile = jnp.concatenate([w_own[ROWS], e_own[ROWS]], 0)
    from_a = pltpu.roll(a_in[0, LANES + 8 : LANES + 16, :], LANES // 2, 1)
    tile = jnp.where(plane // STEPS == a_base // STEPS, from_a, tile)
    for k in range(STEPS):
        shift = (8 * (b_base + k - STEPS - b_rows[k]) + 2 * LANES) % LANES
        tile = jnp.where(plane == b_base + k, pltpu.roll(rim_b[STEPS], shift, 1), tile)
    w_out[PLANES] = tile[0:STEPS]
    e_out[PLANES] = tile[STEPS : 2 * STEPS]
    co[...] = raw[...].T + coef[...]


def expand(co, cl, ct, cc):
    parts = split(jnp.concatenate([co[pl.ds(q, 8, stride=BODY), :] for q in range(BODY)], 0))
    both_parts = jnp.concatenate(parts, 1)
    tall = 2 * LANES - 16
    row, col = (iota((tall, 2 * LANES), 0), iota((tall, 2 * LANES), 1))
    wanted = LANES - 16 + col // LANES * 4 + col % LANES // (LANES // 4)
    picks = [jnp.where(row == wanted + 8 * odd, 1.0, 0.0).astype(jnp.bfloat16) for odd in range(2)]
    for p in range(PLANES):
        first = LANES - 16 - p // 2 * 16
        pick = picks[p % 2][first : first + LANES, :]
        both = matmul(both_parts, jnp.concatenate([pick, pick], 0))
        a, b = (both[:, :LANES], both[:, LANES:])
        cl[p] = a
        ct[p] = b
        cc[p] = 1.0 - 2.0 * (a * a + b * b)


def expand_rim(co, cl, ct, cc):
    wide = jnp.concatenate([co[pl.ds(q, 8, stride=RIM), :] for q in range(RIM)], 0)
    tall = jnp.concatenate([pltpu.roll(wide, (-8 * p) % LANES, 1) for p in range(PLANES)], 0)
    row, col = (iota((LANES, 2 * LANES), 0), iota((LANES, 2 * LANES), 1))
    pick = jnp.where(row == col // LANES * 4 + col % LANES // (LANES // 4), 1.0, 0.0).astype(jnp.bfloat16)
    both = matmul(jnp.concatenate(split(tall), 1), jnp.concatenate([pick, pick], 0))
    for p in range(PLANES):
        a = both[2 * SIDE * p : 2 * SIDE * (p + 1), :LANES]
        b = both[2 * SIDE * p : 2 * SIDE * (p + 1), LANES:]
        cl[p] = a
        ct[p] = b
        cc[p] = 1.0 - 2.0 * (a * a + b * b)


def relax(p, f, cl, ct, cc, emit):
    regs = [pl.ds(8 * q, 8) for q in range(f.shape[1] // 8)]
    here = [f[p, at, :] for at in regs]
    g = [cl[p, at, :] * x for at, x in zip(regs, here)]
    g = [pltpu.roll(g[-1], 1, 0)] + g + [pltpu.roll(g[0], 7, 0)]
    for q, at in enumerate(regs):
        sides = ct[p + 1, at, :] * f[p + 1, at, :] + ct[p - 1, at, :] * f[p - 1, at, :]
        emit(q, at, cc[p, at, :] * here[q] + cl[p, at, :] * (g[q] + g[q + 2]) + ct[p, at, :] * sides)


def diffuse(f, spare, cl, ct, cc, store, unroll=1):
    for step in range(STEPS):

        def row(p, carry, f=f, spare=spare, last=step == STEPS - 1):
            def emit(q, at, new):
                if last:
                    store(p - STEPS, q, new)
                else:
                    spare[p, at, :] = new

            relax(p, f, cl, ct, cc, emit)
            return carry

        lax.fori_loop(step + 1, PLANES - 1 - step, row, 0, unroll=unroll)
        f, spare = (spare, f)


def diffuse_rim(rim, f, spare, cl, ct, cc, west, east):
    for p in range(PLANES):
        rim[p, 0:STEPS, :] = west[p]
        rim[p, 2 * SIDE - STEPS : 2 * SIDE, :] = east[p]
        for q in range(RIM):
            f[p, 8 * q : 8 * q + 8, :] = rim[p, pl.ds(q, 8, stride=RIM), :]

    def store(r, q, value):
        rim[STEPS + r, pl.ds(q, 8, stride=RIM), :] = value

    diffuse(f, spare, cl, ct, cc, store, RIM_UNROLL)


def body_cell(n, rows):
    rest = n % LANES
    row = jnp.zeros(n.shape, jnp.int32)
    for k, r in enumerate(rows):
        row = jnp.where(n // LANES == k, r, row)
    return row * LANES + (rest % 8) * BODY + rest // 8


def edge_cell(n, rows):
    rest = n % 8
    row = jnp.zeros(n.shape, jnp.int32)
    for k, r in enumerate(rows):
        row = jnp.where(n // 8 == k, r, row)
    return row * LANES + jnp.where(rest < STEPS, rest, rest + LANES - 8)


def scatter(adjoint, code_row, cells):
    code = code_row.astype(jnp.int32)
    cell = jnp.where(code >= 0, code >> 2, -1)
    hot = jnp.concatenate(
        [
            jnp.where(cells == cell[:, t * LANES : (t + 1) * LANES], 1.0, 0.0).astype(jnp.bfloat16)
            for t in range(cell.shape[1] // LANES)
        ],
        1,
    )
    return halves(matmul(hot, jnp.concatenate(split(adjoint), 1)))


def payload_parts(ref):
    slots = ref.shape[0] * LANES // (LANES + 8)
    codes = [ref[slots + 8 * t : slots + 8 * t + 1, :] for t in range(slots // LANES)]
    return ref[0:slots, :], jnp.concatenate(codes, 1)


def near_half_kernel(own, a_in, cl, ct, cc, part, strips, f, spare):
    even, pole = position()
    a_base, _, _, _ = halo_places(even, pole)
    for q in range(BODY):
        at, to = (pl.ds(q, 8, stride=BODY), pl.ds(8 * q, 8))
        for k in range(STEPS):
            f[a_base + k, to, :] = a_in[k, at, :]
        for r in range(ROWS):
            f[STEPS + r, to, :] = own[r, at, :]
    for step in range(STEPS):
        low = jnp.where(even, STEPS + 1 + step, 1 + step)

        def row(i, carry, f=f, spare=spare, low=low, last=step == STEPS - 1):
            def emit(q, at, new):
                if last:
                    part[i, at, :] = new
                else:
                    spare[low + i, at, :] = new

            relax(low + i, f, cl, ct, cc, emit)
            return carry

        lax.fori_loop(0, ROWS + 2 - 2 * step, row, 0, unroll=BODY_UNROLL)
        if step < STEPS - 1:
            first = jnp.where(even, STEPS + 1 + step, ROWS + 1 - step)
            strips[step, 0] = spare[first]
            strips[step, 1] = spare[first + 1]
        f, spare = (spare, f)


def far_half_kernel(own, b_in, strips, cl, ct, cc, part, f, spare):
    even, pole = position()
    _, b_base, _, _ = halo_places(even, pole)
    sign = wind_sign(pole, (1, LANES))
    first = jnp.where(even, 0, ROWS - 2)
    for q in range(BODY):
        at, to = (pl.ds(q, 8, stride=BODY), pl.ds(8 * q, 8))
        for k in range(STEPS):
            f[b_base + k, to, :] = b_in[jnp.where(pole, STEPS - 1 - k, k), at, :] * sign
        for i in range(2):
            f[STEPS + first + i, to, :] = own[first + i, at, :]
    for step in range(STEPS):
        low = jnp.where(even, 1 + step, PLANES - 1 - STEPS - step)

        def row(i, carry, f=f, spare=spare, low=low, last=step == STEPS - 1):
            def emit(q, at, new):
                if last:
                    part[i, at, :] = new
                else:
                    spare[low + i, at, :] = new

            relax(low + i, f, cl, ct, cc, emit)
            return carry

        lax.fori_loop(0, STEPS, row, 0, unroll=BODY_UNROLL)
        if step < STEPS - 1:
            first = jnp.where(even, STEPS + 1 + step, ROWS + 1 - step)
            spare[first] = strips[step, 0]
            spare[first + 1] = strips[step, 1]
        f, spare = (spare, f)


def gather_kernel(near_half, far_half, slots_in, operator, column, code_out, row_out, forward, backward):
    owners, bucket = (slots_in.shape[0], (slots_in.shape[1] - 8) // 2)
    slots = owners * bucket
    even, _ = position()
    lane = iota((1, LANES), 1)
    per_tile = LANES // bucket
    code_parts = []
    for t in range(slots // LANES):
        part = jnp.full((1, LANES), -1.0, F32)
        for n in range(per_tile):
            got = slots_in[t * per_tile + n, 2 * bucket : 2 * bucket + 1, :]
            part = jnp.where(lane // bucket == n, pltpu.roll(got, n * bucket, 1), part)
        code_parts.append(part)
        row_out[8 * t : 8 * t + 8, :] = jnp.broadcast_to(part, (8, LANES))
    code = jnp.concatenate([jnp.broadcast_to(part, (LANES, LANES)).T for part in code_parts], 0)
    code = code.astype(jnp.int32)
    code_out[...] = code
    cell = jnp.where(code >= 0, code >> 2, -1)
    half = STEPS * LANES
    near_row = jnp.where(even, ROWS - STEPS, 0)
    places = iota((1, half), 1)
    ends = (places % 8 == 0) & (places % LANES < 8 * STEPS) | (places % 8 == 7) & (places % LANES >= LANES - 8 * STEPS)
    total = None
    for ref, first in ((near_half, near_row), (far_half, ROWS - STEPS - near_row)):
        cells = jnp.where(ends, -2, body_cell(places, [first + k for k in range(STEPS)]))
        hot = jnp.concatenate(
            [
                jnp.where(cells[:, t : t + LANES] == cell, 1.0, 0.0).astype(jnp.bfloat16)
                for t in range(0, half, LANES)
            ],
            1,
        )
        got = matmul(hot, jnp.concatenate(split(ref[...].reshape(half, LANES)), 1))
        total = got if total is None else total + got
    column[...] = halves(total)
    op_high, op_low = split(operator[...])
    zero = jnp.zeros((LANES, LANES), jnp.bfloat16)
    forward[...] = jnp.concatenate(
        [jnp.concatenate([op_high[n], op_low[n]], 1) for n in range(3)]
        + [jnp.concatenate([op_high[n], zero], 1) for n in range(3)],
        0,
    )
    backward[...] = jnp.concatenate(
        [
            jnp.concatenate([op_high[0], op_high[1], op_high[2]] * 2, 1),
            jnp.concatenate([op_low[0], op_low[1], op_low[2], zero, zero, zero], 1),
        ],
        0,
    )


def observe_kernel(
    column_in, code_in, row_in, forward, backward, own, a_in, b_in, co, from_west, from_east, slots_in,
    dep_out, pay_out, f_out, rl, rt, rc,
    rim, f, spare, co_rim, ends,
):
    even, pole = position()
    a_base, b_base, _, _ = halo_places(even, pole)
    sign = wind_sign(pole, (1, LANES))
    co_rim[0:STEPS, :] = from_west[PLANES]
    co_rim[STEPS:SIDE, :] = co[0:8, :]
    co_rim[SIDE : 2 * SIDE - STEPS, :] = co[LANES - 8 : LANES, :]
    co_rim[2 * SIDE - STEPS : 2 * SIDE, :] = from_east[PLANES]
    expand_rim(co_rim, rl, rt, rc)
    sides = ((slice(STEPS, SIDE), slice(0, 8)), (slice(SIDE, 2 * SIDE - STEPS), slice(LANES - 8, LANES)))
    for to, at in sides:
        for k in range(STEPS):
            rim[a_base + k, to, :] = a_in[k, at, :]
            rim[b_base + k, to, :] = b_in[jnp.where(pole, STEPS - 1 - k, k), at, :] * sign
        for r in range(ROWS):
            rim[STEPS + r, to, :] = own[r, at, :]
    diffuse_rim(rim, f, spare, rl, rt, rc, from_west, from_east)
    slots = column_in.shape[0]
    bucket = (slots_in.shape[1] - 8) // 2
    code = code_in[...]
    cell = jnp.where(code >= 0, code >> 2, -1)
    kind = jnp.where(code >= 0, code & 3, -1)
    for r in range(ROWS):
        ends[8 * r : 8 * r + STEPS, :] = rim[STEPS + r, STEPS : 2 * STEPS, :]
        ends[8 * r + STEPS : 8 * r + 8, :] = rim[STEPS + r, 2 * SIDE - 2 * STEPS : 2 * SIDE - STEPS, :]
    ends[8 * ROWS : LANES, :] = jnp.zeros((LANES - 8 * ROWS, LANES), F32)
    hot = jnp.where(edge_cell(iota((1, LANES), 1), range(ROWS)) == cell, 1.0, 0.0).astype(jnp.bfloat16)
    column = column_in[...] + halves(matmul(hot, jnp.concatenate(split(ends[...]), 1)))

    masks = [kind == n for n in range(3)]

    def by_kind(x):
        return jnp.concatenate([jnp.where(m, part, jnp.zeros_like(part)) for part in split(x) for m in masks], 1)

    model = halves(matmul(by_kind(column), forward[...]))
    values = slots_in[:, 0:bucket, :].reshape(slots, LANES)
    weights = slots_in[:, bucket : 2 * bucket, :].reshape(slots, LANES)
    departures = jnp.where(code >= 0, values - model, 0.0)
    dep_out[...] = departures
    adjoint = halves(matmul(by_kind(weights * departures), backward[...], ((1,), (1,))))
    pay_out[0:slots, :] = adjoint
    pay_out[slots:, :] = row_in[...]
    code_row = jnp.concatenate([row_in[8 * t : 8 * t + 1, :] for t in range(slots // LANES)], 1)
    depth = ROWS * LANES
    f_out[...] = scatter(adjoint, code_row, body_cell(iota((depth, LANES), 0), range(ROWS))).reshape(f_out.shape)


def edge_forcing_kernel(f_in, a_in, b_in, w_out, e_out):
    even, pole = position()
    a_base, b_base, a_rows, b_rows = halo_places(even, pole)
    sign = wind_sign(pole, (1, LANES))
    for ref, rows, base, scale in ((a_in, a_rows, a_base, 1.0), (b_in, b_rows, b_base, sign)):
        got = scatter(*payload_parts(ref), edge_cell(iota((8 * STEPS, LANES), 0), rows)) * scale
        for k in range(STEPS):
            w_out[base + k] = got[8 * k : 8 * k + STEPS]
            e_out[base + k] = got[8 * k + STEPS : 8 * k + 8]
    for r in range(ROWS):
        w_out[STEPS + r] = f_in[r, pl.ds(0, STEPS, stride=8), :]
        e_out[STEPS + r] = f_in[r, pl.ds(8 * (BODY - STEPS) + 7, STEPS, stride=8), :]


def smooth_kernel(f_in, a_in, b_in, cl, ct, cc, smooth, rim, f, spare):
    even, pole = position()
    a_base, b_base, a_rows, b_rows = halo_places(even, pole)
    sign = wind_sign(pole, (1, LANES))
    for ref, rows, base, scale in ((a_in, a_rows, a_base, 1.0), (b_in, b_rows, b_base, sign)):
        got = scatter(*payload_parts(ref), body_cell(iota((STEPS * LANES, LANES), 0), rows)) * scale
        for k in range(STEPS):
            f[base + k] = got[k * LANES : (k + 1) * LANES]
    for r in range(ROWS):
        f[STEPS + r] = f_in[r]
    for p in range(PLANES):
        rim[p, 0:STEPS, :] = jnp.zeros((STEPS, LANES), F32)
        rim[p, STEPS:SIDE, :] = f[p, pl.ds(0, 8, stride=8), :]
        rim[p, SIDE : 2 * SIDE - STEPS, :] = f[p, pl.ds(8 * (BODY - 8) + 7, 8, stride=8), :]
        rim[p, 2 * SIDE - STEPS : 2 * SIDE, :] = jnp.zeros((STEPS, LANES), F32)

    def store(r, q, value):
        smooth[r, pl.ds(q, 8, stride=BODY), :] = value

    diffuse(f, spare, cl, ct, cc, store, BODY_UNROLL)


def last_kernel(inc, smooth, rim_in, from_west, from_east, rl, rt, rc, back, out, dep_out, rim, f, spare, wide):
    dep_out[...] = back[...]
    rim[...] = rim_in[...]
    diffuse_rim(rim, f, spare, rl, rt, rc, from_west, from_east)
    for r in range(ROWS):
        wide[...] = smooth[r]
        wide[0:STEPS, :] = rim[STEPS + r, STEPS : 2 * STEPS, :]
        wide[LANES - STEPS : LANES, :] = rim[STEPS + r, 2 * SIDE - 2 * STEPS : 2 * SIDE - STEPS, :]
        at = pl.ds(r, LANES, stride=ROWS)
        out[at, :] = inc[at, :] - wide[...].T


def call(kernel, outs, args, scratch=(), spaces=None, out_spaces=None, flops=0, limit=20):
    spaces = spaces or {}
    specs = [pl.BlockSpec(memory_space=spaces.get(n, VMEM)) for n in range(len(args))]
    size = 4 * sum(x.size for x in list(args) + list(outs))
    args = [pltpu.with_memory_space_constraint(x, HBM) if spaces.get(n) is HBM else x for n, x in enumerate(args)]
    return pl.pallas_call(
        kernel,
        out_shape=outs,
        in_specs=specs,
        out_specs=[pl.BlockSpec(memory_space=(out_spaces or {}).get(n, VMEM)) for n in range(len(outs))],
        scratch_shapes=list(scratch),
        compiler_params=pltpu.CompilerParams(vmem_limit_bytes=limit * MIB),
        cost_estimate=pl.CostEstimate(flops=flops, bytes_accessed=size, transcendentals=0),
    )(*args)


def routes():
    lons, lats = (lax.axis_size("lon"), lax.axis_size("lat"))
    at = lambda lon, lat: lon % lons * lats + lat
    cells = [(lon, lat) for lon in range(lons) for lat in range(lats)]
    inner = [(at(o, a), at(o, a ^ 1)) for o, a in cells]
    outer = []
    for o, a in cells:
        if a in (0, lats - 1):
            outer.append((at(o, a), at(o + lons // 2, a)))
        else:
            outer.append((at(o, a), at(o, a - 1 if a % 2 == 0 else a + 1)))
    east = [(at(o, a), at(o + 1, a)) for o, a in cells]
    west = [(at(o, a), at(o - 1, a)) for o, a in cells]
    return inner, outer, east, west


def local(
    increment, coef_lon, coef_lat, obs_values, obs_weight, obs_operator, obs_columns, obs_types, obs_counts
):
    shape = lambda *dims: jax.ShapeDtypeStruct(dims, F32)
    inner, outer, east, west = routes()
    send = lambda x, route: lax.ppermute(x, ("lon", "lat"), route)
    lats = lax.axis_size("lat")
    slots = obs_values.shape[0]
    bucket = slots // lats
    tiles = slots // LANES
    fields = increment.shape[0]
    inc = increment.reshape(-1, LANES)
    cl = coef_lon.reshape(fields * ROWS, LANES)
    ct = coef_lat.reshape(fields * ROWS, LANES)

    own, coef, b_send, a_send, rim_b, w_own, e_own, slots_send = call(
        pack_kernel,
        [
            shape(ROWS, LANES, LANES),
            shape(LANES, LANES),
            shape(STEPS, LANES, LANES),
            shape(STEPS, LANES + 16, LANES),
            shape(2 * STEPS + 1, 8, LANES),
            shape(ROWS + 1, STEPS, LANES),
            shape(ROWS + 1, STEPS, LANES),
            shape(lats, 2 * bucket + 8, LANES),
        ],
        [
            inc,
            cl,
            ct,
            obs_values.reshape(lats, bucket, LANES),
            obs_weight.reshape(lats, bucket, LANES),
            obs_columns.reshape(1, slots),
            obs_types.reshape(1, slots),
            obs_counts,
        ],
        [
            VMEM(inc.shape, F32),
            VMEM(cl.shape, F32),
            VMEM(ct.shape, F32),
            VMEM((LANES, LANES), F32),
            VMEM((1, slots), jnp.int32),
            VMEM((1, slots), jnp.int32),
            pltpu.SMEM(obs_counts.shape, jnp.int32),
            VMEM((lats, 2 * bucket + 8, LANES), F32),
            pltpu.SemaphoreType.DMA((9,)),
        ],
        spaces={n: HBM for n in range(8)},
        out_spaces={7: pl.ANY},
    )
    a_in = send(a_send, inner)
    rim_b = send(rim_b, outer)
    b_in = send(b_send, outer)
    slots_send, _ = lax.optimization_barrier((slots_send, a_in))
    slots_in = lax.all_to_all(slots_send, "lat", split_axis=0, concat_axis=0, tiled=True)
    edge = shape(PLANES + 1, STEPS, LANES)
    block = shape(ROWS, LANES, LANES)
    planes = shape(PLANES, LANES, LANES)
    ends = shape(PLANES, 2 * SIDE, LANES)
    body_buffers = [VMEM(planes.shape, F32)] * 2
    rim_buffers = [VMEM(ends.shape, F32)] * 3
    w_send, e_send, co = call(
        edge_kernel,
        [edge, edge, shape(LANES, LANES)],
        [w_own, e_own, coef, a_in, rim_b],
        [VMEM((LANES, LANES), F32)],
        flops=EDGE_COST,
    )
    from_west = send(e_send, east)
    from_east = send(w_send, west)
    wl, wt, wc = call(expand, [planes, planes, planes], [co], flops=EXPAND_COST)
    half = shape(STEPS, LANES, LANES)
    near_half, strips = call(
        near_half_kernel,
        [half, shape(STEPS - 1, 2, LANES, LANES)],
        [own, a_in, wl, wt, wc],
        body_buffers,
        flops=STATE_COST,
    )
    (far_half,) = call(
        far_half_kernel, [half], [own, b_in, strips, wl, wt, wc], body_buffers, flops=10**8
    )
    column, code, code_row, forward, backward = call(
        gather_kernel,
        [
            shape(slots, LANES),
            jax.ShapeDtypeStruct((slots, LANES), jnp.int32),
            shape(8 * tiles, LANES),
            jax.ShapeDtypeStruct((6 * LANES, 2 * LANES), jnp.bfloat16),
            jax.ShapeDtypeStruct((2 * LANES, 6 * LANES), jnp.bfloat16),
        ],
        [near_half, far_half, slots_in, obs_operator],
        flops=10**8,
    )
    departures, payload, forcing, rl, rt, rc = call(
        observe_kernel,
        [shape(slots, LANES), shape(slots + 8 * tiles, LANES), block, ends, ends, ends],
        [column, code, code_row, forward, backward, own, a_in, b_in, co, from_west, from_east, slots_in],
        rim_buffers + [VMEM((2 * SIDE, LANES), F32), VMEM((LANES, LANES), F32)],
        flops=10**8,
    )
    a_in = send(payload, inner)
    b_in = send(payload, outer)
    back = lax.all_to_all(
        departures.reshape(lats, bucket, LANES), "lat", split_axis=0, concat_axis=0, tiled=True
    )
    co, _ = lax.optimization_barrier((co, payload))
    wl, wt, wc = call(expand, [planes, planes, planes], [co], flops=EXPAND_COST)
    edge = shape(PLANES, STEPS, LANES)
    w_send, e_send = call(edge_forcing_kernel, [edge, edge], [forcing, a_in, b_in], flops=10**8)
    from_west = send(e_send, east)
    from_east = send(w_send, west)
    smooth, rim = call(
        smooth_kernel, [block, ends], [forcing, a_in, b_in, wl, wt, wc], body_buffers, flops=SMOOTH_COST
    )
    gradient, departures = call(
        last_kernel,
        [shape(*inc.shape), shape(slots, LANES)],
        [inc, smooth, rim, from_west, from_east, rl, rt, rc, back.reshape(slots, LANES)],
        rim_buffers + [VMEM((LANES, LANES), F32)],
        flops=10**8,
    )
    return (gradient.reshape(increment.shape), departures)


def solution(mesh):
    return jax.shard_map(
        local,
        mesh=mesh,
        in_specs=(
            P(None, None, "lat", "lon"),
            P(None, "lat", "lon"),
            P(None, "lat", "lon"),
            P(("lon", "lat"), None),
            P(("lon", "lat"), None),
            P(),
            P(("lon", "lat")),
            P(("lon", "lat")),
            P(("lon", "lat")),
        ),
        out_specs=(P(None, None, "lat", "lon"), P(("lon", "lat"), None)),
        check_vma=False,
    )
```

```python
import functools

import jax
import jax.numpy as jnp
from jax import lax
from jax.experimental import pallas as pl
from jax.experimental.pallas import tpu as pltpu
from jax.sharding import PartitionSpec as P

STEPS = 4
ROWS = 8
LANES = 128
PLANES = ROWS + 2 * STEPS
BODY = LANES // 8
RIM = 3
SIDE = 4 * RIM
VMEM = pltpu.VMEM
HBM = pltpu.HBM
MIB = 1 << 20
RIM_UNROLL = True
BODY_UNROLL = True
EDGE_COST = 10**10
EXPAND_COST = 10**8
STATE_COST = 10**9
SMOOTH_COST = 10**10
F32 = jnp.float32


def iota(shape, axis):
    return lax.broadcasted_iota(jnp.int32, shape, axis)


def position():
    lat, count = (lax.axis_index("lat"), lax.axis_size("lat"))
    return lat % 2 == 0, jnp.logical_or(lat == 0, lat == count - 1)


def halo_places(even, pole):
    a_base = jnp.where(even, PLANES - STEPS, 0)
    b_base = jnp.where(even, 0, PLANES - STEPS)
    a_rows = [jnp.where(even, k, STEPS + k) for k in range(STEPS)]
    b_rows = [
        jnp.where(
            pole,
            jnp.where(even, STEPS - 1 - k, ROWS - 1 - k),
            jnp.where(even, STEPS + k, k),
        )
        for k in range(STEPS)
    ]
    return a_base, b_base, a_rows, b_rows


def wind_sign(pole, shape):
    flipped = jnp.logical_and(iota(shape, len(shape) - 1) >= LANES // 2, pole)
    return jnp.where(flipped, -1.0, 1.0).astype(F32)


def split(x):
    high = x.astype(jnp.bfloat16)
    low = (x - high.astype(F32)).astype(jnp.bfloat16)
    return high, low


def matmul(a, b, dims=((1,), (0,))):
    return lax.dot_general(a, b, (dims, ((), ())), preferred_element_type=F32)


def halves(x):
    return x[:, :LANES] + x[:, LANES:]


def pack_kernel(
    inc_hbm, cl_hbm, ct_hbm, values, weights, columns_hbm, types_hbm, counts_hbm,
    own, coef, b_out, a_out, rim_b, w_out, e_out, slots_out,
    inc, cl, ct, raw, columns, types, counts, staged, sems,
):
    owners, bucket = (slots_out.shape[0], values.shape[1])
    moves = (
        (columns_hbm, columns),
        (types_hbm, types),
        (counts_hbm, counts),
        (inc_hbm, inc),
        (cl_hbm, cl),
        (ct_hbm, ct),
        (values, staged.at[:, pl.ds(0, bucket), :]),
        (weights, staged.at[:, pl.ds(bucket, bucket), :]),
        (staged, slots_out),
    )
    copies = [pltpu.make_async_copy(src, dst, sems.at[n]) for n, (src, dst) in enumerate(moves)]
    for copy in copies[:8]:
        copy.start()
    for copy in copies[:3]:
        copy.wait()
    slots = columns.shape[1]
    lane = iota((1, slots), 1)
    limit = jnp.zeros((1, slots), jnp.int32)
    for d in range(owners):
        limit = jnp.where(lane // bucket == d, counts[d], limit)
    code = jnp.where(lane % bucket < limit, columns[...] * 4 + types[...], -1).astype(F32)
    for d in range(owners):
        at = d * bucket
        window = code[:, at // LANES * LANES : at // LANES * LANES + LANES]
        moved = pltpu.roll(window, (-at) % LANES, 1)
        staged[d, 2 * bucket : 2 * bucket + 8, :] = jnp.broadcast_to(moved, (8, LANES))
    for copy in copies[3:8]:
        copy.wait()
    copies[8].start()
    fields = cl.shape[0] // ROWS
    even, _ = position()
    raw[...] = jnp.zeros(raw.shape, F32)
    for r in range(ROWS):
        own[r] = inc[pl.ds(r, LANES, stride=ROWS), :].T
        at = 8 * (STEPS + r)
        raw[at : at + fields, :] = cl[pl.ds(r, fields, stride=ROWS), :]
        raw[at + fields : at + 2 * fields, :] = ct[pl.ds(r, fields, stride=ROWS), :]
        w_out[r] = own[r, 0:STEPS, :]
        e_out[r] = own[r, LANES - STEPS : LANES, :]
    coef[...] = raw[...].T
    w_out[ROWS] = coef[0:STEPS, :]
    e_out[ROWS] = coef[LANES - STEPS : LANES, :]
    a_row = jnp.where(even, STEPS, 0)
    b_row = STEPS - a_row
    for out, first in ((b_out, b_row), (a_out, a_row)):
        for k in range(STEPS):
            out[k, 0:LANES, :] = own[first + k]
    ends = jnp.concatenate([coef[0:STEPS, :], coef[LANES - STEPS : LANES, :]], 0)
    rim_b[STEPS] = ends
    for k in range(STEPS):
        rim_b[k, 0:STEPS, :] = own[b_row + k, 0:STEPS, :]
        rim_b[k, STEPS : 2 * STEPS, :] = own[b_row + k, LANES - STEPS : LANES, :]
        rim_b[STEPS + 1 + k] = raw[pl.ds(pl.multiple_of(8 * (STEPS + b_row + k), 8), 8), :]
        a_out[k, LANES : LANES + 8, :] = raw[pl.ds(pl.multiple_of(8 * (STEPS + a_row + k), 8), 8), :]
        a_out[k, LANES + 8 : LANES + 16, :] = ends
    copies[8].wait()


def edge_kernel(w_own, e_own, coef, a_in, rim_b, w_out, e_out, co, raw):
    even, pole = position()
    a_base, b_base, _, b_rows = halo_places(even, pole)
    sign = wind_sign(pole, (1, LANES))
    raw[...] = jnp.zeros(raw.shape, F32)
    for k in range(STEPS):
        kk = jnp.where(pole, STEPS - 1 - k, k)
        w_out[a_base + k] = a_in[k, 0:STEPS, :]
        e_out[a_base + k] = a_in[k, LANES - STEPS : LANES, :]
        rim = rim_b[kk] * sign
        w_out[b_base + k] = rim[0:STEPS]
        e_out[b_base + k] = rim[STEPS : 2 * STEPS]
        raw[pl.ds(pl.multiple_of(8 * (a_base + k), 8), 8), :] = a_in[k, LANES : LANES + 8, :]
        raw[pl.ds(pl.multiple_of(8 * (b_base + k), 8), 8), :] = rim_b[STEPS + 1 + kk]
    for r in range(ROWS):
        w_out[STEPS + r] = w_own[r]
        e_out[STEPS + r] = e_own[r]
    plane = iota((8, LANES), 1) // 8
    tile = jnp.concatenate([w_own[ROWS], e_own[ROWS]], 0)
    from_a = pltpu.roll(a_in[0, LANES + 8 : LANES + 16, :], LANES // 2, 1)
    tile = jnp.where(plane // STEPS == a_base // STEPS, from_a, tile)
    for k in range(STEPS):
        shift = (8 * (b_base + k - STEPS - b_rows[k]) + 2 * LANES) % LANES
        tile = jnp.where(plane == b_base + k, pltpu.roll(rim_b[STEPS], shift, 1), tile)
    w_out[PLANES] = tile[0:STEPS]
    e_out[PLANES] = tile[STEPS : 2 * STEPS]
    co[...] = raw[...].T + coef[...]


def expand(co, cl, ct, cc):
    parts = split(jnp.concatenate([co[pl.ds(q, 8, stride=BODY), :] for q in range(BODY)], 0))
    both_parts = jnp.concatenate(parts, 1)
    tall = 2 * LANES - 16
    row, col = (iota((tall, 2 * LANES), 0), iota((tall, 2 * LANES), 1))
    wanted = LANES - 16 + col // LANES * 4 + col % LANES // (LANES // 4)
    picks = [jnp.where(row == wanted + 8 * odd, 1.0, 0.0).astype(jnp.bfloat16) for odd in range(2)]
    for p in range(PLANES):
        first = LANES - 16 - p // 2 * 16
        pick = picks[p % 2][first : first + LANES, :]
        both = matmul(both_parts, jnp.concatenate([pick, pick], 0))
        a, b = (both[:, :LANES], both[:, LANES:])
        cl[p] = a
        ct[p] = b
        cc[p] = 1.0 - 2.0 * (a * a + b * b)


def expand_rim(co, cl, ct, cc):
    wide = jnp.concatenate([co[pl.ds(q, 8, stride=RIM), :] for q in range(RIM)], 0)
    tall = jnp.concatenate([pltpu.roll(wide, (-8 * p) % LANES, 1) for p in range(PLANES)], 0)
    row, col = (iota((LANES, 2 * LANES), 0), iota((LANES, 2 * LANES), 1))
    pick = jnp.where(row == col // LANES * 4 + col % LANES // (LANES // 4), 1.0, 0.0).astype(jnp.bfloat16)
    both = matmul(jnp.concatenate(split(tall), 1), jnp.concatenate([pick, pick], 0))
    for p in range(PLANES):
        a = both[2 * SIDE * p : 2 * SIDE * (p + 1), :LANES]
        b = both[2 * SIDE * p : 2 * SIDE * (p + 1), LANES:]
        cl[p] = a
        ct[p] = b
        cc[p] = 1.0 - 2.0 * (a * a + b * b)


def relax(p, f, cl, ct, cc, emit):
    regs = [pl.ds(8 * q, 8) for q in range(f.shape[1] // 8)]
    here = [f[p, at, :] for at in regs]
    g = [cl[p, at, :] * x for at, x in zip(regs, here)]
    g = [pltpu.roll(g[-1], 1, 0)] + g + [pltpu.roll(g[0], 7, 0)]
    for q, at in enumerate(regs):
        sides = ct[p + 1, at, :] * f[p + 1, at, :] + ct[p - 1, at, :] * f[p - 1, at, :]
        emit(q, at, cc[p, at, :] * here[q] + cl[p, at, :] * (g[q] + g[q + 2]) + ct[p, at, :] * sides)


def diffuse(f, spare, cl, ct, cc, store, unroll=1):
    for step in range(STEPS):

        def row(p, carry, f=f, spare=spare, last=step == STEPS - 1):
            def emit(q, at, new):
                if last:
                    store(p - STEPS, q, new)
                else:
                    spare[p, at, :] = new

            relax(p, f, cl, ct, cc, emit)
            return carry

        lax.fori_loop(step + 1, PLANES - 1 - step, row, 0, unroll=unroll)
        f, spare = (spare, f)


def diffuse_rim(rim, f, spare, cl, ct, cc, west, east):
    for p in range(PLANES):
        rim[p, 0:STEPS, :] = west[p]
        rim[p, 2 * SIDE - STEPS : 2 * SIDE, :] = east[p]
        for q in range(RIM):
            f[p, 8 * q : 8 * q + 8, :] = rim[p, pl.ds(q, 8, stride=RIM), :]

    def store(r, q, value):
        rim[STEPS + r, pl.ds(q, 8, stride=RIM), :] = value

    diffuse(f, spare, cl, ct, cc, store, RIM_UNROLL)


def body_cell(n, rows):
    rest = n % LANES
    row = jnp.zeros(n.shape, jnp.int32)
    for k, r in enumerate(rows):
        row = jnp.where(n // LANES == k, r, row)
    return row * LANES + (rest % 8) * BODY + rest // 8


def edge_cell(n, rows):
    rest = n % 8
    row = jnp.zeros(n.shape, jnp.int32)
    for k, r in enumerate(rows):
        row = jnp.where(n // 8 == k, r, row)
    return row * LANES + jnp.where(rest < STEPS, rest, rest + LANES - 8)


def scatter(adjoint, code_row, cells):
    code = code_row.astype(jnp.int32)
    cell = jnp.where(code >= 0, code >> 2, -1)
    hot = jnp.concatenate(
        [
            jnp.where(cells == cell[:, t * LANES : (t + 1) * LANES], 1.0, 0.0).astype(jnp.bfloat16)
            for t in range(cell.shape[1] // LANES)
        ],
        1,
    )
    return halves(matmul(hot, jnp.concatenate(split(adjoint), 1)))


def payload_parts(ref):
    slots = ref.shape[0] * LANES // (LANES + 8)
    codes = [ref[slots + 8 * t : slots + 8 * t + 1, :] for t in range(slots // LANES)]
    return ref[0:slots, :], jnp.concatenate(codes, 1)


def near_half_kernel(own, a_in, cl, ct, cc, part, strips, f, spare):
    even, pole = position()
    a_base, _, _, _ = halo_places(even, pole)
    for q in range(BODY):
        at, to = (pl.ds(q, 8, stride=BODY), pl.ds(8 * q, 8))
        for k in range(STEPS):
            f[a_base + k, to, :] = a_in[k, at, :]
        for r in range(ROWS):
            f[STEPS + r, to, :] = own[r, at, :]
    for step in range(STEPS):
        low = jnp.where(even, STEPS + 1 + step, 1 + step)

        def row(i, carry, f=f, spare=spare, low=low, last=step == STEPS - 1):
            def emit(q, at, new):
                if last:
                    part[i, at, :] = new
                else:
                    spare[low + i, at, :] = new

            relax(low + i, f, cl, ct, cc, emit)
            return carry

        lax.fori_loop(0, ROWS + 2 - 2 * step, row, 0, unroll=BODY_UNROLL)
        if step < STEPS - 1:
            first = jnp.where(even, STEPS + 1 + step, ROWS + 1 - step)
            strips[step, 0] = spare[first]
            strips[step, 1] = spare[first + 1]
        f, spare = (spare, f)


def far_half_kernel(own, b_in, strips, cl, ct, cc, part, f, spare):
    even, pole = position()
    _, b_base, _, _ = halo_places(even, pole)
    sign = wind_sign(pole, (1, LANES))
    first = jnp.where(even, 0, ROWS - 2)
    for q in range(BODY):
        at, to = (pl.ds(q, 8, stride=BODY), pl.ds(8 * q, 8))
        for k in range(STEPS):
            f[b_base + k, to, :] = b_in[jnp.where(pole, STEPS - 1 - k, k), at, :] * sign
        for i in range(2):
            f[STEPS + first + i, to, :] = own[first + i, at, :]
    for step in range(STEPS):
        low = jnp.where(even, 1 + step, PLANES - 1 - STEPS - step)

        def row(i, carry, f=f, spare=spare, low=low, last=step == STEPS - 1):
            def emit(q, at, new):
                if last:
                    part[i, at, :] = new
                else:
                    spare[low + i, at, :] = new

            relax(low + i, f, cl, ct, cc, emit)
            return carry

        lax.fori_loop(0, STEPS, row, 0, unroll=BODY_UNROLL)
        if step < STEPS - 1:
            first = jnp.where(even, STEPS + 1 + step, ROWS + 1 - step)
            spare[first] = strips[step, 0]
            spare[first + 1] = strips[step, 1]
        f, spare = (spare, f)


def gather_kernel(near_half, far_half, slots_in, operator, column, code_out, row_out, forward, backward):
    owners, bucket = (slots_in.shape[0], (slots_in.shape[1] - 8) // 2)
    slots = owners * bucket
    even, _ = position()
    lane = iota((1, LANES), 1)
    per_tile = LANES // bucket
    code_parts = []
    for t in range(slots // LANES):
        part = jnp.full((1, LANES), -1.0, F32)
        for n in range(per_tile):
            got = slots_in[t * per_tile + n, 2 * bucket : 2 * bucket + 1, :]
            part = jnp.where(lane // bucket == n, pltpu.roll(got, n * bucket, 1), part)
        code_parts.append(part)
        row_out[8 * t : 8 * t + 8, :] = jnp.broadcast_to(part, (8, LANES))
    code = jnp.concatenate([jnp.broadcast_to(part, (LANES, LANES)).T for part in code_parts], 0)
    code = code.astype(jnp.int32)
    code_out[...] = code
    cell = jnp.where(code >= 0, code >> 2, -1)
    half = STEPS * LANES
    near_row = jnp.where(even, ROWS - STEPS, 0)
    places = iota((1, half), 1)
    ends = (places % 8 == 0) & (places % LANES < 8 * STEPS) | (places % 8 == 7) & (places % LANES >= LANES - 8 * STEPS)
    total = None
    for ref, first in ((near_half, near_row), (far_half, ROWS - STEPS - near_row)):
        cells = jnp.where(ends, -2, body_cell(places, [first + k for k in range(STEPS)]))
        hot = jnp.concatenate(
            [
                jnp.where(cells[:, t : t + LANES] == cell, 1.0, 0.0).astype(jnp.bfloat16)
                for t in range(0, half, LANES)
            ],
            1,
        )
        got = matmul(hot, jnp.concatenate(split(ref[...].reshape(half, LANES)), 1))
        total = got if total is None else total + got
    column[...] = halves(total)
    op_high, op_low = split(operator[...])
    zero = jnp.zeros((LANES, LANES), jnp.bfloat16)
    forward[...] = jnp.concatenate(
        [jnp.concatenate([op_high[n], op_low[n]], 1) for n in range(3)]
        + [jnp.concatenate([op_high[n], zero], 1) for n in range(3)],
        0,
    )
    backward[...] = jnp.concatenate(
        [
            jnp.concatenate([op_high[0], op_high[1], op_high[2]] * 2, 1),
            jnp.concatenate([op_low[0], op_low[1], op_low[2], zero, zero, zero], 1),
        ],
        0,
    )


def observe_kernel(
    column_in, code_in, row_in, forward, backward, own, a_in, b_in, co, from_west, from_east, slots_in,
    dep_out, pay_out, f_out, rl, rt, rc,
    rim, f, spare, co_rim, ends,
):
    even, pole = position()
    a_base, b_base, _, _ = halo_places(even, pole)
    sign = wind_sign(pole, (1, LANES))
    co_rim[0:STEPS, :] = from_west[PLANES]
    co_rim[STEPS:SIDE, :] = co[0:8, :]
    co_rim[SIDE : 2 * SIDE - STEPS, :] = co[LANES - 8 : LANES, :]
    co_rim[2 * SIDE - STEPS : 2 * SIDE, :] = from_east[PLANES]
    expand_rim(co_rim, rl, rt, rc)
    sides = ((slice(STEPS, SIDE), slice(0, 8)), (slice(SIDE, 2 * SIDE - STEPS), slice(LANES - 8, LANES)))
    for to, at in sides:
        for k in range(STEPS):
            rim[a_base + k, to, :] = a_in[k, at, :]
            rim[b_base + k, to, :] = b_in[jnp.where(pole, STEPS - 1 - k, k), at, :] * sign
        for r in range(ROWS):
            rim[STEPS + r, to, :] = own[r, at, :]
    diffuse_rim(rim, f, spare, rl, rt, rc, from_west, from_east)
    slots = column_in.shape[0]
    bucket = (slots_in.shape[1] - 8) // 2
    code = code_in[...]
    cell = jnp.where(code >= 0, code >> 2, -1)
    kind = jnp.where(code >= 0, code & 3, -1)
    for r in range(ROWS):
        ends[8 * r : 8 * r + STEPS, :] = rim[STEPS + r, STEPS : 2 * STEPS, :]
        ends[8 * r + STEPS : 8 * r + 8, :] = rim[STEPS + r, 2 * SIDE - 2 * STEPS : 2 * SIDE - STEPS, :]
    ends[8 * ROWS : LANES, :] = jnp.zeros((LANES - 8 * ROWS, LANES), F32)
    hot = jnp.where(edge_cell(iota((1, LANES), 1), range(ROWS)) == cell, 1.0, 0.0).astype(jnp.bfloat16)
    column = column_in[...] + halves(matmul(hot, jnp.concatenate(split(ends[...]), 1)))

    masks = [kind == n for n in range(3)]

    def by_kind(x):
        return jnp.concatenate([jnp.where(m, part, jnp.zeros_like(part)) for part in split(x) for m in masks], 1)

    model = halves(matmul(by_kind(column), forward[...]))
    values = slots_in[:, 0:bucket, :].reshape(slots, LANES)
    weights = slots_in[:, bucket : 2 * bucket, :].reshape(slots, LANES)
    departures = jnp.where(code >= 0, values - model, 0.0)
    dep_out[...] = departures
    adjoint = halves(matmul(by_kind(weights * departures), backward[...], ((1,), (1,))))
    pay_out[0:slots, :] = adjoint
    pay_out[slots:, :] = row_in[...]
    code_row = jnp.concatenate([row_in[8 * t : 8 * t + 1, :] for t in range(slots // LANES)], 1)
    depth = ROWS * LANES
    f_out[...] = scatter(adjoint, code_row, body_cell(iota((depth, LANES), 0), range(ROWS))).reshape(f_out.shape)


def edge_forcing_kernel(f_in, a_in, b_in, w_out, e_out):
    even, pole = position()
    a_base, b_base, a_rows, b_rows = halo_places(even, pole)
    sign = wind_sign(pole, (1, LANES))
    for ref, rows, base, scale in ((a_in, a_rows, a_base, 1.0), (b_in, b_rows, b_base, sign)):
        got = scatter(*payload_parts(ref), edge_cell(iota((8 * STEPS, LANES), 0), rows)) * scale
        for k in range(STEPS):
            w_out[base + k] = got[8 * k : 8 * k + STEPS]
            e_out[base + k] = got[8 * k + STEPS : 8 * k + 8]
    for r in range(ROWS):
        w_out[STEPS + r] = f_in[r, pl.ds(0, STEPS, stride=8), :]
        e_out[STEPS + r] = f_in[r, pl.ds(8 * (BODY - STEPS) + 7, STEPS, stride=8), :]


def smooth_kernel(f_in, a_in, b_in, cl, ct, cc, smooth, rim, f, spare):
    even, pole = position()
    a_base, b_base, a_rows, b_rows = halo_places(even, pole)
    sign = wind_sign(pole, (1, LANES))
    for ref, rows, base, scale in ((a_in, a_rows, a_base, 1.0), (b_in, b_rows, b_base, sign)):
        got = scatter(*payload_parts(ref), body_cell(iota((STEPS * LANES, LANES), 0), rows)) * scale
        for k in range(STEPS):
            f[base + k] = got[k * LANES : (k + 1) * LANES]
    for r in range(ROWS):
        f[STEPS + r] = f_in[r]
    for p in range(PLANES):
        rim[p, 0:STEPS, :] = jnp.zeros((STEPS, LANES), F32)
        rim[p, STEPS:SIDE, :] = f[p, pl.ds(0, 8, stride=8), :]
        rim[p, SIDE : 2 * SIDE - STEPS, :] = f[p, pl.ds(8 * (BODY - 8) + 7, 8, stride=8), :]
        rim[p, 2 * SIDE - STEPS : 2 * SIDE, :] = jnp.zeros((STEPS, LANES), F32)

    def store(r, q, value):
        smooth[r, pl.ds(q, 8, stride=BODY), :] = value

    diffuse(f, spare, cl, ct, cc, store, BODY_UNROLL)


def last_kernel(inc, smooth, rim_in, from_west, from_east, rl, rt, rc, back, out, dep_out, rim, f, spare, wide):
    dep_out[...] = back[...]
    rim[...] = rim_in[...]
    diffuse_rim(rim, f, spare, rl, rt, rc, from_west, from_east)
    for r in range(ROWS):
        wide[...] = smooth[r]
        wide[0:STEPS, :] = rim[STEPS + r, STEPS : 2 * STEPS, :]
        wide[LANES - STEPS : LANES, :] = rim[STEPS + r, 2 * SIDE - 2 * STEPS : 2 * SIDE - STEPS, :]
        at = pl.ds(r, LANES, stride=ROWS)
        out[at, :] = inc[at, :] - wide[...].T


def call(kernel, outs, args, scratch=(), spaces=None, out_spaces=None, flops=0, limit=20):
    spaces = spaces or {}
    specs = [pl.BlockSpec(memory_space=spaces.get(n, VMEM)) for n in range(len(args))]
    size = 4 * sum(x.size for x in list(args) + list(outs))
    args = [pltpu.with_memory_space_constraint(x, HBM) if spaces.get(n) is HBM else x for n, x in enumerate(args)]
    return pl.pallas_call(
        kernel,
        out_shape=outs,
        in_specs=specs,
        out_specs=[pl.BlockSpec(memory_space=(out_spaces or {}).get(n, VMEM)) for n in range(len(outs))],
        scratch_shapes=list(scratch),
        compiler_params=pltpu.CompilerParams(vmem_limit_bytes=limit * MIB),
        cost_estimate=pl.CostEstimate(flops=flops, bytes_accessed=size, transcendentals=0),
    )(*args)


def routes():
    lons, lats = (lax.axis_size("lon"), lax.axis_size("lat"))
    at = lambda lon, lat: lon % lons * lats + lat
    cells = [(lon, lat) for lon in range(lons) for lat in range(lats)]
    inner = [(at(o, a), at(o, a ^ 1)) for o, a in cells]
    outer = []
    for o, a in cells:
        if a in (0, lats - 1):
            outer.append((at(o, a), at(o + lons // 2, a)))
        else:
            outer.append((at(o, a), at(o, a - 1 if a % 2 == 0 else a + 1)))
    east = [(at(o, a), at(o + 1, a)) for o, a in cells]
    west = [(at(o, a), at(o - 1, a)) for o, a in cells]
    return inner, outer, east, west


def local(
    increment, coef_lon, coef_lat, obs_values, obs_weight, obs_operator, obs_columns, obs_types, obs_counts
):
    shape = lambda *dims: jax.ShapeDtypeStruct(dims, F32)
    inner, outer, east, west = routes()
    send = lambda x, route: lax.ppermute(x, ("lon", "lat"), route)
    lats = lax.axis_size("lat")
    slots = obs_values.shape[0]
    bucket = slots // lats
    tiles = slots // LANES
    fields = increment.shape[0]
    inc = increment.reshape(-1, LANES)
    cl = coef_lon.reshape(fields * ROWS, LANES)
    ct = coef_lat.reshape(fields * ROWS, LANES)

    own, coef, b_send, a_send, rim_b, w_own, e_own, slots_send = call(
        pack_kernel,
        [
            shape(ROWS, LANES, LANES),
            shape(LANES, LANES),
            shape(STEPS, LANES, LANES),
            shape(STEPS, LANES + 16, LANES),
            shape(2 * STEPS + 1, 8, LANES),
            shape(ROWS + 1, STEPS, LANES),
            shape(ROWS + 1, STEPS, LANES),
            shape(lats, 2 * bucket + 8, LANES),
        ],
        [
            inc,
            cl,
            ct,
            obs_values.reshape(lats, bucket, LANES),
            obs_weight.reshape(lats, bucket, LANES),
            obs_columns.reshape(1, slots),
            obs_types.reshape(1, slots),
            obs_counts,
        ],
        [
            VMEM(inc.shape, F32),
            VMEM(cl.shape, F32),
            VMEM(ct.shape, F32),
            VMEM((LANES, LANES), F32),
            VMEM((1, slots), jnp.int32),
            VMEM((1, slots), jnp.int32),
            pltpu.SMEM(obs_counts.shape, jnp.int32),
            VMEM((lats, 2 * bucket + 8, LANES), F32),
            pltpu.SemaphoreType.DMA((9,)),
        ],
        spaces={n: HBM for n in range(8)},
        out_spaces={7: pl.ANY},
    )
    a_in = send(a_send, inner)
    rim_b = send(rim_b, outer)
    b_in = send(b_send, outer)
    slots_send, _ = lax.optimization_barrier((slots_send, a_in))
    slots_in = lax.all_to_all(slots_send, "lat", split_axis=0, concat_axis=0, tiled=True)
    edge = shape(PLANES + 1, STEPS, LANES)
    block = shape(ROWS, LANES, LANES)
    planes = shape(PLANES, LANES, LANES)
    ends = shape(PLANES, 2 * SIDE, LANES)
    body_buffers = [VMEM(planes.shape, F32)] * 2
    rim_buffers = [VMEM(ends.shape, F32)] * 3
    w_send, e_send, co = call(
        edge_kernel,
        [edge, edge, shape(LANES, LANES)],
        [w_own, e_own, coef, a_in, rim_b],
        [VMEM((LANES, LANES), F32)],
        flops=EDGE_COST,
    )
    from_west = send(e_send, east)
    from_east = send(w_send, west)
    wl, wt, wc = call(expand, [planes, planes, planes], [co], flops=EXPAND_COST)
    half = shape(STEPS, LANES, LANES)
    near_half, strips = call(
        near_half_kernel,
        [half, shape(STEPS - 1, 2, LANES, LANES)],
        [own, a_in, wl, wt, wc],
        body_buffers,
        flops=STATE_COST,
    )
    (far_half,) = call(
        far_half_kernel, [half], [own, b_in, strips, wl, wt, wc], body_buffers, flops=10**8
    )
    column, code, code_row, forward, backward = call(
        gather_kernel,
        [
            shape(slots, LANES),
            jax.ShapeDtypeStruct((slots, LANES), jnp.int32),
            shape(8 * tiles, LANES),
            jax.ShapeDtypeStruct((6 * LANES, 2 * LANES), jnp.bfloat16),
            jax.ShapeDtypeStruct((2 * LANES, 6 * LANES), jnp.bfloat16),
        ],
        [near_half, far_half, slots_in, obs_operator],
        flops=10**8,
    )
    departures, payload, forcing, rl, rt, rc = call(
        observe_kernel,
        [shape(slots, LANES), shape(slots + 8 * tiles, LANES), block, ends, ends, ends],
        [column, code, code_row, forward, backward, own, a_in, b_in, co, from_west, from_east, slots_in],
        rim_buffers + [VMEM((2 * SIDE, LANES), F32), VMEM((LANES, LANES), F32)],
        flops=10**8,
    )
    a_in = send(payload, inner)
    b_in = send(payload, outer)
    back = lax.all_to_all(
        departures.reshape(lats, bucket, LANES), "lat", split_axis=0, concat_axis=0, tiled=True
    )
    co, _ = lax.optimization_barrier((co, payload))
    wl, wt, wc = call(expand, [planes, planes, planes], [co], flops=EXPAND_COST)
    edge = shape(PLANES, STEPS, LANES)
    w_send, e_send = call(edge_forcing_kernel, [edge, edge], [forcing, a_in, b_in], flops=10**8)
    from_west = send(e_send, east)
    from_east = send(w_send, west)
    smooth, rim = call(
        smooth_kernel, [block, ends], [forcing, a_in, b_in, wl, wt, wc], body_buffers, flops=SMOOTH_COST
    )
    gradient, departures = call(
        last_kernel,
        [shape(*inc.shape), shape(slots, LANES)],
        [inc, smooth, rim, from_west, from_east, rl, rt, rc, back.reshape(slots, LANES)],
        rim_buffers + [VMEM((LANES, LANES), F32)],
        flops=10**8,
    )
    return (gradient.reshape(increment.shape), departures)


def solution(mesh):
    return jax.shard_map(
        local,
        mesh=mesh,
        in_specs=(
            P(None, None, "lat", "lon"),
            P(None, "lat", "lon"),
            P(None, "lat", "lon"),
            P(("lon", "lat"), None),
            P(("lon", "lat"), None),
            P(),
            P(("lon", "lat")),
            P(("lon", "lat")),
            P(("lon", "lat")),
        ),
        out_specs=(P(None, None, "lat", "lon"), P(("lon", "lat"), None)),
        check_vma=False,
    )
```
